32 devices in a mesh: seq: 4 (over z), fft: 8 (over y, x, core).
Axes of the slice: x: 2, y: 2, z: 4, core: 2. Of those that a mesh axis runs over, the one named last changes fastest.
Arguments:
- features: bfloat16 [256, 4096], P(None, ('seq', 'fft')), may hold values from -6 to 6
- sink_order: int32 [32, 128], P(('seq', 'fft')), may hold values from 0 to 127, each once within a row
- cotangent: bfloat16 [256, 4096], P(None, ('seq', 'fft')), may hold values from -6 to 6
- w_in: bfloat16 [768, 256], replicated, may hold values from -0.375 to 0.375
- short_taps: float32 [768, 3], replicated, may hold values from -1 to 1
- w_out: bfloat16 [256, 256], replicated, may hold values from -0.375 to 0.375
- filter_one: float32 [256, 4096], P(('seq', 'fft')), may hold values from -2 to 2
- filter_two: float32 [256, 4096], P(('seq', 'fft')), may hold values from -2 to 2
Outputs:
- grad_features: bfloat16 [256, 4096], P(None, ('seq', 'fft'))
- grad_w_in: float32 [768, 256], replicated
- grad_w_out: float32 [256, 256], replicated
- grad_short: float32 [768, 3], replicated
- grad_filter_one: float32 [256, 4096], P(('seq', 'fft'))
- grad_filter_two: float32 [256, 4096], P(('seq', 'fft'))
The draws below stay inside these ranges and needn't reach their ends.
Inputs may be any that keep to these rules, and one draw needn't show every extreme that they name: Each row of sink_order names every position of a block of 128 sinks once.
All inputs are finite; a program needn't handle non-finite values.
Results may differ from the reference program's by a relative error of at most 0.0089.
Values may be sent and summed in bfloat16 or wider, within the bound.
No kernel may reach another device: no remote copies, remote signals or barrier semaphores. Data moves between devices by JAX's collectives and lax.ppermute only.
A program may use at most 64 MiB of HBM per device.

```python
import math
import jax
import jax.numpy as jnp
from jax import lax

D = 256
ROWS_DEV = 128
BLOCKS = 32
SINKS = 4096


def filter_draw(key, salt):
    key = jax.random.fold_in(key, salt)
    keys = jax.random.split(key, 6)
    sample_location = jnp.arange(SINKS, dtype=jnp.float32)[None, :]
    share = 0.5
    slow = jax.random.uniform(keys[0], (D, 1), dtype=jnp.float32) < share
    slow_rate = jnp.exp(jax.random.uniform(keys[1], (D, 1), dtype=jnp.float32, minval=math.log(0.2 / SINKS), maxval=math.log(2.0 / SINKS)))
    fast_rate = jnp.exp(jax.random.uniform(keys[2], (D, 1), dtype=jnp.float32, minval=math.log(1.0 / 50.0), maxval=math.log(1.0 / 20.0)))
    decay = jnp.where(slow, slow_rate, fast_rate)
    decay_profile = jnp.exp(-decay * sample_location)
    sample_points = jax.random.uniform(keys[3], (D, 3), dtype=jnp.float32) * SINKS
    delay_losses = jax.random.uniform(keys[4], (D, 3), dtype=jnp.float32, minval=0.5, maxval=0.8)
    for pulse_train in range(3):
        decay_profile = decay_profile * jnp.where(sample_location >= sample_points[:, pulse_train:pulse_train + 1], delay_losses[:, pulse_train:pulse_train + 1], 1.0)
    gain_factor = jnp.sqrt(-jnp.expm1(-2.0 * decay))
    noise = jax.random.uniform(keys[5], (D, SINKS), dtype=jnp.float32, minval=-1.7, maxval=1.7)
    return (noise * decay_profile * gain_factor).astype(jnp.float32)


def draw_filter_one(key, part):
    return filter_draw(key, 11)


def draw_filter_two(key, part):
    return filter_draw(key, 23)


def steps_of(rng, extent, cuts, smallest, largest):
    factor_of, own = 1.0, jax.random.fold_in(rng, 6)
    for position, shards_of in cuts:
        heights = jnp.exp(jax.random.uniform(jax.random.fold_in(own, position), (shards_of,), jnp.float32, smallest / len(cuts), largest / len(cuts)))
        factor_of = factor_of * jnp.repeat(heights, extent[position] // shards_of).reshape([-1 if axis == position else 1 for axis in range(len(extent))])
    return factor_of


def centred(stream_key, shape, deviation, most, cuts=(), kind=jnp.bfloat16):
    level = steps_of(stream_key, shape, cuts, -0.22, 0.18) if cuts else 1.0
    values = jax.random.normal(stream_key, shape, jnp.float32) * deviation * level
    return jnp.minimum(jnp.maximum(values, -most), most).astype(kind)


def setup_inputs(seed: int = 0) -> dict:
    splits = jax.random.split(jax.random.key(seed), 9)
    features = centred(splits[0], (D, SINKS), 1.0, 6.0, ((1, 32),))
    sink_order = jax.vmap(lambda own: jax.random.permutation(own, ROWS_DEV))(jax.random.split(splits[1], BLOCKS)).reshape((BLOCKS, ROWS_DEV)).astype(jnp.int32)
    cotangent = centred(splits[2], (D, SINKS), 1.0, 6.0, ((1, 32),))
    w_in = centred(splits[3], (3 * D, D), D ** -0.5, 0.375)
    short_taps = jnp.clip(jax.random.uniform(splits[4], (3 * D, 3), jnp.float32, -1.0, 1.0), -1.0, 1.0)
    w_out = centred(splits[5], (D, D), D ** -0.5, 0.375)
    filter_one = draw_filter_one(jax.random.fold_in(splits[8], 71), 0)
    filter_two = draw_filter_two(jax.random.fold_in(splits[8], 71), 0)
    return dict(features=features, sink_order=sink_order, cotangent=cotangent, w_in=w_in, short_taps=short_taps, w_out=w_out, filter_one=filter_one, filter_two=filter_two)


def long_conv(filt, signal):
    total = 2 * SINKS
    spec_a = jnp.fft.rfft(filt, n=total, axis=1)
    spec_b = jnp.fft.rfft(signal, n=total, axis=1)
    return jnp.fft.irfft(spec_a * spec_b, n=total, axis=1)[:, :SINKS]

def long_corr(first, second):
    total = 2 * SINKS
    spec_a = jnp.fft.rfft(first, n=total, axis=1)
    spec_b = jnp.fft.rfft(second, n=total, axis=1)
    return jnp.fft.irfft(jnp.conj(spec_a) * spec_b, n=total, axis=1)[:, :SINKS]

def reference(features, sink_order, cotangent, w_in, short_taps, w_out, filter_one, filter_two):
    scale = 1.0 / math.sqrt(SINKS)
    block_ids = jnp.arange(BLOCKS, dtype=jnp.int32)[:, None] * jnp.ones((1, ROWS_DEV), jnp.int32)
    order = sink_order.astype(jnp.int32)
    feat_blocks = features.reshape(D, BLOCKS, ROWS_DEV)
    seq_input = feat_blocks[:, block_ids, order].reshape(D, SINKS)
    projected = jnp.dot(w_in, seq_input, preferred_element_type=jnp.float32)
    padded = jnp.pad(projected, ((0, 0), (2, 0)))
    mixed = short_taps[:, 0:1] * padded[:, 2:2 + SINKS]
    for offset in range(1, 3):
        mixed = mixed + short_taps[:, offset:offset + 1] * padded[:, 2 - offset:2 - offset + SINKS]
    streams = mixed.astype(jnp.bfloat16)
    value = streams[:D].astype(jnp.float32)
    gate_one = streams[D:2 * D].astype(jnp.float32)
    gate_two = streams[2 * D:].astype(jnp.float32)
    out_grad = jnp.dot(w_out.T, cotangent, preferred_element_type=jnp.float32).astype(jnp.bfloat16)
    out_gradf = out_grad.astype(jnp.float32)
    first_mix = long_conv(filter_one, value)
    first_out = gate_one * first_mix
    second_mix = long_conv(filter_two, first_out)
    second_out = (gate_two * second_mix).astype(jnp.bfloat16)
    grad_gate_two = (out_gradf * second_mix).astype(jnp.bfloat16)
    grad_second_mix = out_gradf * gate_two
    grad_first_out = long_corr(filter_two, grad_second_mix)
    grad_filter_two = long_corr(first_out, grad_second_mix) * scale
    grad_gate_one = (grad_first_out * first_mix).astype(jnp.bfloat16)
    grad_first_mix = grad_first_out * gate_one
    grad_value = long_corr(filter_one, grad_first_mix).astype(jnp.bfloat16)
    grad_filter_one = long_corr(value, grad_first_mix) * scale
    grad_streams = jnp.concatenate([grad_value, grad_gate_one, grad_gate_two], axis=0)
    grad_padded = jnp.pad(grad_streams, ((0, 0), (0, 2)))
    grad_mixed = short_taps[:, 0:1] * grad_padded[:, 0:SINKS]
    for offset in range(1, 3):
        grad_mixed = grad_mixed + short_taps[:, offset:offset + 1] * grad_padded[:, offset:offset + SINKS]
    grad_projected = grad_mixed.astype(jnp.bfloat16)
    grad_streamsf = grad_streams.astype(jnp.float32)
    tap_terms = []
    for offset in range(3):
        tap_terms.append(lax.optimization_barrier(jnp.sum(grad_streamsf * padded[:, 2 - offset:2 - offset + SINKS], axis=1)))
    grad_short = jnp.stack(tap_terms, axis=1) * scale
    grad_w_in = lax.dot_general(grad_projected, seq_input, (((1,), (1,)), ((), ())), preferred_element_type=jnp.float32) * scale
    grad_w_out = lax.dot_general(cotangent, second_out, (((1,), (1,)), ((), ())), preferred_element_type=jnp.float32) * scale
    grad_seq = lax.dot_general(w_in, grad_projected, (((0,), (0,)), ((), ())), preferred_element_type=jnp.float32).astype(jnp.bfloat16)
    grad_blocks = grad_seq.reshape(D, BLOCKS, ROWS_DEV)
    unordered = jnp.zeros_like(grad_blocks).at[:, block_ids, order].set(grad_blocks)
    grad_features = unordered.reshape(D, SINKS)
    return (grad_features, grad_w_in, grad_w_out, grad_short, grad_filter_one, grad_filter_two)
```

```python
import math

import jax
import jax.numpy as jnp
import numpy as np
from jax import lax
from jax.experimental import pallas as pl
from jax.experimental.pallas import tpu as pltpu
from jax.sharding import PartitionSpec as P

AXES = ("seq", "fft")
LANES = 128
bf16 = jnp.bfloat16
f32 = jnp.float32
PARAMS = pltpu.CompilerParams(vmem_limit_bytes=48 * 1024 * 1024)


def halves(table):
    high = table.astype(np.float32).astype(jnp.bfloat16)
    low = (table - high.astype(np.float64)).astype(np.float32).astype(jnp.bfloat16)
    return high, low


def make_tables(count, channels):
    length = count * LANES
    outer = np.arange(count, dtype=np.float64)
    inner = np.arange(LANES, dtype=np.float64)
    angle = 2.0 * np.pi * (outer[:, None] + 0.25) * outer[None, :] / count
    first = np.concatenate([np.cos(angle), -np.sin(angle)], axis=0)
    first = np.kron(first, np.eye(channels))
    turn = 2.0 * np.pi * (inner[:, None] * inner[None, :] % LANES) / LANES
    cos, sin = np.cos(turn), np.sin(turn)
    second = np.block([[cos, -sin], [sin, cos]])
    twist = 2.0 * np.pi * (outer[:, None] + 0.25) * inner[None, :] / length
    twist = np.repeat(twist, channels, axis=0)
    return dict(
        first=halves(first),
        first_back=halves(first.T / length),
        second=halves(second),
        second_back=halves(second.T),
        twist=(np.cos(twist).astype(np.float32), -np.sin(twist).astype(np.float32)),
    )


def split(value):
    high = value.astype(bf16)
    low = (value - high.astype(f32)).astype(bf16)
    return high, low


def dot(left, right):
    return jnp.dot(left, right, preferred_element_type=f32)


def dot_pairs(left, right):
    return dot(left[0], right[0]) + dot(left[0], right[1]) + dot(left[1], right[0])


def forward(signals, first, second, twist):
    rows = signals[0].shape[0]
    stage = dot_pairs(first, split(jnp.concatenate(signals, axis=1)))
    parts = []
    for i in range(len(signals)):
        re = stage[:rows, i * LANES : (i + 1) * LANES]
        im = stage[rows:, i * LANES : (i + 1) * LANES]
        parts.append(
            jnp.concatenate(
                [re * twist[0] - im * twist[1], re * twist[1] + im * twist[0]], axis=1
            )
        )
    spec = dot_pairs(split(jnp.concatenate(parts, axis=0)), second)
    return [
        (spec[i * rows : (i + 1) * rows, :LANES], spec[i * rows : (i + 1) * rows, LANES:])
        for i in range(len(signals))
    ]


def backward(spectra, first_back, second_back, twist):
    rows = spectra[0][0].shape[0]
    stacked = jnp.concatenate([jnp.concatenate(pair, axis=1) for pair in spectra], axis=0)
    stage = dot_pairs(split(stacked), second_back)
    parts = []
    for i in range(len(spectra)):
        re = stage[i * rows : (i + 1) * rows, :LANES]
        im = stage[i * rows : (i + 1) * rows, LANES:]
        parts.append(
            jnp.concatenate(
                [re * twist[0] + im * twist[1], im * twist[0] - re * twist[1]], axis=0
            )
        )
    out = dot_pairs(first_back, split(jnp.concatenate(parts, axis=1)))
    return [out[:, i * LANES : (i + 1) * LANES] for i in range(len(spectra))]


def times(a, b):
    return (a[0] * b[0] - a[1] * b[1], a[0] * b[1] + a[1] * b[0])


def conj_times(a, b):
    return (a[0] * b[0] + a[1] * b[1], a[0] * b[1] - a[1] * b[0])


def one_hot(order):
    size = order.shape[1]
    place = lax.broadcasted_iota(jnp.int32, (size, size), 0)
    return (place == order).astype(f32).astype(bf16)


def project_kernel(features, order, cotangent, w_in, w_out, streams_out, gather_out):
    width, row_count = features.shape
    seq_input = dot(features[...], one_hot(order[...])).astype(bf16)
    projected = dot(w_in[...], seq_input)
    out_grad = lax.dot_general(
        w_out[...], cotangent[...], (((0,), (0,)), ((), ())), preferred_element_type=f32
    )
    if len(streams_out.shape) == 3:
        blocks = streams_out.shape[0]
        parts = [projected[s * width : (s + 1) * width] for s in range(3)] + [out_grad]
        parts = [part.reshape(blocks, width // blocks, row_count) for part in parts]
        streams_out[...] = jnp.concatenate(parts, axis=1).astype(bf16)
    else:
        streams_out[: 3 * width] = projected.astype(bf16)
        streams_out[3 * width :] = out_grad.astype(bf16)
    gather_out[:width] = seq_input
    gather_out[width:] = cotangent[...]


def read_signal(ref, rows):
    if ref.shape[1] == LANES:
        return ref[...]
    return jnp.concatenate(
        [ref[:, i * LANES : (i + 1) * LANES] for i in range(ref.shape[1] // LANES)], axis=0
    )


def write_signal(ref, value):
    if ref.shape[1] == LANES:
        ref[...] = value
        return
    channels = ref.shape[0]
    for i in range(ref.shape[1] // LANES):
        ref[:, i * LANES : (i + 1) * LANES] = value[i * channels : (i + 1) * channels]


def filter_kernel(filter_one, filter_two, fh, fl, sh, sl, tr, ti, spec_one, spec_two):
    rows = spec_one.shape[0]
    signals = [read_signal(filter_one, rows), read_signal(filter_two, rows)]
    one, two = forward(
        signals, (fh[...], fl[...]), (sh[...], sl[...]), (tr[...], ti[...])
    )
    spec_one[:, :LANES] = one[0]
    spec_one[:, LANES:] = one[1]
    spec_two[:, :LANES] = two[0]
    spec_two[:, LANES:] = two[1]


def shifted(value, steps, channels):
    if steps == 0:
        return value
    rows, lanes = value.shape
    lane = lax.broadcasted_iota(jnp.int32, value.shape, 1)
    row = lax.broadcasted_iota(jnp.int32, value.shape, 0)
    turned = pltpu.roll(value, steps % lanes, 1)
    if steps > 0:
        carried = jnp.where(row < channels, 0.0, pltpu.roll(turned, channels, 0))
        return jnp.where(lane < steps, carried, turned)
    carried = jnp.where(row >= rows - channels, 0.0, pltpu.roll(turned, rows - channels, 0))
    return jnp.where(lane >= lanes + steps, carried, turned)


def mix_kernel(
    channels,
    scale,
    streams,
    taps,
    spec_one,
    spec_two,
    fh,
    fl,
    gh,
    gl,
    sh,
    sl,
    bh,
    bl,
    tr,
    ti,
    sent_out,
    short_out,
    grad_one,
    grad_two,
):
    twist = (tr[...], ti[...])
    rows = twist[0].shape[0]
    eight = taps.shape[0]
    first, second = (fh[...], fl[...]), (sh[...], sl[...])
    first_back, second_back = (gh[...], gl[...]), (bh[...], bl[...])
    if streams.shape[0] == 4 and streams.shape[1] == rows:
        pieces = [streams[s].astype(f32) for s in range(4)]
    else:
        whole = streams[...].astype(f32)
        pieces = [
            whole[:, s * channels : (s + 1) * channels].reshape(rows, LANES) for s in range(4)
        ]
    out_grad = pieces[3]

    def tap(s, k):
        column = jnp.broadcast_to(taps[:, 3 * s + k : 3 * s + k + 1], (eight, LANES))
        column = jnp.broadcast_to(column[None], (rows // eight, eight, LANES))
        return column.reshape(rows, LANES)

    late = [[shifted(pieces[s], k, channels) for k in range(3)] for s in range(3)]
    value, gate_one, gate_two = [
        sum(tap(s, k) * late[s][k] for k in range(3)) for s in range(3)
    ]
    h_one = (spec_one[:, :LANES], spec_one[:, LANES:])
    h_two = (spec_two[:, :LANES], spec_two[:, LANES:])
    value_spec, second_spec = forward([value, out_grad * gate_two], first, second, twist)
    first_mix, grad_first_out = backward(
        [times(h_one, value_spec), conj_times(h_two, second_spec)],
        first_back,
        second_back,
        twist,
    )
    first_spec, grad_first_spec = forward(
        [gate_one * first_mix, gate_one * grad_first_out], first, second, twist
    )
    second_mix, grad_value = backward(
        [times(h_two, first_spec), conj_times(h_one, grad_first_spec)],
        first_back,
        second_back,
        twist,
    )
    two, one = backward(
        [conj_times(first_spec, second_spec), conj_times(value_spec, grad_first_spec)],
        first_back,
        second_back,
        twist,
    )
    write_signal(grad_two, two * scale)
    write_signal(grad_one, one * scale)
    grads = [grad_value, grad_first_out * first_mix, out_grad * second_mix]
    sent = []
    lane = lax.broadcasted_iota(jnp.int32, (eight, LANES), 1)
    short = jnp.zeros((eight, LANES), f32)
    for s in range(3):
        sent.append(sum(tap(s, k) * shifted(grads[s], -k, channels) for k in range(3)))
        for k in range(3):
            folded = (grads[s] * late[s][k]).reshape(rows // eight, eight, LANES).sum(axis=0)
            total = jnp.sum(folded, axis=1, keepdims=True) * scale
            short = jnp.where(lane == 3 * s + k, total, short)
    sent.append(gate_two * second_mix)
    short_out[...] = short
    if len(sent_out.shape) == 3 and sent_out.shape[0] == 4 and sent_out.shape[1] == rows:
        for s in range(4):
            sent_out[s] = sent[s].astype(bf16)
    else:
        parts = [part.reshape(rows // channels, channels, LANES) for part in sent]
        sent_out[...] = jnp.concatenate(parts, axis=1).astype(bf16)


def weights_kernel(channels, scale, sent, gathered, short, out):
    blocks = sent.shape[0]
    width = gathered.shape[1] // 2
    total = jnp.zeros((4 * channels, 2 * width), f32)
    step = 2 if blocks % 2 == 0 else 1
    for i in range(0, blocks, step):
        left = jnp.concatenate([sent[i + j] for j in range(step)], axis=1)
        right = jnp.concatenate([gathered[i + j] for j in range(step)], axis=1)
        total = total + lax.dot_general(
            left, right, (((1,), (1,)), ((), ())), preferred_element_type=f32
        )
    total = total * scale
    parts = []
    for h in range(width // LANES):
        low, high = h * LANES, (h + 1) * LANES
        parts.append(total[: 3 * channels, low:high])
        parts.append(total[3 * channels :, width + low : width + high])
    parts.append(short[...])
    own = jnp.concatenate(parts, axis=0)
    own = jnp.broadcast_to(own[None], (blocks,) + own.shape)
    moved = sent[...].astype(f32)[:, : 3 * channels]
    out[...] = jnp.concatenate([moved, own], axis=1).astype(bf16)


def unorder(grad_projected, w_in, order):
    grad_seq = lax.dot_general(
        w_in, grad_projected, (((0,), (0,)), ((), ())), preferred_element_type=f32
    ).astype(bf16)
    return lax.dot_general(
        grad_seq, one_hot(order), (((1,), (1,)), ((), ())), preferred_element_type=f32
    ).astype(bf16)


def finish_kernel(channels, back, w_in, order, features_out, w_in_out, w_out_out, short_out):
    width = w_in.shape[1]
    blocks = back.shape[0]
    whole = back[...].astype(f32)

    def rows_of(start):
        return whole[:, start : start + channels].reshape(blocks * channels, LANES)

    moved = jnp.concatenate([rows_of(s * channels) for s in range(3)], axis=0).astype(bf16)
    features_out[...] = unorder(moved, w_in[...], order[...])
    for h in range(width // LANES):
        low, high = h * LANES, (h + 1) * LANES
        base = 3 * channels + 4 * channels * h
        for s in range(3):
            w_in_out[s * width : (s + 1) * width, low:high] = rows_of(base + s * channels)
        w_out_out[low:high, :] = rows_of(base + 3 * channels).T
    short = rows_of(3 * channels + 4 * channels * (width // LANES))
    for s in range(3):
        short_out[s * width : (s + 1) * width, :] = short[:, 3 * s : 3 * s + 3]


def features_kernel(moved, w_in, order, features_out):
    features_out[...] = unorder(moved[...], w_in[...], order[...])


def shape(dims, dtype=f32):
    return jax.ShapeDtypeStruct(dims, dtype)


def local(features, sink_order, cotangent, w_in, short_taps, w_out, filter_one, filter_two):
    width, row_count = features.shape
    blocks = lax.axis_size("seq") * lax.axis_size("fft")
    channels, length = filter_one.shape
    rows = channels * blocks
    scale = 1.0 / math.sqrt(length)
    whole = channels % 8 == 0
    tables = make_tables(blocks, channels)
    eight = channels if whole else 8
    mine = lax.axis_index(AXES)

    def call(kernel, outs, *args):
        return pl.pallas_call(kernel, out_shape=outs, compiler_params=PARAMS)(*args)

    dims = (blocks, 4 * channels, LANES) if whole else (4 * width, LANES)
    streams, own = call(
        project_kernel,
        (shape(dims, bf16), shape((2 * width, row_count), bf16)),
        features,
        sink_order,
        cotangent,
        w_in,
        w_out,
    )
    if not whole:
        streams = streams.reshape(4, blocks, channels, LANES).transpose(1, 0, 2, 3)
        streams = streams.reshape(blocks, 4 * channels, LANES)
    gathered = lax.all_gather(own, AXES, axis=0, tiled=False)
    arrived = lax.all_to_all(streams, AXES, split_axis=0, concat_axis=0, tiled=True)
    taps = lax.dynamic_slice_in_dim(short_taps.reshape(3, width, 3), mine * channels, channels, 1)
    taps = taps.transpose(1, 0, 2).reshape(channels, 9)
    if not whole:
        taps = jnp.tile(taps, (8 // channels, 1))
        arrived = arrived.reshape(blocks, 4, channels, LANES).transpose(1, 0, 2, 3)
        arrived = arrived.reshape(4, rows, LANES)
        filter_one, filter_two = [
            h.reshape(channels, blocks, LANES).transpose(1, 0, 2).reshape(rows, LANES)
            for h in (filter_one, filter_two)
        ]
    spec = shape((rows, 2 * LANES))
    spec_one, spec_two = call(
        filter_kernel,
        (spec, spec),
        filter_one,
        filter_two,
        *tables["first"],
        *tables["second"],
        *tables["twist"],
    )
    dims = (blocks, 4 * channels, LANES) if whole else (4, rows, LANES)
    sent, short, grad_one, grad_two = call(
        lambda *refs: mix_kernel(channels, scale, *refs),
        (
            shape(dims, bf16),
            shape((eight, LANES)),
            shape(filter_one.shape),
            shape(filter_two.shape),
        ),
        arrived,
        taps,
        spec_one,
        spec_two,
        *tables["first"],
        *tables["first_back"],
        *tables["second"],
        *tables["second_back"],
        *tables["twist"],
    )
    height = channels * (4 + 4 * (width // LANES))
    if whole:
        packed = call(
            lambda *refs: weights_kernel(channels, scale, *refs),
            shape((blocks, height, LANES), bf16),
            sent,
            gathered,
            short,
        )
        back = lax.all_to_all(packed, AXES, split_axis=0, concat_axis=0, tiled=True)
        outs = call(
            lambda *refs: finish_kernel(channels, *refs),
            (
                shape(features.shape, bf16),
                shape((3 * width, width)),
                shape((width, width)),
                shape((3 * width, 3)),
            ),
            back,
            w_in,
            sink_order,
        )
        return (*outs, grad_one, grad_two)
    sent = sent.reshape(4, blocks, channels, LANES)
    grad_in = jnp.einsum(
        "sbcp,bwp->scw", sent[:3], gathered[:, :width], preferred_element_type=f32
    )
    grad_out = jnp.einsum(
        "bcp,bwp->cw", sent[3], gathered[:, width:], preferred_element_type=f32
    )
    own = jnp.concatenate([grad_in, grad_out[None]]) * scale
    own = own.reshape(4 * channels * (width // LANES), LANES)
    short = short.reshape(8 // channels, channels, LANES).sum(axis=0)
    own = jnp.concatenate([own, short]).astype(bf16)
    moved = sent[:3].transpose(1, 0, 2, 3).reshape(blocks, 3 * channels, LANES)
    own = jnp.broadcast_to(own[None], (blocks,) + own.shape)
    packed = jnp.concatenate([moved, own], axis=1)
    back = lax.all_to_all(packed, AXES, split_axis=0, concat_axis=0, tiled=True)
    moved = back[:, : 3 * channels].reshape(blocks, 3, channels, LANES)
    moved = moved.transpose(1, 0, 2, 3).reshape(3 * width, LANES)
    weights = back[:, 3 * channels : height - channels].astype(f32)
    weights = weights.reshape(blocks, 4, channels, width).transpose(1, 0, 2, 3)
    weights = weights.reshape(4 * width, width)
    short = back[:, height - channels :, :9].astype(f32).reshape(width, 3, 3)
    short = short.transpose(1, 0, 2).reshape(3 * width, 3)
    grad_features = call(
        features_kernel, shape(features.shape, bf16), moved, w_in, sink_order
    )
    grad_one, grad_two = [
        g.reshape(blocks, channels, LANES).transpose(1, 0, 2).reshape(channels, length)
        for g in (grad_one, grad_two)
    ]
    return (
        grad_features,
        weights[: 3 * width],
        weights[3 * width :].T,
        short,
        grad_one,
        grad_two,
    )


def solution(mesh):
    columns, blocks_first, copied = P(None, AXES), P(AXES, None), P()
    return jax.shard_map(
        local,
        mesh=mesh,
        in_specs=(
            columns,
            blocks_first,
            columns,
            copied,
            copied,
            copied,
            blocks_first,
            blocks_first,
        ),
        out_specs=(columns, copied, copied, copied, blocks_first, blocks_first),
        check_vma=False,
    )
```

```python
import math

import jax
import jax.numpy as jnp
import numpy as np
from jax import lax
from jax.experimental import pallas as pl
from jax.experimental.pallas import tpu as pltpu
from jax.sharding import PartitionSpec as P

AXES = ("seq", "fft")
LANES = 128
bf16 = jnp.bfloat16
f32 = jnp.float32
PARAMS = pltpu.CompilerParams(vmem_limit_bytes=48 * 1024 * 1024)


def halves(table):
    high = table.astype(np.float32).astype(jnp.bfloat16)
    low = (table - high.astype(np.float64)).astype(np.float32).astype(jnp.bfloat16)
    return high, low


def make_tables(count, channels):
    length = count * LANES
    outer = np.arange(count, dtype=np.float64)
    inner = np.arange(LANES, dtype=np.float64)
    angle = 2.0 * np.pi * (outer[:, None] + 0.25) * outer[None, :] / count
    first = np.concatenate([np.cos(angle), -np.sin(angle)], axis=0)
    first = np.kron(first, np.eye(channels))
    turn = 2.0 * np.pi * (inner[:, None] * inner[None, :] % LANES) / LANES
    cos, sin = np.cos(turn), np.sin(turn)
    second = np.block([[cos, -sin], [sin, cos]])
    twist = 2.0 * np.pi * (outer[:, None] + 0.25) * inner[None, :] / length
    twist = np.repeat(twist, channels, axis=0)
    back = first.T / length
    rows = count * channels
    back = np.concatenate([back[:, :rows], back[:, rows:]], axis=0)
    packed = [half for t in (first, back, second, second.T) for half in halves(t)]
    twist = np.concatenate([np.cos(twist), -np.sin(twist)], axis=1).astype(np.float32)
    return np.concatenate(packed, axis=0), twist


def tables_of(table, twist):
    rows = twist.shape[0]
    at, found = 0, []
    for size in (2 * rows, 2 * rows, 2 * LANES, 2 * LANES):
        pair = []
        for half in range(2):
            pair.append(table[at : at + size])
            at += size
        found.append(tuple(pair))
    found[1] = tuple(jnp.concatenate([t[:rows], t[rows:]], axis=1) for t in found[1])
    return (*found, (twist[:, :LANES], twist[:, LANES:]))


def split(value):
    high = value.astype(bf16)
    low = (value - high.astype(f32)).astype(bf16)
    return high, low


def dot(left, right):
    return jnp.dot(left, right, preferred_element_type=f32)


def dot_pairs(left, right):
    return dot(left[0], right[0]) + dot(left[0], right[1]) + dot(left[1], right[0])


def forward(signals, first, second, twist):
    rows = signals[0].shape[0]
    stage = dot_pairs(first, split(jnp.concatenate(signals, axis=1)))
    parts = []
    for i in range(len(signals)):
        re = stage[:rows, i * LANES : (i + 1) * LANES]
        im = stage[rows:, i * LANES : (i + 1) * LANES]
        parts.append(
            jnp.concatenate(
                [re * twist[0] - im * twist[1], re * twist[1] + im * twist[0]], axis=1
            )
        )
    spec = dot_pairs(split(jnp.concatenate(parts, axis=0)), second)
    return [
        (spec[i * rows : (i + 1) * rows, :LANES], spec[i * rows : (i + 1) * rows, LANES:])
        for i in range(len(signals))
    ]


def backward(spectra, first_back, second_back, twist):
    rows = spectra[0][0].shape[0]
    stacked = jnp.concatenate([jnp.concatenate(pair, axis=1) for pair in spectra], axis=0)
    stage = dot_pairs(split(stacked), second_back)
    parts = []
    for i in range(len(spectra)):
        re = stage[i * rows : (i + 1) * rows, :LANES]
        im = stage[i * rows : (i + 1) * rows, LANES:]
        parts.append(
            jnp.concatenate(
                [re * twist[0] + im * twist[1], im * twist[0] - re * twist[1]], axis=0
            )
        )
    out = dot_pairs(first_back, split(jnp.concatenate(parts, axis=1)))
    return [out[:, i * LANES : (i + 1) * LANES] for i in range(len(spectra))]


def times(a, b):
    return (a[0] * b[0] - a[1] * b[1], a[0] * b[1] + a[1] * b[0])


def conj_times(a, b):
    return (a[0] * b[0] + a[1] * b[1], a[0] * b[1] - a[1] * b[0])


def one_hot(order):
    size = order.shape[1]
    place = lax.broadcasted_iota(jnp.int32, (size, size), 0)
    return (place == order).astype(f32).astype(bf16)


def project_kernel(
    features_at,
    order_at,
    cotangent_at,
    w_in_at,
    w_out_at,
    streams_out,
    gather_out,
    features,
    order,
    cotangent,
    w_in,
    w_out,
    done,
):
    copies = [
        pltpu.make_async_copy(source, target, done.at[i])
        for i, (source, target) in enumerate(
            [
                (order_at, order),
                (features_at, features),
                (w_in_at, w_in),
                (cotangent_at, cotangent),
                (w_out_at, w_out),
            ]
        )
    ]
    for copy in copies:
        copy.start()
    width, row_count = features.shape
    copies[0].wait()
    copies[1].wait()
    seq_input = dot(features[...], one_hot(order[...])).astype(bf16)
    copies[2].wait()
    projected = dot(w_in[...], seq_input)
    copies[3].wait()
    copies[4].wait()
    out_grad = lax.dot_general(
        w_out[...], cotangent[...], (((0,), (0,)), ((), ())), preferred_element_type=f32
    )
    if len(streams_out.shape) == 3:
        blocks = streams_out.shape[0]
        parts = [projected[s * width : (s + 1) * width] for s in range(3)] + [out_grad]
        parts = [part.reshape(blocks, width // blocks, row_count) for part in parts]
        streams_out[...] = jnp.concatenate(parts, axis=1).astype(bf16)
    else:
        streams_out[: 3 * width] = projected.astype(bf16)
        streams_out[3 * width :] = out_grad.astype(bf16)
    gather_out[:width] = seq_input
    gather_out[width:] = cotangent[...]


def read_signal(ref, rows):
    if ref.shape[1] == LANES:
        return ref[...]
    return jnp.concatenate(
        [ref[:, i * LANES : (i + 1) * LANES] for i in range(ref.shape[1] // LANES)], axis=0
    )


def write_signal(ref, value):
    if ref.shape[1] == LANES:
        ref[...] = value
        return
    channels = ref.shape[0]
    for i in range(ref.shape[1] // LANES):
        ref[:, i * LANES : (i + 1) * LANES] = value[i * channels : (i + 1) * channels]


def filter_kernel(
    filter_one, filter_two, table, twist, spec_one, spec_two, table_out, twist_out
):
    rows = spec_one.shape[0]
    signals = [read_signal(filter_one, rows), read_signal(filter_two, rows)]
    first, _, second, _, turns = tables_of(table, twist)
    one, two = forward(signals, first, second, turns)
    spec_one[...] = jnp.concatenate(one, axis=1)
    spec_two[...] = jnp.concatenate(two, axis=1)
    table_out[...] = table[...]
    twist_out[...] = twist[...]


def shifted(value, steps, channels):
    if steps == 0:
        return value
    rows, lanes = value.shape
    lane = lax.broadcasted_iota(jnp.int32, value.shape, 1)
    row = lax.broadcasted_iota(jnp.int32, value.shape, 0)
    turned = pltpu.roll(value, steps % lanes, 1)
    if steps > 0:
        carried = jnp.where(row < channels, 0.0, pltpu.roll(turned, channels, 0))
        return jnp.where(lane < steps, carried, turned)
    carried = jnp.where(row >= rows - channels, 0.0, pltpu.roll(turned, rows - channels, 0))
    return jnp.where(lane >= lanes + steps, carried, turned)


def mix_kernel(
    channels,
    scale,
    streams,
    taps,
    spec_one,
    spec_two,
    table,
    twist,
    sent_out,
    short_out,
    product_one,
    product_two,
):
    rows = twist.shape[0]
    eight = taps.shape[0]
    first, first_back, second, second_back, twist = tables_of(table, twist)
    if streams.shape[0] == 4 and streams.shape[1] == rows:
        pieces = [streams[s].astype(f32) for s in range(4)]
    else:
        whole = streams[...].astype(f32)
        pieces = [
            whole[:, s * channels : (s + 1) * channels].reshape(rows, LANES) for s in range(4)
        ]
    out_grad = pieces[3]

    def tap(s, k):
        column = jnp.broadcast_to(taps[:, 3 * s + k : 3 * s + k + 1], (eight, LANES))
        column = jnp.broadcast_to(column[None], (rows // eight, eight, LANES))
        return column.reshape(rows, LANES)

    late = [[shifted(pieces[s], k, channels) for k in range(3)] for s in range(3)]
    value, gate_one, gate_two = [
        sum(tap(s, k) * late[s][k] for k in range(3)) for s in range(3)
    ]
    h_one = (spec_one[:, :LANES], spec_one[:, LANES:])
    h_two = (spec_two[:, :LANES], spec_two[:, LANES:])
    value_spec, second_spec = forward([value, out_grad * gate_two], first, second, twist)
    first_mix, grad_first_out = backward(
        [times(h_one, value_spec), conj_times(h_two, second_spec)],
        first_back,
        second_back,
        twist,
    )
    first_spec, grad_first_spec = forward(
        [gate_one * first_mix, gate_one * grad_first_out], first, second, twist
    )
    second_mix, grad_value = backward(
        [times(h_two, first_spec), conj_times(h_one, grad_first_spec)],
        first_back,
        second_back,
        twist,
    )
    product_one[...] = jnp.concatenate(conj_times(value_spec, grad_first_spec), axis=1)
    product_two[...] = jnp.concatenate(conj_times(first_spec, second_spec), axis=1)
    grads = [grad_value, grad_first_out * first_mix, out_grad * second_mix]
    sent = []
    lane = lax.broadcasted_iota(jnp.int32, (eight, LANES), 1)
    short = jnp.zeros((eight, LANES), f32)
    for s in range(3):
        sent.append(sum(tap(s, k) * shifted(grads[s], -k, channels) for k in range(3)))
        for k in range(3):
            folded = (grads[s] * late[s][k]).reshape(rows // eight, eight, LANES).sum(axis=0)
            total = jnp.sum(folded, axis=1, keepdims=True) * scale
            short = jnp.where(lane == 3 * s + k, total, short)
    sent.append(gate_two * second_mix)
    short_out[...] = short
    if len(sent_out.shape) == 3 and sent_out.shape[0] == 4 and sent_out.shape[1] == rows:
        for s in range(4):
            sent_out[s] = sent[s].astype(bf16)
    else:
        parts = [part.reshape(rows // channels, channels, LANES) for part in sent]
        sent_out[...] = jnp.concatenate(parts, axis=1).astype(bf16)


def filter_grads_kernel(scale, product_one, product_two, table, twist, grad_one, grad_two):
    _, first_back, _, second_back, twist = tables_of(table, twist)
    spectra = [(ref[:, :LANES], ref[:, LANES:]) for ref in (product_one, product_two)]
    one, two = backward(spectra, first_back, second_back, twist)
    write_signal(grad_one, one * scale)
    write_signal(grad_two, two * scale)


def weights_kernel(channels, scale, lines, met, gathered, partial_out, moved_out):
    plane, width = gathered.shape[0], gathered.shape[1] // 2
    height = 4 * channels
    total = jnp.zeros((lines * height, 2 * width), f32)
    step = 2 if plane % 2 == 0 else 1
    for i in range(0, plane, step):
        left = jnp.concatenate(
            [
                jnp.concatenate([met[line * plane + i + j] for line in range(lines)], axis=0)
                for j in range(step)
            ],
            axis=1,
        )
        right = jnp.concatenate([gathered[i + j] for j in range(step)], axis=1)
        total = total + lax.dot_general(
            left, right, (((1,), (1,)), ((), ())), preferred_element_type=f32
        )
    total = total * scale
    for line in range(lines):
        parts = []
        for h in range(width // LANES):
            low, high = h * LANES, (h + 1) * LANES
            base = line * height
            parts.append(total[base : base + 3 * channels, low:high])
            parts.append(total[base + 3 * channels : base + height, width + low : width + high])
        partial_out[line] = jnp.concatenate(parts, axis=0).astype(bf16)
    whole = met[...].astype(f32)
    parts = [
        whole[line * plane : (line + 1) * plane, : 3 * channels] for line in range(lines)
    ]
    moved_out[...] = jnp.concatenate(parts, axis=1).astype(bf16)


def sum_kernel(partials, short, out):
    total = jnp.sum(partials[...].astype(f32), axis=0)
    short = short[...]
    out[...] = jnp.concatenate([total, short, jnp.zeros_like(short)], axis=0).astype(bf16)


def unorder(grad_projected, w_in, order):
    grad_seq = lax.dot_general(
        w_in, grad_projected, (((0,), (0,)), ((), ())), preferred_element_type=f32
    ).astype(bf16)
    return lax.dot_general(
        grad_seq, one_hot(order), (((1,), (1,)), ((), ())), preferred_element_type=f32
    ).astype(bf16)


def finish_kernel(channels, all_rows, w_in_out, w_out_out, short_out):
    blocks = all_rows.shape[0]
    width = w_out_out.shape[0]
    whole = all_rows[...].astype(f32)

    def rows_of(start):
        return whole[:, start : start + channels].reshape(blocks * channels, LANES)

    for h in range(width // LANES):
        low, high = h * LANES, (h + 1) * LANES
        base = 4 * channels * h
        for s in range(3):
            w_in_out[s * width : (s + 1) * width, low:high] = rows_of(base + s * channels)
        w_out_out[low:high, :] = rows_of(base + 3 * channels).T
    short = rows_of(4 * channels * (width // LANES)).T
    for s in range(3):
        short_out[:, s * width : (s + 1) * width] = short[3 * s : 3 * s + 3, :]


def moved_kernel(channels, moved, w_in, order, features_out):
    plane = moved.shape[0]
    lines = moved.shape[1] // (3 * channels)
    whole = moved[...].astype(f32)
    parts = []
    for s in range(3):
        for line in range(lines):
            start = (3 * line + s) * channels
            parts.append(whole[:, start : start + channels].reshape(plane * channels, LANES))
    grad_projected = jnp.concatenate(parts, axis=0).astype(bf16)
    features_out[...] = unorder(grad_projected, w_in[...], order[...])


def features_kernel(moved, w_in, order, features_out):
    features_out[...] = unorder(moved[...], w_in[...], order[...])


def shape(dims, dtype=f32):
    return jax.ShapeDtypeStruct(dims, dtype)


def local(features, sink_order, cotangent, w_in, short_taps, w_out, filter_one, filter_two):
    width, row_count = features.shape
    lines, plane = lax.axis_size("seq"), lax.axis_size("fft")
    blocks = lines * plane
    channels, length = filter_one.shape
    rows = channels * blocks
    scale = 1.0 / math.sqrt(length)
    whole = channels % 8 == 0
    table, twist = make_tables(blocks, channels)
    eight = channels if whole else 8
    mine = lax.axis_index(AXES)

    def call(kernel, outs, *args, **options):
        return pl.pallas_call(kernel, out_shape=outs, compiler_params=PARAMS, **options)(*args)

    dims = (blocks, 4 * channels, LANES) if whole else (4 * width, LANES)
    streams, own = pl.pallas_call(
        project_kernel,
        out_shape=(shape(dims, bf16), shape((2 * width, row_count), bf16)),
        in_specs=[pl.BlockSpec(memory_space=pl.ANY)] * 5,
        scratch_shapes=[
            pltpu.VMEM(a.shape, a.dtype)
            for a in (features, sink_order, cotangent, w_in, w_out)
        ]
        + [pltpu.SemaphoreType.DMA((5,))],
        compiler_params=pltpu.CompilerParams(vmem_limit_bytes=60 * 1024 * 1024),
    )(features, sink_order, cotangent, w_in, w_out)
    if not whole:
        streams = streams.reshape(4, blocks, channels, LANES).transpose(1, 0, 2, 3)
        streams = streams.reshape(blocks, 4 * channels, LANES)
    gathered = lax.all_gather(own, "fft" if whole else AXES, axis=0, tiled=False)
    arrived = lax.all_to_all(streams, AXES, split_axis=0, concat_axis=0, tiled=True)
    taps = lax.dynamic_slice_in_dim(short_taps.reshape(3, width, 3), mine * channels, channels, 1)
    taps = taps.transpose(1, 0, 2).reshape(channels, 9)
    if not whole:
        taps = jnp.tile(taps, (8 // channels, 1))
        arrived = arrived.reshape(blocks, 4, channels, LANES).transpose(1, 0, 2, 3)
        arrived = arrived.reshape(4, rows, LANES)
        filter_one, filter_two = [
            h.reshape(channels, blocks, LANES).transpose(1, 0, 2).reshape(rows, LANES)
            for h in (filter_one, filter_two)
        ]
    spec = shape((rows, 2 * LANES))
    spec_one, spec_two, table, twist = call(
        filter_kernel,
        (spec, spec, shape(table.shape, bf16), shape(twist.shape)),
        filter_one,
        filter_two,
        table,
        twist,
    )
    dims = (blocks, 4 * channels, LANES) if whole else (4, rows, LANES)
    sent, short, product_one, product_two = call(
        lambda *refs: mix_kernel(channels, scale, *refs),
        (shape(dims, bf16), shape((eight, LANES)), spec, spec),
        arrived,
        taps,
        spec_one,
        spec_two,
        table,
        twist,
    )
    grad_one, grad_two = call(
        lambda *refs: filter_grads_kernel(scale, *refs),
        (shape(filter_one.shape), shape(filter_two.shape)),
        product_one,
        product_two,
        table,
        twist,
    )
    height = channels * 4 * (width // LANES)
    if whole:
        met = lax.all_to_all(sent, "seq", split_axis=0, concat_axis=0, tiled=True)
        partial, moved = call(
            lambda *refs: weights_kernel(channels, scale, lines, *refs),
            (
                shape((lines, height, LANES), bf16),
                shape((plane, 3 * lines * channels, LANES), bf16),
            ),
            met,
            gathered,
        )
        partial = lax.all_to_all(partial, "seq", split_axis=0, concat_axis=0, tiled=True)
        own = call(sum_kernel, shape((height + 2 * channels, LANES), bf16), partial, short)
        all_rows = lax.all_gather(own, AXES, axis=0, tiled=False)
        moved = lax.all_to_all(moved, "fft", split_axis=0, concat_axis=0, tiled=True)
        grad_features = call(
            lambda *refs: moved_kernel(channels, *refs),
            shape(features.shape, bf16),
            moved,
            w_in,
            sink_order,
        )
        grad_w_in, grad_w_out, short = call(
            lambda *refs: finish_kernel(channels, *refs),
            (shape((3 * width, width)), shape((width, width)), shape((3, 3 * width))),
            all_rows,
        )
        return (grad_features, grad_w_in, grad_w_out, short.T, grad_one, grad_two)
    sent = sent.reshape(4, blocks, channels, LANES)
    grad_in = jnp.einsum(
        "sbcp,bwp->scw", sent[:3], gathered[:, :width], preferred_element_type=f32
    )
    grad_out = jnp.einsum(
        "bcp,bwp->cw", sent[3], gathered[:, width:], preferred_element_type=f32
    )
    own = jnp.concatenate([grad_in, grad_out[None]]) * scale
    own = own.reshape(height, LANES)
    short = short.reshape(8 // channels, channels, LANES).sum(axis=0)
    own = jnp.concatenate([own, short]).astype(bf16)
    moved = sent[:3].transpose(1, 0, 2, 3).reshape(blocks, 3 * channels, LANES)
    own = jnp.broadcast_to(own[None], (blocks,) + own.shape)
    packed = jnp.concatenate([moved, own], axis=1)
    back = lax.all_to_all(packed, AXES, split_axis=0, concat_axis=0, tiled=True)
    moved = back[:, : 3 * channels].reshape(blocks, 3, channels, LANES)
    moved = moved.transpose(1, 0, 2, 3).reshape(3 * width, LANES)
    weights = back[:, 3 * channels : 3 * channels + height].astype(f32)
    weights = weights.reshape(blocks, 4, channels, width).transpose(1, 0, 2, 3)
    weights = weights.reshape(4 * width, width)
    short = back[:, 3 * channels + height :, :9].astype(f32).reshape(width, 3, 3)
    short = short.transpose(1, 0, 2).reshape(3 * width, 3)
    grad_features = call(
        features_kernel, shape(features.shape, bf16), moved, w_in, sink_order
    )
    grad_one, grad_two = [
        g.reshape(blocks, channels, LANES).transpose(1, 0, 2).reshape(channels, length)
        for g in (grad_one, grad_two)
    ]
    return (
        grad_features,
        weights[: 3 * width],
        weights[3 * width :].T,
        short,
        grad_one,
        grad_two,
    )


def solution(mesh):
    columns, blocks_first, copied = P(None, AXES), P(AXES, None), P()
    return jax.shard_map(
        local,
        mesh=mesh,
        in_specs=(
            columns,
            blocks_first,
            columns,
            copied,
            copied,
            copied,
            blocks_first,
            blocks_first,
        ),
        out_specs=(columns, copied, copied, copied, blocks_first, blocks_first),
        check_vma=False,
    )
```

```python
import math

import jax
import jax.numpy as jnp
import numpy as np
from jax import lax
from jax.experimental import pallas as pl
from jax.experimental.pallas import tpu as pltpu
from jax.sharding import PartitionSpec as P

AXES = ("seq", "fft")
LANES = 128
bf16 = jnp.bfloat16
f32 = jnp.float32
PARAMS = pltpu.CompilerParams(vmem_limit_bytes=48 * 1024 * 1024)


def halves(table):
    high = table.astype(np.float32).astype(jnp.bfloat16)
    low = (table - high.astype(np.float64)).astype(np.float32).astype(jnp.bfloat16)
    return high, low


def make_tables(count, channels):
    length = count * LANES
    outer = np.arange(count, dtype=np.float64)
    inner = np.arange(LANES, dtype=np.float64)
    angle = 2.0 * np.pi * (outer[:, None] + 0.25) * outer[None, :] / count
    first = np.concatenate([np.cos(angle), -np.sin(angle)], axis=0)
    first = np.kron(first, np.eye(channels))
    turn = 2.0 * np.pi * (inner[:, None] * inner[None, :] % LANES) / LANES
    cos, sin = np.cos(turn), np.sin(turn)
    second = np.block([[cos, -sin], [sin, cos]])
    twist = 2.0 * np.pi * (outer[:, None] + 0.25) * inner[None, :] / length
    twist = np.repeat(twist, channels, axis=0)
    back = first.T / length
    rows = count * channels
    back = np.concatenate([back[:, :rows], back[:, rows:]], axis=0)
    packed = [half for t in (first, back, second, second.T) for half in halves(t)]
    twist = np.concatenate([np.cos(twist), -np.sin(twist)], axis=1).astype(np.float32)
    return np.concatenate(packed, axis=0), twist


def tables_of(table, twist):
    rows = twist.shape[0]
    at, found = 0, []
    for size in (2 * rows, 2 * rows, 2 * LANES, 2 * LANES):
        pair = []
        for half in range(2):
            pair.append(table[at : at + size])
            at += size
        found.append(tuple(pair))
    found[1] = tuple(jnp.concatenate([t[:rows], t[rows:]], axis=1) for t in found[1])
    return (*found, (twist[:, :LANES], twist[:, LANES:]))


def split(value):
    high = value.astype(bf16)
    low = (value - high.astype(f32)).astype(bf16)
    return high, low


def dot(left, right):
    return jnp.dot(left, right, preferred_element_type=f32)


def dot_pairs(left, right):
    return dot(left[0], right[0]) + dot(left[0], right[1]) + dot(left[1], right[0])


def forward(signals, first, second, twist):
    rows = signals[0].shape[0]
    stage = dot_pairs(first, split(jnp.concatenate(signals, axis=1)))
    parts = []
    for i in range(len(signals)):
        re = stage[:rows, i * LANES : (i + 1) * LANES]
        im = stage[rows:, i * LANES : (i + 1) * LANES]
        parts.append(
            jnp.concatenate(
                [re * twist[0] - im * twist[1], re * twist[1] + im * twist[0]], axis=1
            )
        )
    spec = dot_pairs(split(jnp.concatenate(parts, axis=0)), second)
    return [
        (spec[i * rows : (i + 1) * rows, :LANES], spec[i * rows : (i + 1) * rows, LANES:])
        for i in range(len(signals))
    ]


def backward(spectra, first_back, second_back, twist):
    rows = spectra[0][0].shape[0]
    stacked = jnp.concatenate([jnp.concatenate(pair, axis=1) for pair in spectra], axis=0)
    stage = dot_pairs(split(stacked), second_back)
    parts = []
    for i in range(len(spectra)):
        re = stage[i * rows : (i + 1) * rows, :LANES]
        im = stage[i * rows : (i + 1) * rows, LANES:]
        parts.append(
            jnp.concatenate(
                [re * twist[0] + im * twist[1], im * twist[0] - re * twist[1]], axis=0
            )
        )
    out = dot_pairs(first_back, split(jnp.concatenate(parts, axis=1)))
    return [out[:, i * LANES : (i + 1) * LANES] for i in range(len(spectra))]


def times(a, b):
    return (a[0] * b[0] - a[1] * b[1], a[0] * b[1] + a[1] * b[0])


def conj_times(a, b):
    return (a[0] * b[0] + a[1] * b[1], a[0] * b[1] - a[1] * b[0])


def one_hot(order):
    size = order.shape[1]
    place = lax.broadcasted_iota(jnp.int32, (size, size), 0)
    return (place == order).astype(f32).astype(bf16)


def project_kernel(
    features_at,
    order_at,
    cotangent_at,
    w_in_at,
    w_out_at,
    streams_out,
    gather_out,
    features,
    order,
    cotangent,
    w_in,
    w_out,
    done,
):
    copies = [
        pltpu.make_async_copy(source, target, done.at[i])
        for i, (source, target) in enumerate(
            [
                (order_at, order),
                (features_at, features),
                (w_in_at, w_in),
                (cotangent_at, cotangent),
                (w_out_at, w_out),
            ]
        )
    ]
    for copy in copies:
        copy.start()
    width, row_count = features.shape
    copies[0].wait()
    copies[1].wait()
    seq_input = dot(features[...], one_hot(order[...])).astype(bf16)
    copies[2].wait()
    projected = dot(w_in[...], seq_input)
    copies[3].wait()
    copies[4].wait()
    out_grad = lax.dot_general(
        w_out[...], cotangent[...], (((0,), (0,)), ((), ())), preferred_element_type=f32
    )
    if len(streams_out.shape) == 3:
        blocks = streams_out.shape[0]
        parts = [projected[s * width : (s + 1) * width] for s in range(3)] + [out_grad]
        parts = [part.reshape(blocks, width // blocks, row_count) for part in parts]
        streams_out[...] = jnp.concatenate(parts, axis=1).astype(bf16)
    else:
        streams_out[: 3 * width] = projected.astype(bf16)
        streams_out[3 * width :] = out_grad.astype(bf16)
    own = jnp.concatenate([seq_input, cotangent[...]], axis=0)
    if len(gather_out.shape) == 2:
        gather_out[...] = own
    else:
        for i in range(gather_out.shape[0]):
            gather_out[i] = own


def read_signal(ref, rows):
    if ref.shape[1] == LANES:
        return ref[...]
    return jnp.concatenate(
        [ref[:, i * LANES : (i + 1) * LANES] for i in range(ref.shape[1] // LANES)], axis=0
    )


def write_signal(ref, value):
    if ref.shape[1] == LANES:
        ref[...] = value
        return
    channels = ref.shape[0]
    for i in range(ref.shape[1] // LANES):
        ref[:, i * LANES : (i + 1) * LANES] = value[i * channels : (i + 1) * channels]


def filter_kernel(
    filter_one, filter_two, table, twist, spec_one, spec_two, table_out, twist_out
):
    rows = spec_one.shape[0]
    signals = [read_signal(filter_one, rows), read_signal(filter_two, rows)]
    first, _, second, _, turns = tables_of(table, twist)
    one, two = forward(signals, first, second, turns)
    spec_one[...] = jnp.concatenate(one, axis=1)
    spec_two[...] = jnp.concatenate(two, axis=1)
    table_out[...] = table[...]
    twist_out[...] = twist[...]


def shifted(value, steps, channels):
    if steps == 0:
        return value
    rows, lanes = value.shape
    lane = lax.broadcasted_iota(jnp.int32, value.shape, 1)
    row = lax.broadcasted_iota(jnp.int32, value.shape, 0)
    turned = pltpu.roll(value, steps % lanes, 1)
    if steps > 0:
        carried = jnp.where(row < channels, 0.0, pltpu.roll(turned, channels, 0))
        return jnp.where(lane < steps, carried, turned)
    carried = jnp.where(row >= rows - channels, 0.0, pltpu.roll(turned, rows - channels, 0))
    return jnp.where(lane >= lanes + steps, carried, turned)


def mix_kernel(
    channels,
    scale,
    streams,
    taps,
    spec_one,
    spec_two,
    table,
    twist,
    line,
    short_out,
    product_one,
    product_two,
    *sent_out,
):
    rows = twist.shape[0]
    eight = taps.shape[0]
    first, first_back, second, second_back, twist = tables_of(table, twist)
    if streams.shape[0] == 4 and streams.shape[1] == rows:
        pieces = [streams[s].astype(f32) for s in range(4)]
    else:
        whole = streams[...].astype(f32)
        pieces = [
            whole[:, s * channels : (s + 1) * channels].reshape(rows, LANES) for s in range(4)
        ]
    out_grad = pieces[3]

    def tap(s, k):
        column = jnp.broadcast_to(taps[:, 3 * s + k : 3 * s + k + 1], (eight, LANES))
        column = jnp.broadcast_to(column[None], (rows // eight, eight, LANES))
        return column.reshape(rows, LANES)

    late = [[shifted(pieces[s], k, channels) for k in range(3)] for s in range(3)]
    value, gate_one, gate_two = [
        sum(tap(s, k) * late[s][k] for k in range(3)) for s in range(3)
    ]
    h_one = (spec_one[:, :LANES], spec_one[:, LANES:])
    h_two = (spec_two[:, :LANES], spec_two[:, LANES:])
    value_spec, second_spec = forward([value, out_grad * gate_two], first, second, twist)
    first_mix, grad_first_out = backward(
        [times(h_one, value_spec), conj_times(h_two, second_spec)],
        first_back,
        second_back,
        twist,
    )
    first_spec, grad_first_spec = forward(
        [gate_one * first_mix, gate_one * grad_first_out], first, second, twist
    )
    second_mix, grad_value = backward(
        [times(h_two, first_spec), conj_times(h_one, grad_first_spec)],
        first_back,
        second_back,
        twist,
    )
    product_one[...] = jnp.concatenate(conj_times(value_spec, grad_first_spec), axis=1)
    product_two[...] = jnp.concatenate(conj_times(first_spec, second_spec), axis=1)
    grads = [grad_value, grad_first_out * first_mix, out_grad * second_mix]
    sent = []
    lane = lax.broadcasted_iota(jnp.int32, (eight, LANES), 1)
    short = jnp.zeros((eight, LANES), f32)
    for s in range(3):
        sent.append(sum(tap(s, k) * shifted(grads[s], -k, channels) for k in range(3)))
        for k in range(3):
            folded = (grads[s] * late[s][k]).reshape(rows // eight, eight, LANES).sum(axis=0)
            total = jnp.sum(folded, axis=1, keepdims=True) * scale
            short = jnp.where(lane == 3 * s + k, total, short)
    sent.append(gate_two * second_mix)
    short_out[...] = short
    if len(sent_out) == 1:
        for s in range(4):
            sent_out[0][s] = sent[s].astype(bf16)
        return
    parts = [part.reshape(rows // channels, channels, LANES) for part in sent]
    packed = jnp.concatenate(parts, axis=1).astype(bf16)
    *sent_out, store = sent_out
    lines, plane = store.shape[:2]
    for i in range(lines):
        store[i] = packed[i * plane : (i + 1) * plane]
    for step in range(lines):
        sent_out[step][...] = store[lax.rem(line[0] + step, lines)]


def filter_grads_kernel(scale, product_one, product_two, table, twist, grad_one, grad_two):
    _, first_back, _, second_back, twist = tables_of(table, twist)
    spectra = [(ref[:, :LANES], ref[:, LANES:]) for ref in (product_one, product_two)]
    one, two = backward(spectra, first_back, second_back, twist)
    write_signal(grad_one, one * scale)
    write_signal(grad_two, two * scale)


def weights_kernel(channels, scale, *refs):
    line, short, gathered, *met, partial_out, moved_out = refs
    lines = len(met)
    plane, width = gathered.shape[0], gathered.shape[1] // 2
    height = 4 * channels
    total = jnp.zeros((lines * height, 2 * width), f32)
    step = 2 if plane % 2 == 0 else 1
    for i in range(0, plane, step):
        left = jnp.concatenate(
            [jnp.concatenate([m[i + j] for m in met], axis=0) for j in range(step)], axis=1
        )
        right = jnp.concatenate([gathered[i + j] for j in range(step)], axis=1)
        total = total + lax.dot_general(
            left, right, (((1,), (1,)), ((), ())), preferred_element_type=f32
        )
    total = total * scale
    size = height * (width // LANES)
    for k in range(lines):
        parts = []
        for h in range(width // LANES):
            low, high = h * LANES, (h + 1) * LANES
            base = k * height
            parts.append(total[base : base + 3 * channels, low:high])
            parts.append(total[base + 3 * channels : base + height, width + low : width + high])
        owner = lax.rem(line[0] + lines - k, lines)
        spot = pl.ds(pl.multiple_of(owner * size, size), size)
        partial_out[spot] = jnp.concatenate(parts, axis=0).astype(bf16)
    tail = jnp.concatenate([short[...]] * lines, axis=0)
    owner = lax.broadcasted_iota(jnp.int32, tail.shape, 0) // channels
    partial_out[lines * size :] = jnp.where(owner == line[0], tail, 0.0).astype(bf16)
    parts = [m[...].astype(f32)[:, : 3 * channels] for m in met]
    moved_out[...] = jnp.concatenate(parts, axis=1).astype(bf16)


def sum_kernel(*refs):
    moved, *partials, out = refs
    total = sum(part[...].astype(f32) for part in partials).astype(bf16)
    size = total.shape[0]
    for i in range(out.shape[0]):
        out[i, :size] = total
        out[i, size:] = moved[i]


def unorder(grad_projected, w_in, order):
    grad_seq = lax.dot_general(
        w_in, grad_projected, (((0,), (0,)), ((), ())), preferred_element_type=f32
    ).astype(bf16)
    return lax.dot_general(
        grad_seq, one_hot(order), (((1,), (1,)), ((), ())), preferred_element_type=f32
    ).astype(bf16)


def finish_kernel(
    channels, lines, line, back, w_in, order, features_out, w_in_out, w_out_out, short_out, store
):
    plane, width = back.shape[0], w_in.shape[1]
    share = plane * channels
    whole = back[...].astype(f32)

    def rows_of(start):
        return whole[:, start : start + channels].reshape(share, LANES)

    height = 4 * channels
    size = height * (width // LANES)
    tail = lines * size + lines * channels
    for k in range(lines):
        owner = lax.rem(line[0] + lines - k, lines)
        for s in range(3):
            spot = pl.ds(pl.multiple_of(s * width + owner * share, share), share)
            store[spot] = rows_of(tail + (3 * k + s) * channels)
    features_out[...] = unorder(store[...].astype(bf16), w_in[...], order[...])
    for i in range(lines):
        for h in range(width // LANES):
            low, high = h * LANES, (h + 1) * LANES
            base = i * size + h * height
            for s in range(3):
                spot = s * width + i * share
                w_in_out[spot : spot + share, low:high] = rows_of(base + s * channels)
    for h in range(width // LANES):
        parts = [rows_of(i * size + h * height + 3 * channels) for i in range(lines)]
        w_out_out[h * LANES : (h + 1) * LANES, :] = jnp.concatenate(parts, axis=0).T
    parts = [rows_of(lines * size + i * channels) for i in range(lines)]
    short = jnp.concatenate(parts, axis=0).T
    for s in range(3):
        short_out[:, s * width : (s + 1) * width] = short[3 * s : 3 * s + 3, :]


def features_kernel(moved, w_in, order, features_out):
    features_out[...] = unorder(moved[...], w_in[...], order[...])


def shape(dims, dtype=f32):
    return jax.ShapeDtypeStruct(dims, dtype)


def local(features, sink_order, cotangent, w_in, short_taps, w_out, filter_one, filter_two):
    width, row_count = features.shape
    lines, plane = lax.axis_size("seq"), lax.axis_size("fft")
    blocks = lines * plane
    channels, length = filter_one.shape
    rows = channels * blocks
    scale = 1.0 / math.sqrt(length)
    whole = channels % 8 == 0
    table, twist = make_tables(blocks, channels)
    eight = channels if whole else 8
    mine = lax.axis_index(AXES)

    def call(kernel, outs, *args, **options):
        return pl.pallas_call(kernel, out_shape=outs, compiler_params=PARAMS, **options)(*args)

    dims = (blocks, 4 * channels, LANES) if whole else (4 * width, LANES)
    copies = (plane,) if whole else ()
    streams, own = pl.pallas_call(
        project_kernel,
        out_shape=(shape(dims, bf16), shape((*copies, 2 * width, row_count), bf16)),
        in_specs=[pl.BlockSpec(memory_space=pl.ANY)] * 5,
        scratch_shapes=[
            pltpu.VMEM(a.shape, a.dtype)
            for a in (features, sink_order, cotangent, w_in, w_out)
        ]
        + [pltpu.SemaphoreType.DMA((5,))],
        compiler_params=pltpu.CompilerParams(vmem_limit_bytes=60 * 1024 * 1024),
    )(features, sink_order, cotangent, w_in, w_out)
    if not whole:
        streams = streams.reshape(4, blocks, channels, LANES).transpose(1, 0, 2, 3)
        streams = streams.reshape(blocks, 4 * channels, LANES)
    if whole:
        gathered = lax.all_to_all(own, "fft", split_axis=0, concat_axis=0, tiled=True)
    else:
        gathered = lax.all_gather(own, AXES, axis=0, tiled=False)
    arrived = lax.all_to_all(streams, AXES, split_axis=0, concat_axis=0, tiled=True)
    taps = lax.dynamic_slice_in_dim(short_taps.reshape(3, width, 3), mine * channels, channels, 1)
    taps = taps.transpose(1, 0, 2).reshape(channels, 9)
    if not whole:
        taps = jnp.tile(taps, (8 // channels, 1))
        arrived = arrived.reshape(blocks, 4, channels, LANES).transpose(1, 0, 2, 3)
        arrived = arrived.reshape(4, rows, LANES)
        filter_one, filter_two = [
            h.reshape(channels, blocks, LANES).transpose(1, 0, 2).reshape(rows, LANES)
            for h in (filter_one, filter_two)
        ]
    spec = shape((rows, 2 * LANES))
    spec_one, spec_two, table, twist = call(
        filter_kernel,
        (spec, spec, shape(table.shape, bf16), shape(twist.shape)),
        filter_one,
        filter_two,
        table,
        twist,
    )
    line = lax.axis_index("seq").astype(jnp.int32).reshape(1)
    scalar = pl.BlockSpec(memory_space=pltpu.SMEM)
    held = pl.BlockSpec(memory_space=pltpu.VMEM)
    chunk = (plane, 4 * channels, LANES)
    dims = [shape(chunk, bf16)] * lines if whole else [shape((4, rows, LANES), bf16)]
    short, product_one, product_two, *sent = call(
        lambda *refs: mix_kernel(channels, scale, *refs),
        (shape((eight, LANES)), spec, spec, *dims),
        arrived,
        taps,
        spec_one,
        spec_two,
        table,
        twist,
        line,
        in_specs=[held] * 6 + [scalar],
        scratch_shapes=[pltpu.VMEM((lines, *chunk), bf16)] if whole else [],
    )
    grad_one, grad_two = call(
        lambda *refs: filter_grads_kernel(scale, *refs),
        (shape(filter_one.shape), shape(filter_two.shape)),
        product_one,
        product_two,
        table,
        twist,
    )
    height = channels * 4 * (width // LANES)
    if whole:
        def ahead(value, steps):
            pairs = [(i, (i + steps) % lines) for i in range(lines)]
            return lax.ppermute(value, "seq", pairs)

        met = [sent[0]] + [ahead(sent[k], k) for k in range(1, lines)]
        size = lines * height + lines * channels
        partial, moved = call(
            lambda *refs: weights_kernel(channels, scale, *refs),
            (
                shape((size, LANES), bf16),
                shape((plane, 3 * lines * channels, LANES), bf16),
            ),
            line,
            short,
            gathered,
            *met,
            in_specs=[scalar] + [held] * (2 + lines),
        )
        partials = [partial] + [ahead(partial, k) for k in range(1, lines)]
        payload = call(
            sum_kernel,
            shape((plane, size + 3 * lines * channels, LANES), bf16),
            moved,
            *partials,
        )
        back = lax.all_to_all(payload, "fft", split_axis=0, concat_axis=0, tiled=True)
        grad_features, grad_w_in, grad_w_out, short = call(
            lambda *refs: finish_kernel(channels, lines, *refs),
            (
                shape(features.shape, bf16),
                shape((3 * width, width)),
                shape((width, width)),
                shape((3, 3 * width)),
            ),
            line,
            back,
            w_in,
            sink_order,
            in_specs=[scalar] + [held] * 3,
            scratch_shapes=[pltpu.VMEM((3 * width, LANES), f32)],
        )
        return (grad_features, grad_w_in, grad_w_out, short.T, grad_one, grad_two)
    sent = sent[0]
    sent = sent.reshape(4, blocks, channels, LANES)
    grad_in = jnp.einsum(
        "sbcp,bwp->scw", sent[:3], gathered[:, :width], preferred_element_type=f32
    )
    grad_out = jnp.einsum(
        "bcp,bwp->cw", sent[3], gathered[:, width:], preferred_element_type=f32
    )
    own = jnp.concatenate([grad_in, grad_out[None]]) * scale
    own = own.reshape(height, LANES)
    short = short.reshape(8 // channels, channels, LANES).sum(axis=0)
    own = jnp.concatenate([own, short]).astype(bf16)
    moved = sent[:3].transpose(1, 0, 2, 3).reshape(blocks, 3 * channels, LANES)
    own = jnp.broadcast_to(own[None], (blocks,) + own.shape)
    packed = jnp.concatenate([moved, own], axis=1)
    back = lax.all_to_all(packed, AXES, split_axis=0, concat_axis=0, tiled=True)
    moved = back[:, : 3 * channels].reshape(blocks, 3, channels, LANES)
    moved = moved.transpose(1, 0, 2, 3).reshape(3 * width, LANES)
    weights = back[:, 3 * channels : 3 * channels + height].astype(f32)
    weights = weights.reshape(blocks, 4, channels, width).transpose(1, 0, 2, 3)
    weights = weights.reshape(4 * width, width)
    short = back[:, 3 * channels + height :, :9].astype(f32).reshape(width, 3, 3)
    short = short.transpose(1, 0, 2).reshape(3 * width, 3)
    grad_features = call(
        features_kernel, shape(features.shape, bf16), moved, w_in, sink_order
    )
    grad_one, grad_two = [
        g.reshape(blocks, channels, LANES).transpose(1, 0, 2).reshape(channels, length)
        for g in (grad_one, grad_two)
    ]
    return (
        grad_features,
        weights[: 3 * width],
        weights[3 * width :].T,
        short,
        grad_one,
        grad_two,
    )


def solution(mesh):
    columns, blocks_first, copied = P(None, AXES), P(AXES, None), P()
    return jax.shard_map(
        local,
        mesh=mesh,
        in_specs=(
            columns,
            blocks_first,
            columns,
            copied,
            copied,
            copied,
            blocks_first,
            blocks_first,
        ),
        out_specs=(columns, copied, copied, copied, blocks_first, blocks_first),
        check_vma=False,
    )
```

```python
import math

import jax
import jax.numpy as jnp
import numpy as np
from jax import lax
from jax.experimental import pallas as pl
from jax.experimental.pallas import tpu as pltpu
from jax.sharding import PartitionSpec as P

AXES = ("seq", "fft")
LANES = 128
bf16 = jnp.bfloat16
f32 = jnp.float32
PARAMS = pltpu.CompilerParams(vmem_limit_bytes=24 * 1024 * 1024)


def halves(table):
    high = table.astype(np.float32).astype(jnp.bfloat16)
    low = (table - high.astype(np.float64)).astype(np.float32).astype(jnp.bfloat16)
    return high, low


def make_tables(count, channels):
    length = count * LANES
    outer = np.arange(count, dtype=np.float64)
    inner = np.arange(LANES, dtype=np.float64)
    angle = 2.0 * np.pi * (outer[:, None] + 0.25) * outer[None, :] / count
    first = np.concatenate([np.cos(angle), -np.sin(angle)], axis=0)
    first = np.kron(first, np.eye(channels))
    turn = 2.0 * np.pi * (inner[:, None] * inner[None, :] % LANES) / LANES
    cos, sin = np.cos(turn), np.sin(turn)
    second = np.block([[cos, -sin], [sin, cos]])
    twist = 2.0 * np.pi * (outer[:, None] + 0.25) * inner[None, :] / length
    twist = np.repeat(twist, channels, axis=0)
    back = first.T / length
    rows = count * channels
    back = np.concatenate([back[:, :rows], back[:, rows:]], axis=0)
    packed = [half for t in (first, back, second, second.T) for half in halves(t)]
    twist = np.concatenate([np.cos(twist), -np.sin(twist)], axis=1).astype(np.float32)
    return np.concatenate(packed, axis=0), twist


def tables_of(table, twist):
    rows = twist.shape[0]
    at, found = 0, []
    for size in (2 * rows, 2 * rows, 2 * LANES, 2 * LANES):
        pair = []
        for half in range(2):
            pair.append(table[at : at + size])
            at += size
        found.append(tuple(pair))
    found[1] = tuple(jnp.concatenate([t[:rows], t[rows:]], axis=1) for t in found[1])
    return (*found, (twist[:, :LANES], twist[:, LANES:]))


def split(value):
    high = value.astype(bf16)
    low = (value - high.astype(f32)).astype(bf16)
    return high, low


def dot(left, right):
    return jnp.dot(left, right, preferred_element_type=f32)


def dot_pairs(left, right):
    return dot(left[0], right[0]) + dot(left[0], right[1]) + dot(left[1], right[0])


def forward(signals, first, second, twist):
    rows = signals[0].shape[0]
    stage = dot_pairs(first, split(jnp.concatenate(signals, axis=1)))
    parts = []
    for i in range(len(signals)):
        re = stage[:rows, i * LANES : (i + 1) * LANES]
        im = stage[rows:, i * LANES : (i + 1) * LANES]
        parts.append(
            jnp.concatenate(
                [re * twist[0] - im * twist[1], re * twist[1] + im * twist[0]], axis=1
            )
        )
    spec = dot_pairs(split(jnp.concatenate(parts, axis=0)), second)
    return [
        (spec[i * rows : (i + 1) * rows, :LANES], spec[i * rows : (i + 1) * rows, LANES:])
        for i in range(len(signals))
    ]


def backward(spectra, first_back, second_back, twist):
    rows = spectra[0][0].shape[0]
    stacked = jnp.concatenate([jnp.concatenate(pair, axis=1) for pair in spectra], axis=0)
    stage = dot_pairs(split(stacked), second_back)
    parts = []
    for i in range(len(spectra)):
        re = stage[i * rows : (i + 1) * rows, :LANES]
        im = stage[i * rows : (i + 1) * rows, LANES:]
        parts.append(
            jnp.concatenate(
                [re * twist[0] + im * twist[1], im * twist[0] - re * twist[1]], axis=0
            )
        )
    out = dot_pairs(first_back, split(jnp.concatenate(parts, axis=1)))
    return [out[:, i * LANES : (i + 1) * LANES] for i in range(len(spectra))]


def times(a, b):
    return (a[0] * b[0] - a[1] * b[1], a[0] * b[1] + a[1] * b[0])


def conj_times(a, b):
    return (a[0] * b[0] + a[1] * b[1], a[0] * b[1] - a[1] * b[0])


def one_hot(order):
    size = order.shape[1]
    place = lax.broadcasted_iota(jnp.int32, (size, size), 0)
    return (place == order).astype(f32).astype(bf16)


def project_kernel(
    features_at,
    order_at,
    cotangent_at,
    w_in_at,
    w_out_at,
    streams_out,
    gather_out,
    features,
    order,
    cotangent,
    w_in,
    w_out,
    done,
):
    copies = [
        pltpu.make_async_copy(source, target, done.at[i])
        for i, (source, target) in enumerate(
            [
                (order_at, order),
                (features_at, features),
                (w_in_at, w_in),
                (cotangent_at, cotangent),
                (w_out_at, w_out),
            ]
        )
    ]
    for copy in copies:
        copy.start()
    width, row_count = features.shape
    copies[0].wait()
    copies[1].wait()
    seq_input = dot(features[...], one_hot(order[...])).astype(bf16)
    copies[2].wait()
    projected = dot(w_in[...], seq_input)
    copies[3].wait()
    copies[4].wait()
    out_grad = lax.dot_general(
        w_out[...], cotangent[...], (((0,), (0,)), ((), ())), preferred_element_type=f32
    )
    if len(streams_out.shape) == 3:
        blocks = streams_out.shape[0]
        parts = [projected[s * width : (s + 1) * width] for s in range(3)] + [out_grad]
        parts = [part.reshape(blocks, width // blocks, row_count) for part in parts]
        streams_out[...] = jnp.concatenate(parts, axis=1).astype(bf16)
    else:
        streams_out[: 3 * width] = projected.astype(bf16)
        streams_out[3 * width :] = out_grad.astype(bf16)
    own = jnp.concatenate([seq_input, cotangent[...]], axis=0)
    gather_out[...] = own


def read_signal(ref, rows):
    if ref.shape[1] == LANES:
        return ref[...]
    return jnp.concatenate(
        [ref[:, i * LANES : (i + 1) * LANES] for i in range(ref.shape[1] // LANES)], axis=0
    )


def write_signal(ref, value):
    if ref.shape[1] == LANES:
        ref[...] = value
        return
    channels = ref.shape[0]
    for i in range(ref.shape[1] // LANES):
        ref[:, i * LANES : (i + 1) * LANES] = value[i * channels : (i + 1) * channels]


def filter_kernel(
    filter_one, filter_two, table, twist, spec_one, spec_two, table_out, twist_out
):
    rows = spec_one.shape[0]
    signals = [read_signal(filter_one, rows), read_signal(filter_two, rows)]
    first, _, second, _, turns = tables_of(table, twist)
    one, two = forward(signals, first, second, turns)
    spec_one[...] = jnp.concatenate(one, axis=1)
    spec_two[...] = jnp.concatenate(two, axis=1)
    table_out[...] = table[...]
    twist_out[...] = twist[...]


def shifted(value, steps, channels):
    if steps == 0:
        return value
    rows, lanes = value.shape
    lane = lax.broadcasted_iota(jnp.int32, value.shape, 1)
    row = lax.broadcasted_iota(jnp.int32, value.shape, 0)
    turned = pltpu.roll(value, steps % lanes, 1)
    if steps > 0:
        carried = jnp.where(row < channels, 0.0, pltpu.roll(turned, channels, 0))
        return jnp.where(lane < steps, carried, turned)
    carried = jnp.where(row >= rows - channels, 0.0, pltpu.roll(turned, rows - channels, 0))
    return jnp.where(lane >= lanes + steps, carried, turned)


def mix_kernel(
    channels,
    scale,
    streams,
    taps,
    spec_one,
    spec_two,
    table,
    twist,
    line,
    short_out,
    product_one,
    product_two,
    *sent_out,
):
    rows = twist.shape[0]
    eight = taps.shape[0]
    first, first_back, second, second_back, twist = tables_of(table, twist)
    if streams.shape[0] == 4 and streams.shape[1] == rows:
        pieces = [streams[s].astype(f32) for s in range(4)]
    else:
        whole = streams[...].astype(f32)
        pieces = [
            whole[:, s * channels : (s + 1) * channels].reshape(rows, LANES) for s in range(4)
        ]
    out_grad = pieces[3]

    def tap(s, k):
        column = jnp.broadcast_to(taps[:, 3 * s + k : 3 * s + k + 1], (eight, LANES))
        column = jnp.broadcast_to(column[None], (rows // eight, eight, LANES))
        return column.reshape(rows, LANES)

    late = [[shifted(pieces[s], k, channels) for k in range(3)] for s in range(3)]
    value, gate_one, gate_two = [
        sum(tap(s, k) * late[s][k] for k in range(3)) for s in range(3)
    ]
    h_one = (spec_one[:, :LANES], spec_one[:, LANES:])
    h_two = (spec_two[:, :LANES], spec_two[:, LANES:])
    value_spec, second_spec = forward([value, out_grad * gate_two], first, second, twist)
    first_mix, grad_first_out = backward(
        [times(h_one, value_spec), conj_times(h_two, second_spec)],
        first_back,
        second_back,
        twist,
    )
    first_spec, grad_first_spec = forward(
        [gate_one * first_mix, gate_one * grad_first_out], first, second, twist
    )
    second_mix, grad_value = backward(
        [times(h_two, first_spec), conj_times(h_one, grad_first_spec)],
        first_back,
        second_back,
        twist,
    )
    product_one[...] = jnp.concatenate(conj_times(value_spec, grad_first_spec), axis=1)
    product_two[...] = jnp.concatenate(conj_times(first_spec, second_spec), axis=1)
    grads = [grad_value, grad_first_out * first_mix, out_grad * second_mix]
    sent = []
    lane = lax.broadcasted_iota(jnp.int32, (eight, LANES), 1)
    short = jnp.zeros((eight, LANES), f32)
    for s in range(3):
        sent.append(sum(tap(s, k) * shifted(grads[s], -k, channels) for k in range(3)))
        for k in range(3):
            folded = (grads[s] * late[s][k]).reshape(rows // eight, eight, LANES).sum(axis=0)
            total = jnp.sum(folded, axis=1, keepdims=True) * scale
            short = jnp.where(lane == 3 * s + k, total, short)
    sent.append(gate_two * second_mix)
    short_out[...] = short
    if len(sent_out) == 1:
        for s in range(4):
            sent_out[0][s] = sent[s].astype(bf16)
        return
    parts = [part.reshape(rows // channels, channels, LANES) for part in sent]
    packed = jnp.concatenate(parts, axis=1).astype(bf16)
    *sent_out, store = sent_out
    lines, plane = store.shape[:2]
    for i in range(lines):
        store[i] = packed[i * plane : (i + 1) * plane]
    for step in range(lines):
        sent_out[step][...] = store[lax.rem(line[0] + step, lines)]


def filter_grads_kernel(scale, product_one, product_two, table, twist, grad_one, grad_two):
    _, first_back, _, second_back, twist = tables_of(table, twist)
    spectra = [(ref[:, :LANES], ref[:, LANES:]) for ref in (product_one, product_two)]
    one, two = backward(spectra, first_back, second_back, twist)
    write_signal(grad_one, one * scale)
    write_signal(grad_two, two * scale)


def member(at, k):
    return jnp.bitwise_xor(at, k)


def weights_kernel(channels, scale, lines, *refs):
    at, short, *refs, partial_out, moved_out = refs
    met, pieces = refs[:lines], refs[lines:]
    plane, width = len(pieces), pieces[0].shape[0] // 2
    height = 4 * channels
    total = jnp.zeros((lines * height, 2 * width), f32)
    step = 2 if plane % 2 == 0 else 1
    for i in range(0, plane, step):
        left = jnp.concatenate(
            [
                jnp.concatenate([m[member(at[1], i + j)] for m in met], axis=0)
                for j in range(step)
            ],
            axis=1,
        )
        right = jnp.concatenate([pieces[i + j][...] for j in range(step)], axis=1)
        total = total + lax.dot_general(
            left, right, (((1,), (1,)), ((), ())), preferred_element_type=f32
        )
    total = total * scale
    size = height * (width // LANES)
    for k in range(lines):
        parts = []
        for h in range(width // LANES):
            low, high = h * LANES, (h + 1) * LANES
            base = k * height
            parts.append(total[base : base + 3 * channels, low:high])
            parts.append(total[base + 3 * channels : base + height, width + low : width + high])
        owner = lax.rem(at[0] + lines - k, lines)
        spot = pl.ds(pl.multiple_of(owner * size, size), size)
        partial_out[spot] = jnp.concatenate(parts, axis=0).astype(bf16)
    tail = jnp.concatenate([short[...]] * lines, axis=0)
    owner = lax.broadcasted_iota(jnp.int32, tail.shape, 0) // channels
    partial_out[lines * size :] = jnp.where(owner == at[0], tail, 0.0).astype(bf16)
    parts = [m[...].astype(f32)[:, : 3 * channels] for m in met]
    moved_out[...] = jnp.concatenate(parts, axis=1).astype(bf16)


def sum_kernel(*refs):
    *partials, out = refs
    out[...] = sum(part[...].astype(f32) for part in partials).astype(bf16)


def unorder(grad_projected, w_in, order):
    grad_seq = lax.dot_general(
        w_in, grad_projected, (((0,), (0,)), ((), ())), preferred_element_type=f32
    ).astype(bf16)
    return lax.dot_general(
        grad_seq, one_hot(order), (((1,), (1,)), ((), ())), preferred_element_type=f32
    ).astype(bf16)


def moved_kernel(channels, lines, at, back, w_in, order, features_out, store):
    plane, width = back.shape[0], w_in.shape[1]
    share = plane * channels
    whole = back[...].astype(f32)
    for k in range(lines):
        owner = lax.rem(at[0] + lines - k, lines)
        for s in range(3):
            start = (3 * k + s) * channels
            spot = pl.ds(pl.multiple_of(s * width + owner * share, share), share)
            store[spot] = whole[:, start : start + channels].reshape(share, LANES)
    features_out[...] = unorder(store[...].astype(bf16), w_in[...], order[...])


def finish_kernel(channels, lines, at, *refs):
    *pieces, w_in_out, w_out_out, short_out, out_rows, short_rows = refs
    width = w_out_out.shape[0]
    share = width // lines
    height = 4 * channels
    size = height * (width // LANES)
    for k, piece in enumerate(pieces):
        rows = piece[...].astype(f32)
        for i in range(lines):
            first = pl.multiple_of(i * share + member(at[1], k) * channels, channels)
            for h in range(width // LANES):
                low, high = h * LANES, (h + 1) * LANES
                base = i * size + h * height
                for s in range(3):
                    spot = pl.ds(pl.multiple_of(s * width + first, channels), channels)
                    start = base + s * channels
                    w_in_out[spot, low:high] = rows[start : start + channels]
                start = base + 3 * channels
                out_rows[pl.ds(first, channels), low:high] = rows[start : start + channels]
            start = lines * size + i * channels
            short_rows[pl.ds(first, channels), :] = rows[start : start + channels]
    w_out_out[...] = out_rows[...].T
    short = short_rows[...].T
    for s in range(3):
        short_out[:, s * width : (s + 1) * width] = short[3 * s : 3 * s + 3, :]


def features_kernel(moved, w_in, order, features_out):
    features_out[...] = unorder(moved[...], w_in[...], order[...])


def swapped(value, plane, distance):
    return lax.ppermute(value, "fft", [(i, i ^ distance) for i in range(plane)])


def spread(value, plane):
    pieces = [value if k == 0 else swapped(value, plane, k) for k in range(0, plane, 2)]
    return [piece for own in pieces for piece in (own, swapped(own, plane, 1))]


def shape(dims, dtype=f32):
    return jax.ShapeDtypeStruct(dims, dtype)


def local(features, sink_order, cotangent, w_in, short_taps, w_out, filter_one, filter_two):
    width, row_count = features.shape
    lines, plane = lax.axis_size("seq"), lax.axis_size("fft")
    blocks = lines * plane
    channels, length = filter_one.shape
    rows = channels * blocks
    scale = 1.0 / math.sqrt(length)
    whole = channels % 8 == 0 and plane % 2 == 0 and plane & (plane - 1) == 0
    table, twist = make_tables(blocks, channels)
    eight = channels if whole else 8
    mine = lax.axis_index(AXES)

    def call(kernel, outs, *args, **options):
        return pl.pallas_call(kernel, out_shape=outs, compiler_params=PARAMS, **options)(*args)

    dims = (blocks, 4 * channels, LANES) if whole else (4 * width, LANES)
    streams, own = pl.pallas_call(
        project_kernel,
        out_shape=(shape(dims, bf16), shape((2 * width, row_count), bf16)),
        in_specs=[pl.BlockSpec(memory_space=pl.ANY)] * 5,
        scratch_shapes=[
            pltpu.VMEM(a.shape, a.dtype)
            for a in (features, sink_order, cotangent, w_in, w_out)
        ]
        + [pltpu.SemaphoreType.DMA((5,))],
        compiler_params=pltpu.CompilerParams(vmem_limit_bytes=60 * 1024 * 1024),
    )(features, sink_order, cotangent, w_in, w_out)
    if not whole:
        streams = streams.reshape(4, blocks, channels, LANES).transpose(1, 0, 2, 3)
        streams = streams.reshape(blocks, 4 * channels, LANES)
    if whole:
        pieces = spread(own, plane)
    else:
        gathered = lax.all_gather(own, AXES, axis=0, tiled=False)
    arrived = lax.all_to_all(streams, AXES, split_axis=0, concat_axis=0, tiled=True)
    taps = lax.dynamic_slice_in_dim(short_taps.reshape(3, width, 3), mine * channels, channels, 1)
    taps = taps.transpose(1, 0, 2).reshape(channels, 9)
    if not whole:
        taps = jnp.tile(taps, (8 // channels, 1))
        arrived = arrived.reshape(blocks, 4, channels, LANES).transpose(1, 0, 2, 3)
        arrived = arrived.reshape(4, rows, LANES)
        filter_one, filter_two = [
            h.reshape(channels, blocks, LANES).transpose(1, 0, 2).reshape(rows, LANES)
            for h in (filter_one, filter_two)
        ]
    spec = shape((rows, 2 * LANES))
    spec_one, spec_two, table, twist = call(
        filter_kernel,
        (spec, spec, shape(table.shape, bf16), shape(twist.shape)),
        filter_one,
        filter_two,
        table,
        twist,
    )
    at = jnp.stack([lax.axis_index("seq"), lax.axis_index("fft")]).astype(jnp.int32)
    scalar = pl.BlockSpec(memory_space=pltpu.SMEM)
    held = pl.BlockSpec(memory_space=pltpu.VMEM)
    chunk = (plane, 4 * channels, LANES)
    dims = [shape(chunk, bf16)] * lines if whole else [shape((4, rows, LANES), bf16)]
    short, product_one, product_two, *sent = call(
        lambda *refs: mix_kernel(channels, scale, *refs),
        (shape((eight, LANES)), spec, spec, *dims),
        arrived,
        taps,
        spec_one,
        spec_two,
        table,
        twist,
        at,
        in_specs=[held] * 6 + [scalar],
        scratch_shapes=[pltpu.VMEM((lines, *chunk), bf16)] if whole else [],
    )
    grad_one, grad_two = call(
        lambda *refs: filter_grads_kernel(scale, *refs),
        (shape(filter_one.shape), shape(filter_two.shape)),
        product_one,
        product_two,
        table,
        twist,
    )
    height = channels * 4 * (width // LANES)
    if whole:
        def ahead(value, steps):
            pairs = [(i, (i + steps) % lines) for i in range(lines)]
            return lax.ppermute(value, "seq", pairs)

        met = [sent[0]] + [ahead(sent[k], k) for k in range(1, lines)]
        size = lines * height + lines * channels
        partial, moved = call(
            lambda *refs: weights_kernel(channels, scale, lines, *refs),
            (
                shape((size, LANES), bf16),
                shape((plane, 3 * lines * channels, LANES), bf16),
            ),
            at,
            short,
            *met,
            *pieces,
            in_specs=[scalar] + [held] * (1 + lines + plane),
        )
        partials = [partial] + [ahead(partial, k) for k in range(1, lines)]
        back = lax.all_to_all(moved, "fft", split_axis=0, concat_axis=0, tiled=True)
        grad_features = call(
            lambda *refs: moved_kernel(channels, lines, *refs),
            shape(features.shape, bf16),
            at,
            back,
            w_in,
            sink_order,
            in_specs=[scalar] + [held] * 3,
            scratch_shapes=[pltpu.VMEM((3 * width, LANES), f32)],
        )
        rows_sum = call(sum_kernel, shape((size, LANES), bf16), *partials)
        grad_w_in, grad_w_out, short = call(
            lambda *refs: finish_kernel(channels, lines, *refs),
            (shape((3 * width, width)), shape((width, width)), shape((3, 3 * width))),
            at,
            *spread(rows_sum, plane),
            in_specs=[scalar] + [held] * plane,
            scratch_shapes=[pltpu.VMEM((width, width), f32), pltpu.VMEM((width, LANES), f32)],
        )
        return (grad_features, grad_w_in, grad_w_out, short.T, grad_one, grad_two)
    sent = sent[0]
    sent = sent.reshape(4, blocks, channels, LANES)
    grad_in = jnp.einsum(
        "sbcp,bwp->scw", sent[:3], gathered[:, :width], preferred_element_type=f32
    )
    grad_out = jnp.einsum(
        "bcp,bwp->cw", sent[3], gathered[:, width:], preferred_element_type=f32
    )
    own = jnp.concatenate([grad_in, grad_out[None]]) * scale
    own = own.reshape(height, LANES)
    short = short.reshape(8 // channels, channels, LANES).sum(axis=0)
    own = jnp.concatenate([own, short]).astype(bf16)
    moved = sent[:3].transpose(1, 0, 2, 3).reshape(blocks, 3 * channels, LANES)
    own = jnp.broadcast_to(own[None], (blocks,) + own.shape)
    packed = jnp.concatenate([moved, own], axis=1)
    back = lax.all_to_all(packed, AXES, split_axis=0, concat_axis=0, tiled=True)
    moved = back[:, : 3 * channels].reshape(blocks, 3, channels, LANES)
    moved = moved.transpose(1, 0, 2, 3).reshape(3 * width, LANES)
    weights = back[:, 3 * channels : 3 * channels + height].astype(f32)
    weights = weights.reshape(blocks, 4, channels, width).transpose(1, 0, 2, 3)
    weights = weights.reshape(4 * width, width)
    short = back[:, 3 * channels + height :, :9].astype(f32).reshape(width, 3, 3)
    short = short.transpose(1, 0, 2).reshape(3 * width, 3)
    grad_features = call(
        features_kernel, shape(features.shape, bf16), moved, w_in, sink_order
    )
    grad_one, grad_two = [
        g.reshape(blocks, channels, LANES).transpose(1, 0, 2).reshape(channels, length)
        for g in (grad_one, grad_two)
    ]
    return (
        grad_features,
        weights[: 3 * width],
        weights[3 * width :].T,
        short,
        grad_one,
        grad_two,
    )


def solution(mesh):
    columns, blocks_first, copied = P(None, AXES), P(AXES, None), P()
    return jax.shard_map(
        local,
        mesh=mesh,
        in_specs=(
            columns,
            blocks_first,
            columns,
            copied,
            copied,
            copied,
            blocks_first,
            blocks_first,
        ),
        out_specs=(columns, copied, copied, copied, blocks_first, blocks_first),
        check_vma=False,
    )
```

```python
import math

import jax
import jax.numpy as jnp
import numpy as np
from jax import lax
from jax.experimental import pallas as pl
from jax.experimental.pallas import tpu as pltpu
from jax.sharding import PartitionSpec as P

AXES = ("seq", "fft")
LANES = 128
bf16 = jnp.bfloat16
f32 = jnp.float32
PARAMS = pltpu.CompilerParams(vmem_limit_bytes=24 * 1024 * 1024)


def halves(table):
    high = table.astype(np.float32).astype(jnp.bfloat16)
    low = (table - high.astype(np.float64)).astype(np.float32).astype(jnp.bfloat16)
    return high, low


def make_tables(count, channels):
    length = count * LANES
    outer = np.arange(count, dtype=np.float64) + 0.25
    inner = np.arange(LANES, dtype=np.float64)
    angle = 2.0 * np.pi * outer[:, None] * outer[None, :] / count
    first = np.kron(np.concatenate([np.cos(angle), np.sin(angle)], axis=0), np.eye(channels))
    turn = 2.0 * np.pi * (inner[:, None] * inner[None, :] % LANES) / LANES
    cos, sin = np.cos(turn), np.sin(turn)
    second = np.block([[cos, -sin], [sin, cos]])
    packed = [half for t in (first, second) for half in halves(t)]
    twist = 2.0 * np.pi * outer[:, None] * (inner[None, :] - LANES / 4) / length
    twist = np.repeat(twist, channels, axis=0)
    twist = np.concatenate([np.cos(twist), -np.sin(twist)], axis=1).astype(np.float32)
    return np.concatenate(packed, axis=0), twist


def tables_of(table, twist):
    rows = twist.shape[0]
    at, found = 0, []
    for size in (2 * rows, 2 * LANES):
        pair = []
        for half in range(2):
            pair.append(table[at : at + size])
            at += size
        found.append(tuple(pair))
    first, second = found
    back = tuple(jnp.concatenate([t[:rows], t[rows:]], axis=1) for t in first)
    return first, back, second, (twist[:, :LANES], twist[:, LANES:])


def split(value):
    high = value.astype(bf16)
    low = (value - high.astype(f32)).astype(bf16)
    return high, low


def dot(left, right):
    return jnp.dot(left, right, preferred_element_type=f32)


def dot_pairs(left, right):
    return dot(left[0], right[0]) + dot(left[0], right[1]) + dot(left[1], right[0])


def forward(signals, first, second, twist):
    rows = signals[0].shape[0]
    stage = dot_pairs(first, split(jnp.concatenate(signals, axis=1)))
    parts = []
    for i in range(len(signals)):
        cos = stage[:rows, i * LANES : (i + 1) * LANES]
        sin = stage[rows:, i * LANES : (i + 1) * LANES]
        parts.append(
            jnp.concatenate(
                [cos * twist[0] + sin * twist[1], cos * twist[1] - sin * twist[0]], axis=1
            )
        )
    spec = dot_pairs(split(jnp.concatenate(parts, axis=0)), second)
    return [
        (spec[i * rows : (i + 1) * rows, :LANES], spec[i * rows : (i + 1) * rows, LANES:])
        for i in range(len(signals))
    ]


def backward(spectra, back, second, twist):
    rows = spectra[0][0].shape[0]
    stacked = jnp.concatenate([jnp.concatenate(pair, axis=1) for pair in spectra], axis=0)
    stage = dot_pairs(split(stacked), second)
    parts = []
    for i in range(len(spectra)):
        re = stage[i * rows : (i + 1) * rows, :LANES]
        im = stage[i * rows : (i + 1) * rows, LANES:]
        parts.append(
            jnp.concatenate(
                [re * twist[0] - im * twist[1], re * twist[1] + im * twist[0]], axis=0
            )
        )
    out = dot_pairs(back, split(jnp.concatenate(parts, axis=1)))
    return [out[:, i * LANES : (i + 1) * LANES] for i in range(len(spectra))]


def times(a, b):
    return (a[0] * b[0] - a[1] * b[1], -(a[0] * b[1] + a[1] * b[0]))


def conj_times(a, b):
    return (a[0] * b[0] + a[1] * b[1], a[1] * b[0] - a[0] * b[1])


def one_hot(order):
    size = order.shape[1]
    place = lax.broadcasted_iota(jnp.int32, (size, size), 0)
    return (place == order).astype(f32).astype(bf16)


def project_kernel(
    features_at,
    order_at,
    cotangent_at,
    w_in_at,
    w_out_at,
    streams_out,
    gather_out,
    features,
    order,
    cotangent,
    w_in,
    w_out,
    done,
):
    copies = [
        pltpu.make_async_copy(source, target, done.at[i])
        for i, (source, target) in enumerate(
            [
                (order_at, order),
                (features_at, features),
                (w_in_at, w_in),
                (cotangent_at, cotangent),
                (w_out_at, w_out),
            ]
        )
    ]
    for copy in copies:
        copy.start()
    width, row_count = features.shape
    copies[0].wait()
    copies[1].wait()
    seq_input = dot(features[...], one_hot(order[...])).astype(bf16)
    copies[2].wait()
    projected = dot(w_in[...], seq_input)
    copies[3].wait()
    copies[4].wait()
    out_grad = lax.dot_general(
        w_out[...], cotangent[...], (((0,), (0,)), ((), ())), preferred_element_type=f32
    )
    if len(streams_out.shape) == 3:
        blocks = streams_out.shape[0]
        parts = [projected[s * width : (s + 1) * width] for s in range(3)] + [out_grad]
        parts = [part.reshape(blocks, width // blocks, row_count) for part in parts]
        streams_out[...] = jnp.concatenate(parts, axis=1).astype(bf16)
    else:
        streams_out[: 3 * width] = projected.astype(bf16)
        streams_out[3 * width :] = out_grad.astype(bf16)
    own = jnp.concatenate([seq_input, cotangent[...]], axis=0)
    gather_out[...] = own


def read_signal(ref, rows):
    if ref.shape[1] == LANES:
        return ref[...]
    return jnp.concatenate(
        [ref[:, i * LANES : (i + 1) * LANES] for i in range(ref.shape[1] // LANES)], axis=0
    )


def write_signal(ref, value):
    if ref.shape[1] == LANES:
        ref[...] = value
        return
    channels = ref.shape[0]
    for i in range(ref.shape[1] // LANES):
        ref[:, i * LANES : (i + 1) * LANES] = value[i * channels : (i + 1) * channels]


def filter_kernel(
    length,
    filter_one,
    filter_two,
    table,
    twist,
    own,
    order,
    spec_one,
    spec_two,
    table_out,
    twist_out,
    own_out,
    order_out,
):
    rows = spec_one.shape[0]
    signals = [read_signal(filter_one, rows), read_signal(filter_two, rows)]
    first, _, second, turns = tables_of(table, twist)
    one, two = forward(signals, first, second, turns)
    spec_one[...] = jnp.concatenate(one, axis=1) * (1.0 / length)
    spec_two[...] = jnp.concatenate(two, axis=1) * (1.0 / length)
    table_out[...] = table[...]
    twist_out[...] = twist[...]
    own_out[...] = own[...]
    order_out[...] = order[...]


def shifted(value, steps, channels):
    if steps == 0:
        return value
    rows, lanes = value.shape
    lane = lax.broadcasted_iota(jnp.int32, value.shape, 1)
    row = lax.broadcasted_iota(jnp.int32, value.shape, 0)
    turned = pltpu.roll(value, steps % lanes, 1)
    if steps > 0:
        carried = jnp.where(row < channels, 0.0, pltpu.roll(turned, channels, 0))
        return jnp.where(lane < steps, carried, turned)
    carried = jnp.where(row >= rows - channels, 0.0, pltpu.roll(turned, rows - channels, 0))
    return jnp.where(lane >= lanes + steps, carried, turned)


def mix_kernel(
    channels,
    scale,
    streams,
    taps,
    spec_one,
    spec_two,
    table,
    twist,
    line,
    short_out,
    product_one,
    product_two,
    *sent_out,
):
    rows = twist.shape[0]
    eight = taps.shape[0]
    first, back, second, twist = tables_of(table, twist)
    if streams.shape[0] == 4 and streams.shape[1] == rows:
        pieces = [streams[s].astype(f32) for s in range(4)]
    else:
        whole = streams[...].astype(f32)
        pieces = [
            whole[:, s * channels : (s + 1) * channels].reshape(rows, LANES) for s in range(4)
        ]
    out_grad = pieces[3]

    def tap(s, k):
        column = jnp.broadcast_to(taps[:, 3 * s + k : 3 * s + k + 1], (eight, LANES))
        column = jnp.broadcast_to(column[None], (rows // eight, eight, LANES))
        return column.reshape(rows, LANES)

    late = [[shifted(pieces[s], k, channels) for k in range(3)] for s in range(3)]
    value, gate_one, gate_two = [
        sum(tap(s, k) * late[s][k] for k in range(3)) for s in range(3)
    ]
    h_one = (spec_one[:, :LANES], spec_one[:, LANES:])
    h_two = (spec_two[:, :LANES], spec_two[:, LANES:])
    value_spec, second_spec = forward([value, out_grad * gate_two], first, second, twist)
    first_mix, grad_first_out = backward(
        [times(h_one, value_spec), conj_times(h_two, second_spec)],
        back,
        second,
        twist,
    )
    first_spec, grad_first_spec = forward(
        [gate_one * first_mix, gate_one * grad_first_out], first, second, twist
    )
    second_mix, grad_value = backward(
        [times(h_two, first_spec), conj_times(h_one, grad_first_spec)],
        back,
        second,
        twist,
    )
    product_one[...] = jnp.concatenate(conj_times(value_spec, grad_first_spec), axis=1)
    product_two[...] = jnp.concatenate(conj_times(first_spec, second_spec), axis=1)
    grads = [grad_value, grad_first_out * first_mix, out_grad * second_mix]
    sent = []
    lane = lax.broadcasted_iota(jnp.int32, (eight, LANES), 1)
    short = jnp.zeros((eight, LANES), f32)
    for s in range(3):
        sent.append(sum(tap(s, k) * shifted(grads[s], -k, channels) for k in range(3)))
        for k in range(3):
            folded = (grads[s] * late[s][k]).reshape(rows // eight, eight, LANES).sum(axis=0)
            total = jnp.sum(folded, axis=1, keepdims=True) * scale
            short = jnp.where(lane == 3 * s + k, total, short)
    sent.append(gate_two * second_mix)
    short_out[...] = short
    if len(sent_out) == 1:
        for s in range(4):
            sent_out[0][s] = sent[s].astype(bf16)
        return
    parts = [part.reshape(rows // channels, channels, LANES) for part in sent]
    packed = jnp.concatenate(parts, axis=1).astype(bf16)
    *sent_out, store = sent_out
    lines, plane = store.shape[:2]
    for i in range(lines):
        store[i] = packed[i * plane : (i + 1) * plane]
    for step in range(lines):
        sent_out[step][...] = store[lax.rem(line[0] + step, lines)]


def filter_grads_kernel(
    scale, product_one, product_two, table, twist, short, grad_one, grad_two, short_out
):
    _, back, second, twist = tables_of(table, twist)
    spectra = [(ref[:, :LANES], ref[:, LANES:]) for ref in (product_one, product_two)]
    one, two = backward(spectra, back, second, twist)
    write_signal(grad_one, one * scale)
    write_signal(grad_two, two * scale)
    short_out[...] = short[...]


def member(at, k):
    return jnp.bitwise_xor(at, k)


def weights_kernel(channels, scale, lines, *refs):
    line, place, short, *refs, partial_out, moved_out = refs
    met, pieces = refs[:lines], refs[lines:]
    plane, width = len(pieces), pieces[0].shape[0] // 2
    height = 4 * channels
    total = jnp.zeros((lines * height, 2 * width), f32)
    step = 2 if plane % 2 == 0 else 1
    for i in range(0, plane, step):
        left = jnp.concatenate(
            [
                jnp.concatenate([m[member(place[0], i + j)] for m in met], axis=0)
                for j in range(step)
            ],
            axis=1,
        )
        right = jnp.concatenate([pieces[i + j][...] for j in range(step)], axis=1)
        total = total + lax.dot_general(
            left, right, (((1,), (1,)), ((), ())), preferred_element_type=f32
        )
    total = total * scale
    size = height * (width // LANES)
    for k in range(lines):
        parts = []
        for h in range(width // LANES):
            low, high = h * LANES, (h + 1) * LANES
            base = k * height
            parts.append(total[base : base + 3 * channels, low:high])
            parts.append(total[base + 3 * channels : base + height, width + low : width + high])
        owner = lax.rem(line[0] + lines - k, lines)
        spot = pl.ds(pl.multiple_of(owner * size, size), size)
        partial_out[spot] = jnp.concatenate(parts, axis=0).astype(bf16)
    tail = jnp.concatenate([short[...]] * lines, axis=0)
    owner = lax.broadcasted_iota(jnp.int32, tail.shape, 0) // channels
    partial_out[lines * size :] = jnp.where(owner == line[0], tail, 0.0).astype(bf16)
    parts = [m[...].astype(f32)[:, : 3 * channels] for m in met]
    moved_out[...] = jnp.concatenate(parts, axis=1).astype(bf16)


def sum_kernel(*refs):
    *partials, out = refs
    out[...] = sum(part[...].astype(f32) for part in partials).astype(bf16)


def unorder(grad_projected, w_in, order):
    grad_seq = lax.dot_general(
        w_in, grad_projected, (((0,), (0,)), ((), ())), preferred_element_type=f32
    ).astype(bf16)
    return lax.dot_general(
        grad_seq, one_hot(order), (((1,), (1,)), ((), ())), preferred_element_type=f32
    ).astype(bf16)


def moved_kernel(channels, lines, line, back, w_in, order, features_out, store):
    plane, width = back.shape[0], w_in.shape[1]
    share = plane * channels
    whole = back[...].astype(f32)
    for k in range(lines):
        owner = lax.rem(line[0] + lines - k, lines)
        for s in range(3):
            start = (3 * k + s) * channels
            spot = pl.ds(pl.multiple_of(s * width + owner * share, share), share)
            store[spot] = whole[:, start : start + channels].reshape(share, LANES)
    features_out[...] = unorder(store[...].astype(bf16), w_in[...], order[...])


def finish_kernel(channels, lines, place, *refs):
    *pieces, w_in_out, w_out_out, short_out, out_rows, short_rows = refs
    width = w_out_out.shape[0]
    share = width // lines
    height = 4 * channels
    size = height * (width // LANES)
    for k, piece in enumerate(pieces):
        rows = piece[...].astype(f32)
        for i in range(lines):
            first = pl.multiple_of(i * share + member(place[0], k) * channels, channels)
            for h in range(width // LANES):
                low, high = h * LANES, (h + 1) * LANES
                base = i * size + h * height
                for s in range(3):
                    spot = pl.ds(pl.multiple_of(s * width + first, channels), channels)
                    start = base + s * channels
                    w_in_out[spot, low:high] = rows[start : start + channels]
                start = base + 3 * channels
                out_rows[pl.ds(first, channels), low:high] = rows[start : start + channels]
            start = lines * size + i * channels
            short_rows[pl.ds(first, channels), :] = rows[start : start + channels]
    w_out_out[...] = out_rows[...].T
    short = short_rows[...].T
    for s in range(3):
        short_out[:, s * width : (s + 1) * width] = short[3 * s : 3 * s + 3, :]


def features_kernel(moved, w_in, order, features_out):
    features_out[...] = unorder(moved[...], w_in[...], order[...])


def swapped(value, plane, distance):
    return lax.ppermute(value, "fft", [(i, i ^ distance) for i in range(plane)])


def spread(value, plane):
    pieces = [value if k == 0 else swapped(value, plane, k) for k in range(0, plane, 2)]
    return [piece for own in pieces for piece in (own, swapped(own, plane, 1))]


def shape(dims, dtype=f32):
    return jax.ShapeDtypeStruct(dims, dtype)


def local(features, sink_order, cotangent, w_in, short_taps, w_out, filter_one, filter_two):
    width, row_count = features.shape
    lines, plane = lax.axis_size("seq"), lax.axis_size("fft")
    blocks = lines * plane
    channels, length = filter_one.shape
    rows = channels * blocks
    scale = 1.0 / math.sqrt(length)
    whole = channels % 8 == 0 and plane % 2 == 0 and plane & (plane - 1) == 0
    table, twist = make_tables(blocks, channels)
    eight = channels if whole else 8
    mine = lax.axis_index(AXES)

    def call(kernel, outs, *args, **options):
        return pl.pallas_call(kernel, out_shape=outs, compiler_params=PARAMS, **options)(*args)

    dims = (blocks, 4 * channels, LANES) if whole else (4 * width, LANES)
    streams, own = pl.pallas_call(
        project_kernel,
        out_shape=(shape(dims, bf16), shape((2 * width, row_count), bf16)),
        in_specs=[pl.BlockSpec(memory_space=pl.ANY)] * 5,
        scratch_shapes=[
            pltpu.VMEM(a.shape, a.dtype)
            for a in (features, sink_order, cotangent, w_in, w_out)
        ]
        + [pltpu.SemaphoreType.DMA((5,))],
        compiler_params=pltpu.CompilerParams(vmem_limit_bytes=60 * 1024 * 1024),
    )(features, sink_order, cotangent, w_in, w_out)
    if not whole:
        streams = streams.reshape(4, blocks, channels, LANES).transpose(1, 0, 2, 3)
        streams = streams.reshape(blocks, 4 * channels, LANES)
    arrived = lax.all_to_all(streams, AXES, split_axis=0, concat_axis=0, tiled=True)
    taps = lax.dynamic_slice_in_dim(short_taps.reshape(3, width, 3), mine * channels, channels, 1)
    taps = taps.transpose(1, 0, 2).reshape(channels, 9)
    if not whole:
        taps = jnp.tile(taps, (8 // channels, 1))
        arrived = arrived.reshape(blocks, 4, channels, LANES).transpose(1, 0, 2, 3)
        arrived = arrived.reshape(4, rows, LANES)
        filter_one, filter_two = [
            h.reshape(channels, blocks, LANES).transpose(1, 0, 2).reshape(rows, LANES)
            for h in (filter_one, filter_two)
        ]
    spec = shape((rows, 2 * LANES))
    spec_one, spec_two, table, twist, own, order = call(
        lambda *refs: filter_kernel(length, *refs),
        (
            spec,
            spec,
            shape(table.shape, bf16),
            shape(twist.shape),
            shape(own.shape, bf16),
            shape(sink_order.shape, jnp.int32),
        ),
        filter_one,
        filter_two,
        table,
        twist,
        own,
        sink_order,
    )
    line = lax.axis_index("seq").astype(jnp.int32).reshape(1)
    place = lax.axis_index("fft").astype(jnp.int32).reshape(1)
    scalar = pl.BlockSpec(memory_space=pltpu.SMEM)
    held = pl.BlockSpec(memory_space=pltpu.VMEM)
    chunk = (plane, 4 * channels, LANES)
    dims = [shape(chunk, bf16)] * lines if whole else [shape((4, rows, LANES), bf16)]
    short, product_one, product_two, *sent = call(
        lambda *refs: mix_kernel(channels, scale, *refs),
        (shape((eight, LANES)), spec, spec, *dims),
        arrived,
        taps,
        spec_one,
        spec_two,
        table,
        twist,
        line,
        in_specs=[held] * 6 + [scalar],
        scratch_shapes=[pltpu.VMEM((lines, *chunk), bf16)] if whole else [],
    )
    grad_one, grad_two, short = call(
        lambda *refs: filter_grads_kernel(scale / length, *refs),
        (shape(filter_one.shape), shape(filter_two.shape), shape(short.shape)),
        product_one,
        product_two,
        table,
        twist,
        short,
    )
    height = channels * 4 * (width // LANES)
    if whole:
        def ahead(value, steps):
            pairs = [(i, (i + steps) % lines) for i in range(lines)]
            return lax.ppermute(value, "seq", pairs)

        met = [sent[0]] + [ahead(sent[k], k) for k in range(1, lines)]
        size = lines * height + lines * channels
        partial, moved = call(
            lambda *refs: weights_kernel(channels, scale, lines, *refs),
            (
                shape((size, LANES), bf16),
                shape((plane, 3 * lines * channels, LANES), bf16),
            ),
            line,
            place,
            short,
            *met,
            *spread(own, plane),
            in_specs=[scalar] * 2 + [held] * (1 + lines + plane),
        )
        partials = [partial] + [ahead(partial, k) for k in range(1, lines)]
        back = lax.all_to_all(moved, "fft", split_axis=0, concat_axis=0, tiled=True)
        grad_features = call(
            lambda *refs: moved_kernel(channels, lines, *refs),
            shape(features.shape, bf16),
            line,
            back,
            w_in,
            order,
            in_specs=[scalar] + [held] * 3,
            scratch_shapes=[pltpu.VMEM((3 * width, LANES), f32)],
        )
        rows_sum = call(sum_kernel, shape((size, LANES), bf16), *partials)
        grad_w_in, grad_w_out, short = call(
            lambda *refs: finish_kernel(channels, lines, *refs),
            (shape((3 * width, width)), shape((width, width)), shape((3, 3 * width))),
            place,
            *spread(rows_sum, plane),
            in_specs=[scalar] + [held] * plane,
            scratch_shapes=[pltpu.VMEM((width, width), f32), pltpu.VMEM((width, LANES), f32)],
        )
        return (grad_features, grad_w_in, grad_w_out, short.T, grad_one, grad_two)
    gathered = lax.all_gather(own, AXES, axis=0, tiled=False)
    sent = sent[0]
    sent = sent.reshape(4, blocks, channels, LANES)
    grad_in = jnp.einsum(
        "sbcp,bwp->scw", sent[:3], gathered[:, :width], preferred_element_type=f32
    )
    grad_out = jnp.einsum(
        "bcp,bwp->cw", sent[3], gathered[:, width:], preferred_element_type=f32
    )
    own = jnp.concatenate([grad_in, grad_out[None]]) * scale
    own = own.reshape(height, LANES)
    short = short.reshape(8 // channels, channels, LANES).sum(axis=0)
    own = jnp.concatenate([own, short]).astype(bf16)
    moved = sent[:3].transpose(1, 0, 2, 3).reshape(blocks, 3 * channels, LANES)
    own = jnp.broadcast_to(own[None], (blocks,) + own.shape)
    packed = jnp.concatenate([moved, own], axis=1)
    back = lax.all_to_all(packed, AXES, split_axis=0, concat_axis=0, tiled=True)
    moved = back[:, : 3 * channels].reshape(blocks, 3, channels, LANES)
    moved = moved.transpose(1, 0, 2, 3).reshape(3 * width, LANES)
    weights = back[:, 3 * channels : 3 * channels + height].astype(f32)
    weights = weights.reshape(blocks, 4, channels, width).transpose(1, 0, 2, 3)
    weights = weights.reshape(4 * width, width)
    short = back[:, 3 * channels + height :, :9].astype(f32).reshape(width, 3, 3)
    short = short.transpose(1, 0, 2).reshape(3 * width, 3)
    grad_features = call(
        features_kernel, shape(features.shape, bf16), moved, w_in, sink_order
    )
    grad_one, grad_two = [
        g.reshape(blocks, channels, LANES).transpose(1, 0, 2).reshape(channels, length)
        for g in (grad_one, grad_two)
    ]
    return (
        grad_features,
        weights[: 3 * width],
        weights[3 * width :].T,
        short,
        grad_one,
        grad_two,
    )


def solution(mesh):
    columns, blocks_first, copied = P(None, AXES), P(AXES, None), P()
    return jax.shard_map(
        local,
        mesh=mesh,
        in_specs=(
            columns,
            blocks_first,
            columns,
            copied,
            copied,
            copied,
            blocks_first,
            blocks_first,
        ),
        out_specs=(columns, copied, copied, copied, blocks_first, blocks_first),
        check_vma=False,
    )
```

```python
import math

import jax
import jax.numpy as jnp
import numpy as np
from jax import lax
from jax.experimental import pallas as pl
from jax.experimental.pallas import tpu as pltpu
from jax.sharding import PartitionSpec as P

AXES = ("seq", "fft")
LANES = 128
bf16 = jnp.bfloat16
f32 = jnp.float32
PARAMS = pltpu.CompilerParams(vmem_limit_bytes=24 * 1024 * 1024)


def halves(table):
    high = table.astype(np.float32).astype(jnp.bfloat16)
    low = (table - high.astype(np.float64)).astype(np.float32).astype(jnp.bfloat16)
    return high, low


def make_tables(count, channels):
    length = count * LANES
    outer = np.arange(count, dtype=np.float64) + 0.25
    inner = np.arange(LANES, dtype=np.float64)
    angle = 2.0 * np.pi * outer[:, None] * outer[None, :] / count
    first = np.kron(np.concatenate([np.cos(angle), np.sin(angle)], axis=0), np.eye(channels))
    turn = 2.0 * np.pi * (inner[:, None] * inner[None, :] % LANES) / LANES
    cos, sin = np.cos(turn), np.sin(turn)
    second = np.block([[cos, -sin], [sin, cos]])
    packed = [half for t in (first, second) for half in halves(t)]
    twist = 2.0 * np.pi * outer[:, None] * (inner[None, :] - LANES / 4) / length
    twist = np.repeat(twist, channels, axis=0)
    twist = np.concatenate([np.cos(twist), -np.sin(twist)], axis=1).astype(np.float32)
    return np.concatenate(packed, axis=0), twist


def tables_of(table, twist):
    rows = twist.shape[0]
    at, found = 0, []
    for size in (2 * rows, 2 * LANES):
        pair = []
        for half in range(2):
            pair.append(table[at : at + size])
            at += size
        found.append(tuple(pair))
    first, second = found
    back = tuple(jnp.concatenate([t[:rows], t[rows:]], axis=1) for t in first)
    return first, back, second, (twist[:, :LANES], twist[:, LANES:])


def split(value):
    high = value.astype(bf16)
    low = (value - high.astype(f32)).astype(bf16)
    return high, low


def dot(left, right):
    return jnp.dot(left, right, preferred_element_type=f32)


def dot_pairs(left, right):
    return dot(left[0], right[0]) + dot(left[0], right[1]) + dot(left[1], right[0])


def forward(signals, first, second, twist):
    rows = signals[0].shape[0]
    stage = dot_pairs(first, split(jnp.concatenate(signals, axis=1)))
    parts = []
    for i in range(len(signals)):
        cos = stage[:rows, i * LANES : (i + 1) * LANES]
        sin = stage[rows:, i * LANES : (i + 1) * LANES]
        parts.append(
            jnp.concatenate(
                [cos * twist[0] + sin * twist[1], cos * twist[1] - sin * twist[0]], axis=1
            )
        )
    spec = dot_pairs(split(jnp.concatenate(parts, axis=0)), second)
    return [
        (spec[i * rows : (i + 1) * rows, :LANES], spec[i * rows : (i + 1) * rows, LANES:])
        for i in range(len(signals))
    ]


def backward(spectra, back, second, twist):
    rows = spectra[0][0].shape[0]
    stacked = jnp.concatenate([jnp.concatenate(pair, axis=1) for pair in spectra], axis=0)
    stage = dot_pairs(split(stacked), second)
    parts = []
    for i in range(len(spectra)):
        re = stage[i * rows : (i + 1) * rows, :LANES]
        im = stage[i * rows : (i + 1) * rows, LANES:]
        parts.append(
            jnp.concatenate(
                [re * twist[0] - im * twist[1], re * twist[1] + im * twist[0]], axis=0
            )
        )
    out = dot_pairs(back, split(jnp.concatenate(parts, axis=1)))
    return [out[:, i * LANES : (i + 1) * LANES] for i in range(len(spectra))]


def times(a, b):
    return (a[0] * b[0] - a[1] * b[1], -(a[0] * b[1] + a[1] * b[0]))


def conj_times(a, b):
    return (a[0] * b[0] + a[1] * b[1], a[1] * b[0] - a[0] * b[1])


def one_hot(order):
    size = order.shape[1]
    place = lax.broadcasted_iota(jnp.int32, (size, size), 0)
    return (place == order).astype(f32).astype(bf16)


def project_kernel(
    features_at,
    order_at,
    cotangent_at,
    w_in_at,
    w_out_at,
    streams_out,
    gather_out,
    features,
    order,
    cotangent,
    w_in,
    w_out,
    done,
):
    copies = [
        pltpu.make_async_copy(source, target, done.at[i])
        for i, (source, target) in enumerate(
            [
                (order_at, order),
                (features_at, features),
                (w_in_at, w_in),
                (cotangent_at, cotangent),
                (w_out_at, w_out),
            ]
        )
    ]
    for copy in copies:
        copy.start()
    width, row_count = features.shape
    copies[0].wait()
    copies[1].wait()
    seq_input = dot(features[...], one_hot(order[...])).astype(bf16)
    copies[2].wait()
    projected = dot(w_in[...], seq_input)
    copies[3].wait()
    copies[4].wait()
    out_grad = lax.dot_general(
        w_out[...], cotangent[...], (((0,), (0,)), ((), ())), preferred_element_type=f32
    )
    if len(streams_out.shape) == 3:
        blocks = streams_out.shape[0]
        parts = [projected[s * width : (s + 1) * width] for s in range(3)] + [out_grad]
        parts = [part.reshape(blocks, width // blocks, row_count) for part in parts]
        streams_out[...] = jnp.concatenate(parts, axis=1).astype(bf16)
    else:
        streams_out[: 3 * width] = projected.astype(bf16)
        streams_out[3 * width :] = out_grad.astype(bf16)
    own = jnp.concatenate([seq_input, cotangent[...]], axis=0)
    gather_out[...] = own


def read_signal(ref, rows):
    if ref.shape[1] == LANES:
        return ref[...]
    return jnp.concatenate(
        [ref[:, i * LANES : (i + 1) * LANES] for i in range(ref.shape[1] // LANES)], axis=0
    )


def write_signal(ref, value):
    if ref.shape[1] == LANES:
        ref[...] = value
        return
    channels = ref.shape[0]
    for i in range(ref.shape[1] // LANES):
        ref[:, i * LANES : (i + 1) * LANES] = value[i * channels : (i + 1) * channels]


def filter_kernel(
    length,
    filter_one,
    filter_two,
    table,
    twist,
    own,
    order,
    spec_one,
    spec_two,
    table_out,
    twist_out,
    own_out,
    order_out,
):
    rows = spec_one.shape[0]
    signals = [read_signal(filter_one, rows), read_signal(filter_two, rows)]
    first, _, second, turns = tables_of(table, twist)
    one, two = forward(signals, first, second, turns)
    spec_one[...] = jnp.concatenate(one, axis=1) * (1.0 / length)
    spec_two[...] = jnp.concatenate(two, axis=1) * (1.0 / length)
    table_out[...] = table[...]
    twist_out[...] = twist[...]
    own_out[...] = own[...]
    order_out[...] = order[...]


def shifted(value, steps, channels):
    if steps == 0:
        return value
    rows, lanes = value.shape
    lane = lax.broadcasted_iota(jnp.int32, value.shape, 1)
    row = lax.broadcasted_iota(jnp.int32, value.shape, 0)
    turned = pltpu.roll(value, steps % lanes, 1)
    if steps > 0:
        carried = jnp.where(row < channels, 0.0, pltpu.roll(turned, channels, 0))
        return jnp.where(lane < steps, carried, turned)
    carried = jnp.where(row >= rows - channels, 0.0, pltpu.roll(turned, rows - channels, 0))
    return jnp.where(lane >= lanes + steps, carried, turned)


def mix_kernel(
    channels,
    scale,
    streams,
    taps,
    spec_one,
    spec_two,
    table,
    twist,
    line,
    short_out,
    product_one,
    product_two,
    *sent_out,
):
    rows = twist.shape[0]
    eight = taps.shape[0]
    first, back, second, twist = tables_of(table, twist)
    if streams.shape[0] == 4 and streams.shape[1] == rows:
        pieces = [streams[s].astype(f32) for s in range(4)]
    else:
        whole = streams[...].astype(f32)
        pieces = [
            whole[:, s * channels : (s + 1) * channels].reshape(rows, LANES) for s in range(4)
        ]
    out_grad = pieces[3]

    def tap(s, k):
        column = jnp.broadcast_to(taps[:, 3 * s + k : 3 * s + k + 1], (eight, LANES))
        column = jnp.broadcast_to(column[None], (rows // eight, eight, LANES))
        return column.reshape(rows, LANES)

    late = [[shifted(pieces[s], k, channels) for k in range(3)] for s in range(3)]
    value, gate_one, gate_two = [
        sum(tap(s, k) * late[s][k] for k in range(3)) for s in range(3)
    ]
    h_one = (spec_one[:, :LANES], spec_one[:, LANES:])
    h_two = (spec_two[:, :LANES], spec_two[:, LANES:])
    value_spec, second_spec = forward([value, out_grad * gate_two], first, second, twist)
    first_mix, grad_first_out = backward(
        [times(h_one, value_spec), conj_times(h_two, second_spec)],
        back,
        second,
        twist,
    )
    first_spec, grad_first_spec = forward(
        [gate_one * first_mix, gate_one * grad_first_out], first, second, twist
    )
    second_mix, grad_value = backward(
        [times(h_two, first_spec), conj_times(h_one, grad_first_spec)],
        back,
        second,
        twist,
    )
    product_one[...] = jnp.concatenate(conj_times(value_spec, grad_first_spec), axis=1)
    product_two[...] = jnp.concatenate(conj_times(first_spec, second_spec), axis=1)
    grads = [grad_value, grad_first_out * first_mix, out_grad * second_mix]
    sent = []
    lane = lax.broadcasted_iota(jnp.int32, (eight, LANES), 1)
    short = jnp.zeros((eight, LANES), f32)
    for s in range(3):
        sent.append(sum(tap(s, k) * shifted(grads[s], -k, channels) for k in range(3)))
        for k in range(3):
            folded = (grads[s] * late[s][k]).reshape(rows // eight, eight, LANES).sum(axis=0)
            total = jnp.sum(folded, axis=1, keepdims=True) * scale
            short = jnp.where(lane == 3 * s + k, total, short)
    sent.append(gate_two * second_mix)
    short_out[...] = short
    if len(sent_out) == 1:
        for s in range(4):
            sent_out[0][s] = sent[s].astype(bf16)
        return
    parts = [part.reshape(rows // channels, channels, LANES) for part in sent]
    packed = jnp.concatenate(parts, axis=1).astype(bf16)
    *sent_out, store = sent_out
    lines, plane = store.shape[:2]
    for i in range(lines):
        store[i] = packed[i * plane : (i + 1) * plane]
    for step in range(lines):
        sent_out[step][...] = store[member(line[0], step)]


def filter_grads_kernel(
    scale, product_one, product_two, table, twist, short, grad_one, grad_two, short_out
):
    _, back, second, twist = tables_of(table, twist)
    spectra = [(ref[:, :LANES], ref[:, LANES:]) for ref in (product_one, product_two)]
    one, two = backward(spectra, back, second, twist)
    write_signal(grad_one, one * scale)
    write_signal(grad_two, two * scale)
    short_out[...] = short[...]


def member(at, k):
    return jnp.bitwise_xor(at, k)


def weights_kernel(channels, scale, lines, *refs):
    line, place, short, *refs, partial_out, moved_out = refs
    met, pieces = refs[:lines], refs[lines:]
    plane, width = len(pieces), pieces[0].shape[0] // 2
    height = 4 * channels
    total = jnp.zeros((lines * height, 2 * width), f32)
    step = 2 if plane % 2 == 0 else 1
    for i in range(0, plane, step):
        left = jnp.concatenate(
            [
                jnp.concatenate([m[member(place[0], i + j)] for m in met], axis=0)
                for j in range(step)
            ],
            axis=1,
        )
        right = jnp.concatenate([pieces[i + j][...] for j in range(step)], axis=1)
        total = total + lax.dot_general(
            left, right, (((1,), (1,)), ((), ())), preferred_element_type=f32
        )
    total = total * scale
    size = height * (width // LANES)
    for k in range(lines):
        parts = []
        for h in range(width // LANES):
            low, high = h * LANES, (h + 1) * LANES
            base = k * height
            parts.append(total[base : base + 3 * channels, low:high])
            parts.append(total[base + 3 * channels : base + height, width + low : width + high])
        owner = member(line[0], k)
        spot = pl.ds(pl.multiple_of(owner * size, size), size)
        partial_out[spot] = jnp.concatenate(parts, axis=0).astype(bf16)
    tail = jnp.concatenate([short[...]] * lines, axis=0)
    owner = lax.broadcasted_iota(jnp.int32, tail.shape, 0) // channels
    partial_out[lines * size :] = jnp.where(owner == line[0], tail, 0.0).astype(bf16)
    parts = [m[...].astype(f32)[:, : 3 * channels] for m in met]
    moved_out[...] = jnp.concatenate(parts, axis=1).astype(bf16)


def sum_kernel(*refs):
    *partials, out = refs
    out[...] = sum(part[...].astype(f32) for part in partials).astype(bf16)


def unorder(grad_projected, w_in, order):
    grad_seq = lax.dot_general(
        w_in, grad_projected, (((0,), (0,)), ((), ())), preferred_element_type=f32
    ).astype(bf16)
    return lax.dot_general(
        grad_seq, one_hot(order), (((1,), (1,)), ((), ())), preferred_element_type=f32
    ).astype(bf16)


def moved_kernel(channels, lines, line, back, w_in, order, features_out, store):
    plane, width = back.shape[0], w_in.shape[1]
    share = plane * channels
    whole = back[...].astype(f32)
    for k in range(lines):
        owner = member(line[0], k)
        for s in range(3):
            start = (3 * k + s) * channels
            spot = pl.ds(pl.multiple_of(s * width + owner * share, share), share)
            store[spot] = whole[:, start : start + channels].reshape(share, LANES)
    features_out[...] = unorder(store[...].astype(bf16), w_in[...], order[...])


def finish_kernel(channels, lines, place, *refs):
    *pieces, w_in_out, w_out_out, short_out, out_rows, short_rows = refs
    width = w_out_out.shape[0]
    share = width // lines
    height = 4 * channels
    size = height * (width // LANES)
    for k, piece in enumerate(pieces):
        rows = piece[...].astype(f32)
        for i in range(lines):
            first = pl.multiple_of(i * share + member(place[0], k) * channels, channels)
            for h in range(width // LANES):
                low, high = h * LANES, (h + 1) * LANES
                base = i * size + h * height
                for s in range(3):
                    spot = pl.ds(pl.multiple_of(s * width + first, channels), channels)
                    start = base + s * channels
                    w_in_out[spot, low:high] = rows[start : start + channels]
                start = base + 3 * channels
                out_rows[pl.ds(first, channels), low:high] = rows[start : start + channels]
            start = lines * size + i * channels
            short_rows[pl.ds(first, channels), :] = rows[start : start + channels]
    w_out_out[...] = out_rows[...].T
    short = short_rows[...].T
    for s in range(3):
        short_out[:, s * width : (s + 1) * width] = short[3 * s : 3 * s + 3, :]


def features_kernel(moved, w_in, order, features_out):
    features_out[...] = unorder(moved[...], w_in[...], order[...])


def swapped(value, axis, count, distance):
    return lax.ppermute(value, axis, [(i, i ^ distance) for i in range(count)])


def spread(value, plane):
    pieces = [value if k == 0 else swapped(value, "fft", plane, k) for k in range(0, plane, 2)]
    return [piece for own in pieces for piece in (own, swapped(own, "fft", plane, 1))]


def shape(dims, dtype=f32):
    return jax.ShapeDtypeStruct(dims, dtype)


def local(features, sink_order, cotangent, w_in, short_taps, w_out, filter_one, filter_two):
    width, row_count = features.shape
    lines, plane = lax.axis_size("seq"), lax.axis_size("fft")
    blocks = lines * plane
    channels, length = filter_one.shape
    rows = channels * blocks
    scale = 1.0 / math.sqrt(length)
    powers = all(n > 1 and n & (n - 1) == 0 for n in (lines, plane))
    whole = channels % 8 == 0 and powers
    table, twist = make_tables(blocks, channels)
    eight = channels if whole else 8
    mine = lax.axis_index(AXES)

    def call(kernel, outs, *args, **options):
        return pl.pallas_call(kernel, out_shape=outs, compiler_params=PARAMS, **options)(*args)

    dims = (blocks, 4 * channels, LANES) if whole else (4 * width, LANES)
    streams, own = pl.pallas_call(
        project_kernel,
        out_shape=(shape(dims, bf16), shape((2 * width, row_count), bf16)),
        in_specs=[pl.BlockSpec(memory_space=pl.ANY)] * 5,
        scratch_shapes=[
            pltpu.VMEM(a.shape, a.dtype)
            for a in (features, sink_order, cotangent, w_in, w_out)
        ]
        + [pltpu.SemaphoreType.DMA((5,))],
        compiler_params=pltpu.CompilerParams(vmem_limit_bytes=60 * 1024 * 1024),
    )(features, sink_order, cotangent, w_in, w_out)
    if not whole:
        streams = streams.reshape(4, blocks, channels, LANES).transpose(1, 0, 2, 3)
        streams = streams.reshape(blocks, 4 * channels, LANES)
    arrived = lax.all_to_all(streams, AXES, split_axis=0, concat_axis=0, tiled=True)
    taps = lax.dynamic_slice_in_dim(short_taps.reshape(3, width, 3), mine * channels, channels, 1)
    taps = taps.transpose(1, 0, 2).reshape(channels, 9)
    if not whole:
        taps = jnp.tile(taps, (8 // channels, 1))
        arrived = arrived.reshape(blocks, 4, channels, LANES).transpose(1, 0, 2, 3)
        arrived = arrived.reshape(4, rows, LANES)
        filter_one, filter_two = [
            h.reshape(channels, blocks, LANES).transpose(1, 0, 2).reshape(rows, LANES)
            for h in (filter_one, filter_two)
        ]
    spec = shape((rows, 2 * LANES))
    spec_one, spec_two, table, twist, own, order = call(
        lambda *refs: filter_kernel(length, *refs),
        (
            spec,
            spec,
            shape(table.shape, bf16),
            shape(twist.shape),
            shape(own.shape, bf16),
            shape(sink_order.shape, jnp.int32),
        ),
        filter_one,
        filter_two,
        table,
        twist,
        own,
        sink_order,
    )
    line = lax.axis_index("seq").astype(jnp.int32).reshape(1)
    place = lax.axis_index("fft").astype(jnp.int32).reshape(1)
    scalar = pl.BlockSpec(memory_space=pltpu.SMEM)
    held = pl.BlockSpec(memory_space=pltpu.VMEM)
    chunk = (plane, 4 * channels, LANES)
    dims = [shape(chunk, bf16)] * lines if whole else [shape((4, rows, LANES), bf16)]
    short, product_one, product_two, *sent = call(
        lambda *refs: mix_kernel(channels, scale, *refs),
        (shape((eight, LANES)), spec, spec, *dims),
        arrived,
        taps,
        spec_one,
        spec_two,
        table,
        twist,
        line,
        in_specs=[held] * 6 + [scalar],
        scratch_shapes=[pltpu.VMEM((lines, *chunk), bf16)] if whole else [],
    )
    grad_one, grad_two, short = call(
        lambda *refs: filter_grads_kernel(scale / length, *refs),
        (shape(filter_one.shape), shape(filter_two.shape), shape(short.shape)),
        product_one,
        product_two,
        table,
        twist,
        short,
    )
    height = channels * 4 * (width // LANES)
    if whole:
        met = [sent[0]] + [swapped(sent[k], "seq", lines, k) for k in range(1, lines)]
        size = lines * height + lines * channels
        partial, moved = call(
            lambda *refs: weights_kernel(channels, scale, lines, *refs),
            (
                shape((size, LANES), bf16),
                shape((plane, 3 * lines * channels, LANES), bf16),
            ),
            line,
            place,
            short,
            *met,
            *[own] + [swapped(own, "fft", plane, k) for k in range(1, plane)],
            in_specs=[scalar] * 2 + [held] * (1 + lines + plane),
        )
        partials = [partial] + [swapped(partial, "seq", lines, k) for k in range(1, lines)]
        back = lax.all_to_all(moved, "fft", split_axis=0, concat_axis=0, tiled=True)
        grad_features = call(
            lambda *refs: moved_kernel(channels, lines, *refs),
            shape(features.shape, bf16),
            line,
            back,
            w_in,
            order,
            in_specs=[scalar] + [held] * 3,
            scratch_shapes=[pltpu.VMEM((3 * width, LANES), f32)],
        )
        rows_sum = call(sum_kernel, shape((size, LANES), bf16), *partials)
        grad_w_in, grad_w_out, short = call(
            lambda *refs: finish_kernel(channels, lines, *refs),
            (shape((3 * width, width)), shape((width, width)), shape((3, 3 * width))),
            place,
            *spread(rows_sum, plane),
            in_specs=[scalar] + [held] * plane,
            scratch_shapes=[pltpu.VMEM((width, width), f32), pltpu.VMEM((width, LANES), f32)],
        )
        return (grad_features, grad_w_in, grad_w_out, short.T, grad_one, grad_two)
    gathered = lax.all_gather(own, AXES, axis=0, tiled=False)
    sent = sent[0]
    sent = sent.reshape(4, blocks, channels, LANES)
    grad_in = jnp.einsum(
        "sbcp,bwp->scw", sent[:3], gathered[:, :width], preferred_element_type=f32
    )
    grad_out = jnp.einsum(
        "bcp,bwp->cw", sent[3], gathered[:, width:], preferred_element_type=f32
    )
    own = jnp.concatenate([grad_in, grad_out[None]]) * scale
    own = own.reshape(height, LANES)
    short = short.reshape(8 // channels, channels, LANES).sum(axis=0)
    own = jnp.concatenate([own, short]).astype(bf16)
    moved = sent[:3].transpose(1, 0, 2, 3).reshape(blocks, 3 * channels, LANES)
    own = jnp.broadcast_to(own[None], (blocks,) + own.shape)
    packed = jnp.concatenate([moved, own], axis=1)
    back = lax.all_to_all(packed, AXES, split_axis=0, concat_axis=0, tiled=True)
    moved = back[:, : 3 * channels].reshape(blocks, 3, channels, LANES)
    moved = moved.transpose(1, 0, 2, 3).reshape(3 * width, LANES)
    weights = back[:, 3 * channels : 3 * channels + height].astype(f32)
    weights = weights.reshape(blocks, 4, channels, width).transpose(1, 0, 2, 3)
    weights = weights.reshape(4 * width, width)
    short = back[:, 3 * channels + height :, :9].astype(f32).reshape(width, 3, 3)
    short = short.transpose(1, 0, 2).reshape(3 * width, 3)
    grad_features = call(
        features_kernel, shape(features.shape, bf16), moved, w_in, sink_order
    )
    grad_one, grad_two = [
        g.reshape(blocks, channels, LANES).transpose(1, 0, 2).reshape(channels, length)
        for g in (grad_one, grad_two)
    ]
    return (
        grad_features,
        weights[: 3 * width],
        weights[3 * width :].T,
        short,
        grad_one,
        grad_two,
    )


def solution(mesh):
    columns, blocks_first, copied = P(None, AXES), P(AXES, None), P()
    return jax.shard_map(
        local,
        mesh=mesh,
        in_specs=(
            columns,
            blocks_first,
            columns,
            copied,
            copied,
            copied,
            blocks_first,
            blocks_first,
        ),
        out_specs=(columns, copied, copied, copied, blocks_first, blocks_first),
        check_vma=False,
    )
```

```python
import math

import jax
import jax.numpy as jnp
import numpy as np
from jax import lax
from jax.experimental import pallas as pl
from jax.experimental.pallas import tpu as pltpu
from jax.sharding import PartitionSpec as P

AXES = ("seq", "fft")
LANES = 128
bf16 = jnp.bfloat16
f32 = jnp.float32
PARAMS = pltpu.CompilerParams(vmem_limit_bytes=24 * 1024 * 1024)


def halves(table):
    high = table.astype(np.float32).astype(jnp.bfloat16)
    low = (table - high.astype(np.float64)).astype(np.float32).astype(jnp.bfloat16)
    return high, low


def make_tables(count, channels):
    length = count * LANES
    outer = np.arange(count, dtype=np.float64) + 0.25
    inner = np.arange(LANES, dtype=np.float64)
    angle = 2.0 * np.pi * outer[:, None] * outer[None, :] / count
    first = np.kron(np.concatenate([np.cos(angle), np.sin(angle)], axis=0), np.eye(channels))
    turn = 2.0 * np.pi * (inner[:, None] * inner[None, :] % LANES) / LANES
    cos, sin = np.cos(turn), np.sin(turn)
    second = np.block([[cos, -sin], [sin, cos]])
    packed = [half for t in (first, second) for half in halves(t)]
    twist = 2.0 * np.pi * outer[:, None] * (inner[None, :] - LANES / 4) / length
    twist = np.repeat(twist, channels, axis=0)
    twist = np.concatenate([np.cos(twist), -np.sin(twist)], axis=1).astype(np.float32)
    return np.concatenate(packed, axis=0), twist


def tables_of(table, twist):
    rows = twist.shape[0]
    at, found = 0, []
    for size in (2 * rows, 2 * LANES):
        pair = []
        for half in range(2):
            pair.append(table[at : at + size])
            at += size
        found.append(tuple(pair))
    first, second = found
    back = tuple(jnp.concatenate([t[:rows], t[rows:]], axis=1) for t in first)
    return first, back, second, (twist[:, :LANES], twist[:, LANES:])


def split(value):
    high = value.astype(bf16)
    low = (value - high.astype(f32)).astype(bf16)
    return high, low


def dot(left, right):
    return jnp.dot(left, right, preferred_element_type=f32)


def dot_pairs(left, right):
    return dot(left[0], right[0]) + dot(left[0], right[1]) + dot(left[1], right[0])


def forward(signals, first, second, twist):
    rows = signals[0].shape[0]
    stage = dot_pairs(first, split(jnp.concatenate(signals, axis=1)))
    parts = []
    for i in range(len(signals)):
        cos = stage[:rows, i * LANES : (i + 1) * LANES]
        sin = stage[rows:, i * LANES : (i + 1) * LANES]
        parts.append(
            jnp.concatenate(
                [cos * twist[0] + sin * twist[1], cos * twist[1] - sin * twist[0]], axis=1
            )
        )
    spec = dot_pairs(split(jnp.concatenate(parts, axis=0)), second)
    return [
        (spec[i * rows : (i + 1) * rows, :LANES], spec[i * rows : (i + 1) * rows, LANES:])
        for i in range(len(signals))
    ]


def backward(spectra, back, second, twist):
    rows = spectra[0][0].shape[0]
    stacked = jnp.concatenate([jnp.concatenate(pair, axis=1) for pair in spectra], axis=0)
    stage = dot_pairs(split(stacked), second)
    parts = []
    for i in range(len(spectra)):
        re = stage[i * rows : (i + 1) * rows, :LANES]
        im = stage[i * rows : (i + 1) * rows, LANES:]
        parts.append(
            jnp.concatenate(
                [re * twist[0] - im * twist[1], re * twist[1] + im * twist[0]], axis=0
            )
        )
    out = dot_pairs(back, split(jnp.concatenate(parts, axis=1)))
    return [out[:, i * LANES : (i + 1) * LANES] for i in range(len(spectra))]


def times(a, b):
    return (a[0] * b[0] - a[1] * b[1], -(a[0] * b[1] + a[1] * b[0]))


def conj_times(a, b):
    return (a[0] * b[0] + a[1] * b[1], a[1] * b[0] - a[0] * b[1])


def one_hot(order):
    size = order.shape[1]
    place = lax.broadcasted_iota(jnp.int32, (size, size), 0)
    return (place == order).astype(f32).astype(bf16)


def project_kernel(
    features_at,
    order_at,
    cotangent_at,
    w_in_at,
    w_out_at,
    streams_out,
    gather_out,
    features,
    order,
    cotangent,
    w_in,
    w_out,
    done,
):
    copies = [
        pltpu.make_async_copy(source, target, done.at[i])
        for i, (source, target) in enumerate(
            [
                (order_at, order),
                (features_at, features),
                (w_in_at, w_in),
                (cotangent_at, cotangent),
                (w_out_at, w_out),
            ]
        )
    ]
    for copy in copies:
        copy.start()
    width, row_count = features.shape
    copies[0].wait()
    copies[1].wait()
    seq_input = dot(features[...], one_hot(order[...])).astype(bf16)
    copies[2].wait()
    projected = dot(w_in[...], seq_input)
    copies[3].wait()
    copies[4].wait()
    out_grad = lax.dot_general(
        w_out[...], cotangent[...], (((0,), (0,)), ((), ())), preferred_element_type=f32
    )
    if len(streams_out.shape) == 3:
        blocks = streams_out.shape[0]
        parts = [projected[s * width : (s + 1) * width] for s in range(3)] + [out_grad]
        parts = [part.reshape(blocks, width // blocks, row_count) for part in parts]
        streams_out[...] = jnp.concatenate(parts, axis=1).astype(bf16)
    else:
        streams_out[: 3 * width] = projected.astype(bf16)
        streams_out[3 * width :] = out_grad.astype(bf16)
    own = jnp.concatenate([seq_input, cotangent[...]], axis=0)
    gather_out[...] = own


def read_signal(ref, rows):
    if ref.shape[1] == LANES:
        return ref[...]
    return jnp.concatenate(
        [ref[:, i * LANES : (i + 1) * LANES] for i in range(ref.shape[1] // LANES)], axis=0
    )


def write_signal(ref, value):
    if ref.shape[1] == LANES:
        ref[...] = value
        return
    channels = ref.shape[0]
    for i in range(ref.shape[1] // LANES):
        ref[:, i * LANES : (i + 1) * LANES] = value[i * channels : (i + 1) * channels]


def filter_kernel(
    length,
    filter_one,
    filter_two,
    table,
    twist,
    own,
    order,
    spec_one,
    spec_two,
    table_out,
    twist_out,
    own_out,
    order_out,
):
    rows = spec_one.shape[0]
    signals = [read_signal(filter_one, rows), read_signal(filter_two, rows)]
    first, _, second, turns = tables_of(table, twist)
    one, two = forward(signals, first, second, turns)
    spec_one[...] = jnp.concatenate(one, axis=1) * (1.0 / length)
    spec_two[...] = jnp.concatenate(two, axis=1) * (1.0 / length)
    table_out[...] = table[...]
    twist_out[...] = twist[...]
    own_out[...] = own[...]
    order_out[...] = order[...]


def shifted(value, steps, channels):
    if steps == 0:
        return value
    rows, lanes = value.shape
    lane = lax.broadcasted_iota(jnp.int32, value.shape, 1)
    row = lax.broadcasted_iota(jnp.int32, value.shape, 0)
    turned = pltpu.roll(value, steps % lanes, 1)
    if steps > 0:
        carried = jnp.where(row < channels, 0.0, pltpu.roll(turned, channels, 0))
        return jnp.where(lane < steps, carried, turned)
    carried = jnp.where(row >= rows - channels, 0.0, pltpu.roll(turned, rows - channels, 0))
    return jnp.where(lane >= lanes + steps, carried, turned)


def mix_kernel(
    channels,
    scale,
    streams,
    taps,
    spec_one,
    spec_two,
    table,
    twist,
    line,
    short_out,
    product_one,
    product_two,
    *sent_out,
):
    rows = twist.shape[0]
    eight = taps.shape[0]
    first, back, second, twist = tables_of(table, twist)
    if streams.shape[0] == 4 and streams.shape[1] == rows:
        pieces = [streams[s].astype(f32) for s in range(4)]
    else:
        whole = streams[...].astype(f32)
        pieces = [
            whole[:, s * channels : (s + 1) * channels].reshape(rows, LANES) for s in range(4)
        ]
    out_grad = pieces[3]

    def tap(s, k):
        column = jnp.broadcast_to(taps[:, 3 * s + k : 3 * s + k + 1], (eight, LANES))
        column = jnp.broadcast_to(column[None], (rows // eight, eight, LANES))
        return column.reshape(rows, LANES)

    late = [[shifted(pieces[s], k, channels) for k in range(3)] for s in range(3)]
    value, gate_one, gate_two = [
        sum(tap(s, k) * late[s][k] for k in range(3)) for s in range(3)
    ]
    h_one = (spec_one[:, :LANES], spec_one[:, LANES:])
    h_two = (spec_two[:, :LANES], spec_two[:, LANES:])
    value_spec, second_spec = forward([value, out_grad * gate_two], first, second, twist)
    first_mix, grad_first_out = backward(
        [times(h_one, value_spec), conj_times(h_two, second_spec)],
        back,
        second,
        twist,
    )
    first_spec, grad_first_spec = forward(
        [gate_one * first_mix, gate_one * grad_first_out], first, second, twist
    )
    second_mix, grad_value = backward(
        [times(h_two, first_spec), conj_times(h_one, grad_first_spec)],
        back,
        second,
        twist,
    )
    product_one[...] = jnp.concatenate(conj_times(value_spec, grad_first_spec), axis=1)
    product_two[...] = jnp.concatenate(conj_times(first_spec, second_spec), axis=1)
    grads = [grad_value, grad_first_out * first_mix, out_grad * second_mix]
    sent = []
    lane = lax.broadcasted_iota(jnp.int32, (eight, LANES), 1)
    short = jnp.zeros((eight, LANES), f32)
    for s in range(3):
        sent.append(sum(tap(s, k) * shifted(grads[s], -k, channels) for k in range(3)))
        for k in range(3):
            folded = (grads[s] * late[s][k]).reshape(rows // eight, eight, LANES).sum(axis=0)
            total = jnp.sum(folded, axis=1, keepdims=True) * scale
            short = jnp.where(lane == 3 * s + k, total, short)
    sent.append(gate_two * second_mix)
    short_out[...] = short
    if len(sent_out) == 1:
        for s in range(4):
            sent_out[0][s] = sent[s].astype(bf16)
        return
    parts = [part.reshape(rows // channels, channels, LANES) for part in sent]
    packed = jnp.concatenate(parts, axis=1).astype(bf16)
    *sent_out, store = sent_out
    lines, plane = store.shape[:2]
    for i in range(lines):
        store[i] = packed[i * plane : (i + 1) * plane]
    for step in range(lines):
        sent_out[step][...] = store[member(line[0], step)]


def filter_grads_kernel(scale, product_one, product_two, table, twist, *refs):
    count = (len(refs) - 2) // 2
    passed, (grad_one, grad_two, *passed_out) = refs[:count], refs[count:]
    _, back, second, twist = tables_of(table, twist)
    spectra = [(ref[:, :LANES], ref[:, LANES:]) for ref in (product_one, product_two)]
    one, two = backward(spectra, back, second, twist)
    write_signal(grad_one, one * scale)
    write_signal(grad_two, two * scale)
    for source, target in zip(passed, passed_out):
        target[...] = source[...]


def member(at, k):
    return jnp.bitwise_xor(at, k)


def weights_kernel(channels, scale, lines, *refs):
    line, place, short, *refs, partial_out, moved_out = refs
    met, pieces = refs[:lines], refs[lines:]
    plane, width = len(pieces), pieces[0].shape[0] // 2
    height = 4 * channels
    total = jnp.zeros((lines * height, 2 * width), f32)
    step = 2 if plane % 2 == 0 else 1
    for i in range(0, plane, step):
        left = jnp.concatenate(
            [
                jnp.concatenate([m[member(place[0], i + j)] for m in met], axis=0)
                for j in range(step)
            ],
            axis=1,
        )
        right = jnp.concatenate([pieces[i + j][...] for j in range(step)], axis=1)
        total = total + lax.dot_general(
            left, right, (((1,), (1,)), ((), ())), preferred_element_type=f32
        )
    total = total * scale
    size = height * (width // LANES)
    for k in range(lines):
        parts = []
        for h in range(width // LANES):
            low, high = h * LANES, (h + 1) * LANES
            base = k * height
            parts.append(total[base : base + 3 * channels, low:high])
            parts.append(total[base + 3 * channels : base + height, width + low : width + high])
        owner = member(line[0], k)
        spot = pl.ds(pl.multiple_of(owner * size, size), size)
        partial_out[spot] = jnp.concatenate(parts, axis=0).astype(bf16)
    tail = jnp.concatenate([short[...]] * lines, axis=0)
    owner = lax.broadcasted_iota(jnp.int32, tail.shape, 0) // channels
    partial_out[lines * size :] = jnp.where(owner == line[0], tail, 0.0).astype(bf16)
    parts = [m[...].astype(f32)[:, : 3 * channels] for m in met]
    moved_out[...] = jnp.concatenate(parts, axis=1).astype(bf16)


def sum_kernel(*refs):
    *partials, out = refs
    out[...] = sum(part[...].astype(f32) for part in partials).astype(bf16)


def unorder(grad_projected, w_in, order):
    grad_seq = lax.dot_general(
        w_in, grad_projected, (((0,), (0,)), ((), ())), preferred_element_type=f32
    ).astype(bf16)
    return lax.dot_general(
        grad_seq, one_hot(order), (((1,), (1,)), ((), ())), preferred_element_type=f32
    ).astype(bf16)


def moved_kernel(
    channels, lines, line, back, w_in, order, passed, features_out, passed_out, store
):
    plane, width = back.shape[0], w_in.shape[1]
    share = plane * channels
    whole = back[...].astype(f32)
    for k in range(lines):
        owner = member(line[0], k)
        for s in range(3):
            start = (3 * k + s) * channels
            spot = pl.ds(pl.multiple_of(s * width + owner * share, share), share)
            store[spot] = whole[:, start : start + channels].reshape(share, LANES)
    passed_out[...] = passed[...]
    features_out[...] = unorder(store[...].astype(bf16), w_in[...], order[...])


def finish_kernel(channels, lines, place, *refs):
    *pieces, w_in_out, w_out_out, short_out, out_rows, short_rows = refs
    width = w_out_out.shape[0]
    share = width // lines
    height = 4 * channels
    size = height * (width // LANES)
    for k, piece in enumerate(pieces):
        rows = piece[...].astype(f32)
        for i in range(lines):
            first = pl.multiple_of(i * share + member(place[0], k) * channels, channels)
            for h in range(width // LANES):
                low, high = h * LANES, (h + 1) * LANES
                base = i * size + h * height
                for s in range(3):
                    spot = pl.ds(pl.multiple_of(s * width + first, channels), channels)
                    start = base + s * channels
                    w_in_out[spot, low:high] = rows[start : start + channels]
                start = base + 3 * channels
                out_rows[pl.ds(first, channels), low:high] = rows[start : start + channels]
            start = lines * size + i * channels
            short_rows[pl.ds(first, channels), :] = rows[start : start + channels]
    w_out_out[...] = out_rows[...].T
    short = short_rows[...].T
    for s in range(3):
        short_out[:, s * width : (s + 1) * width] = short[3 * s : 3 * s + 3, :]


def features_kernel(moved, w_in, order, features_out):
    features_out[...] = unorder(moved[...], w_in[...], order[...])


def swapped(value, axis, count, distance):
    return lax.ppermute(value, axis, [(i, i ^ distance) for i in range(count)])


def shape(dims, dtype=f32):
    return jax.ShapeDtypeStruct(dims, dtype)


def local(features, sink_order, cotangent, w_in, short_taps, w_out, filter_one, filter_two):
    width, row_count = features.shape
    lines, plane = lax.axis_size("seq"), lax.axis_size("fft")
    blocks = lines * plane
    channels, length = filter_one.shape
    rows = channels * blocks
    scale = 1.0 / math.sqrt(length)
    powers = all(n > 1 and n & (n - 1) == 0 for n in (lines, plane))
    whole = channels % 8 == 0 and powers
    table, twist = make_tables(blocks, channels)
    eight = channels if whole else 8
    mine = lax.axis_index(AXES)

    def call(kernel, outs, *args, **options):
        return pl.pallas_call(kernel, out_shape=outs, compiler_params=PARAMS, **options)(*args)

    dims = (blocks, 4 * channels, LANES) if whole else (4 * width, LANES)
    streams, own = pl.pallas_call(
        project_kernel,
        out_shape=(shape(dims, bf16), shape((2 * width, row_count), bf16)),
        in_specs=[pl.BlockSpec(memory_space=pl.ANY)] * 5,
        scratch_shapes=[
            pltpu.VMEM(a.shape, a.dtype)
            for a in (features, sink_order, cotangent, w_in, w_out)
        ]
        + [pltpu.SemaphoreType.DMA((5,))],
        compiler_params=pltpu.CompilerParams(vmem_limit_bytes=60 * 1024 * 1024),
    )(features, sink_order, cotangent, w_in, w_out)
    if not whole:
        streams = streams.reshape(4, blocks, channels, LANES).transpose(1, 0, 2, 3)
        streams = streams.reshape(blocks, 4 * channels, LANES)
    arrived = lax.all_to_all(streams, AXES, split_axis=0, concat_axis=0, tiled=True)
    taps = lax.dynamic_slice_in_dim(short_taps.reshape(3, width, 3), mine * channels, channels, 1)
    taps = taps.transpose(1, 0, 2).reshape(channels, 9)
    if not whole:
        taps = jnp.tile(taps, (8 // channels, 1))
        arrived = arrived.reshape(blocks, 4, channels, LANES).transpose(1, 0, 2, 3)
        arrived = arrived.reshape(4, rows, LANES)
        filter_one, filter_two = [
            h.reshape(channels, blocks, LANES).transpose(1, 0, 2).reshape(rows, LANES)
            for h in (filter_one, filter_two)
        ]
    spec = shape((rows, 2 * LANES))
    spec_one, spec_two, table, twist, own, order = call(
        lambda *refs: filter_kernel(length, *refs),
        (
            spec,
            spec,
            shape(table.shape, bf16),
            shape(twist.shape),
            shape(own.shape, bf16),
            shape(sink_order.shape, jnp.int32),
        ),
        filter_one,
        filter_two,
        table,
        twist,
        own,
        sink_order,
    )
    line = lax.axis_index("seq").astype(jnp.int32).reshape(1)
    place = lax.axis_index("fft").astype(jnp.int32).reshape(1)
    scalar = pl.BlockSpec(memory_space=pltpu.SMEM)
    held = pl.BlockSpec(memory_space=pltpu.VMEM)
    chunk = (plane, 4 * channels, LANES)
    dims = [shape(chunk, bf16)] * lines if whole else [shape((4, rows, LANES), bf16)]
    short, product_one, product_two, *sent = call(
        lambda *refs: mix_kernel(channels, scale, *refs),
        (shape((eight, LANES)), spec, spec, *dims),
        arrived,
        taps,
        spec_one,
        spec_two,
        table,
        twist,
        line,
        in_specs=[held] * 6 + [scalar],
        scratch_shapes=[pltpu.VMEM((lines, *chunk), bf16)] if whole else [],
    )
    passed = [short]
    if whole:
        passed += [swapped(own, "fft", plane, k) for k in range(2, plane, 2)]
    grad_one, grad_two, short, *pieces = call(
        lambda *refs: filter_grads_kernel(scale / length, *refs),
        (
            shape(filter_one.shape),
            shape(filter_two.shape),
            *[shape(a.shape, a.dtype) for a in passed],
        ),
        product_one,
        product_two,
        table,
        twist,
        *passed,
    )
    height = channels * 4 * (width // LANES)
    if whole:
        met = [sent[0]] + [swapped(sent[k], "seq", lines, k) for k in range(1, lines)]
        size = lines * height + lines * channels
        partial, moved = call(
            lambda *refs: weights_kernel(channels, scale, lines, *refs),
            (
                shape((size, LANES), bf16),
                shape((plane, 3 * lines * channels, LANES), bf16),
            ),
            line,
            place,
            short,
            *met,
            *[a for piece in (own, *pieces) for a in (piece, swapped(piece, "fft", plane, 1))],
            in_specs=[scalar] * 2 + [held] * (1 + lines + plane),
        )
        partials = [partial] + [swapped(partial, "seq", lines, k) for k in range(1, lines)]
        back = lax.all_to_all(moved, "fft", split_axis=0, concat_axis=0, tiled=True)
        rows_sum = call(sum_kernel, shape((size, LANES), bf16), *partials)
        across = [swapped(rows_sum, "fft", plane, k) for k in range(2, plane, 2)]
        grad_features, passed = call(
            lambda *refs: moved_kernel(channels, lines, *refs),
            (shape(features.shape, bf16), shape((size, LANES), bf16)),
            line,
            back,
            w_in,
            order,
            rows_sum,
            in_specs=[scalar] + [held] * 4,
            scratch_shapes=[pltpu.VMEM((3 * width, LANES), f32)],
        )
        spread = [rows_sum, swapped(passed, "fft", plane, 1)]
        spread += [a for piece in across for a in (piece, swapped(piece, "fft", plane, 1))]
        grad_w_in, grad_w_out, short = call(
            lambda *refs: finish_kernel(channels, lines, *refs),
            (shape((3 * width, width)), shape((width, width)), shape((3, 3 * width))),
            place,
            *spread,
            in_specs=[scalar] + [held] * plane,
            scratch_shapes=[pltpu.VMEM((width, width), f32), pltpu.VMEM((width, LANES), f32)],
        )
        return (grad_features, grad_w_in, grad_w_out, short.T, grad_one, grad_two)
    gathered = lax.all_gather(own, AXES, axis=0, tiled=False)
    sent = sent[0]
    sent = sent.reshape(4, blocks, channels, LANES)
    grad_in = jnp.einsum(
        "sbcp,bwp->scw", sent[:3], gathered[:, :width], preferred_element_type=f32
    )
    grad_out = jnp.einsum(
        "bcp,bwp->cw", sent[3], gathered[:, width:], preferred_element_type=f32
    )
    own = jnp.concatenate([grad_in, grad_out[None]]) * scale
    own = own.reshape(height, LANES)
    short = short.reshape(8 // channels, channels, LANES).sum(axis=0)
    own = jnp.concatenate([own, short]).astype(bf16)
    moved = sent[:3].transpose(1, 0, 2, 3).reshape(blocks, 3 * channels, LANES)
    own = jnp.broadcast_to(own[None], (blocks,) + own.shape)
    packed = jnp.concatenate([moved, own], axis=1)
    back = lax.all_to_all(packed, AXES, split_axis=0, concat_axis=0, tiled=True)
    moved = back[:, : 3 * channels].reshape(blocks, 3, channels, LANES)
    moved = moved.transpose(1, 0, 2, 3).reshape(3 * width, LANES)
    weights = back[:, 3 * channels : 3 * channels + height].astype(f32)
    weights = weights.reshape(blocks, 4, channels, width).transpose(1, 0, 2, 3)
    weights = weights.reshape(4 * width, width)
    short = back[:, 3 * channels + height :, :9].astype(f32).reshape(width, 3, 3)
    short = short.transpose(1, 0, 2).reshape(3 * width, 3)
    grad_features = call(
        features_kernel, shape(features.shape, bf16), moved, w_in, sink_order
    )
    grad_one, grad_two = [
        g.reshape(blocks, channels, LANES).transpose(1, 0, 2).reshape(channels, length)
        for g in (grad_one, grad_two)
    ]
    return (
        grad_features,
        weights[: 3 * width],
        weights[3 * width :].T,
        short,
        grad_one,
        grad_two,
    )


def solution(mesh):
    columns, blocks_first, copied = P(None, AXES), P(AXES, None), P()
    return jax.shard_map(
        local,
        mesh=mesh,
        in_specs=(
            columns,
            blocks_first,
            columns,
            copied,
            copied,
            copied,
            blocks_first,
            blocks_first,
        ),
        out_specs=(columns, copied, copied, copied, blocks_first, blocks_first),
        check_vma=False,
    )
```

```python
import math

import jax
import jax.numpy as jnp
import numpy as np
from jax import lax
from jax.experimental import pallas as pl
from jax.experimental.pallas import tpu as pltpu
from jax.sharding import PartitionSpec as P

AXES = ("seq", "fft")
LANES = 128
bf16 = jnp.bfloat16
f32 = jnp.float32
PARAMS = pltpu.CompilerParams(vmem_limit_bytes=24 * 1024 * 1024)


def halves(table):
    high = table.astype(np.float32).astype(jnp.bfloat16)
    low = (table - high.astype(np.float64)).astype(np.float32).astype(jnp.bfloat16)
    return high, low


def make_tables(count, channels):
    length = count * LANES
    outer = np.arange(count, dtype=np.float64) + 0.25
    inner = np.arange(LANES, dtype=np.float64)
    angle = 2.0 * np.pi * outer[:, None] * outer[None, :] / count
    first = np.kron(np.concatenate([np.cos(angle), np.sin(angle)], axis=0), np.eye(channels))
    turn = 2.0 * np.pi * (inner[:, None] * inner[None, :] % LANES) / LANES
    cos, sin = np.cos(turn), np.sin(turn)
    second = np.block([[cos, -sin], [sin, cos]])
    packed = [half for t in (first, second) for half in halves(t)]
    twist = 2.0 * np.pi * outer[:, None] * (inner[None, :] - LANES / 4) / length
    twist = np.repeat(twist, channels, axis=0)
    twist = np.concatenate([np.cos(twist), -np.sin(twist)], axis=1).astype(np.float32)
    return np.concatenate(packed, axis=0), twist


def tables_of(table, twist):
    rows = twist.shape[0]
    at, found = 0, []
    for size in (2 * rows, 2 * LANES):
        pair = []
        for half in range(2):
            pair.append(table[at : at + size])
            at += size
        found.append(tuple(pair))
    first, second = found
    back = tuple(jnp.concatenate([t[:rows], t[rows:]], axis=1) for t in first)
    return first, back, second, (twist[:, :LANES], twist[:, LANES:])


def split(value):
    high = value.astype(bf16)
    low = (value - high.astype(f32)).astype(bf16)
    return high, low


def dot(left, right):
    return jnp.dot(left, right, preferred_element_type=f32)


def dot_pairs(left, right):
    return dot(left[0], right[0]) + dot(left[0], right[1]) + dot(left[1], right[0])


def forward(signals, first, second, twist):
    rows = signals[0].shape[0]
    stage = dot_pairs(first, split(jnp.concatenate(signals, axis=1)))
    parts = []
    for i in range(len(signals)):
        cos = stage[:rows, i * LANES : (i + 1) * LANES]
        sin = stage[rows:, i * LANES : (i + 1) * LANES]
        parts.append(
            jnp.concatenate(
                [cos * twist[0] + sin * twist[1], cos * twist[1] - sin * twist[0]], axis=1
            )
        )
    spec = dot_pairs(split(jnp.concatenate(parts, axis=0)), second)
    return [
        (spec[i * rows : (i + 1) * rows, :LANES], spec[i * rows : (i + 1) * rows, LANES:])
        for i in range(len(signals))
    ]


def backward(spectra, back, second, twist):
    rows = spectra[0][0].shape[0]
    stacked = jnp.concatenate([jnp.concatenate(pair, axis=1) for pair in spectra], axis=0)
    stage = dot_pairs(split(stacked), second)
    parts = []
    for i in range(len(spectra)):
        re = stage[i * rows : (i + 1) * rows, :LANES]
        im = stage[i * rows : (i + 1) * rows, LANES:]
        parts.append(
            jnp.concatenate(
                [re * twist[0] - im * twist[1], re * twist[1] + im * twist[0]], axis=0
            )
        )
    out = dot_pairs(back, split(jnp.concatenate(parts, axis=1)))
    return [out[:, i * LANES : (i + 1) * LANES] for i in range(len(spectra))]


def times(a, b):
    return (a[0] * b[0] - a[1] * b[1], -(a[0] * b[1] + a[1] * b[0]))


def conj_times(a, b):
    return (a[0] * b[0] + a[1] * b[1], a[1] * b[0] - a[0] * b[1])


def one_hot(order):
    size = order.shape[1]
    place = lax.broadcasted_iota(jnp.int32, (size, size), 0)
    return (place == order).astype(f32).astype(bf16)


def project_kernel(
    features_at,
    order_at,
    cotangent_at,
    w_in_at,
    w_out_at,
    streams_out,
    gather_out,
    features,
    order,
    cotangent,
    w_in,
    w_out,
    done,
):
    copies = [
        pltpu.make_async_copy(source, target, done.at[i])
        for i, (source, target) in enumerate(
            [
                (order_at, order),
                (features_at, features),
                (w_in_at, w_in),
                (cotangent_at, cotangent),
                (w_out_at, w_out),
            ]
        )
    ]
    for copy in copies:
        copy.start()
    width, row_count = features.shape
    copies[0].wait()
    copies[1].wait()
    seq_input = dot(features[...], one_hot(order[...])).astype(bf16)
    copies[2].wait()
    projected = dot(w_in[...], seq_input)
    copies[3].wait()
    copies[4].wait()
    out_grad = lax.dot_general(
        w_out[...], cotangent[...], (((0,), (0,)), ((), ())), preferred_element_type=f32
    )
    if len(streams_out.shape) == 3:
        blocks = streams_out.shape[0]
        parts = [projected[s * width : (s + 1) * width] for s in range(3)] + [out_grad]
        parts = [part.reshape(blocks, width // blocks, row_count) for part in parts]
        streams_out[...] = jnp.concatenate(parts, axis=1).astype(bf16)
    else:
        streams_out[: 3 * width] = projected.astype(bf16)
        streams_out[3 * width :] = out_grad.astype(bf16)
    own = jnp.concatenate([seq_input, cotangent[...]], axis=0)
    gather_out[...] = own


def read_signal(ref, rows):
    if ref.shape[1] == LANES:
        return ref[...]
    return jnp.concatenate(
        [ref[:, i * LANES : (i + 1) * LANES] for i in range(ref.shape[1] // LANES)], axis=0
    )


def write_signal(ref, value):
    if ref.shape[1] == LANES:
        ref[...] = value
        return
    channels = ref.shape[0]
    for i in range(ref.shape[1] // LANES):
        ref[:, i * LANES : (i + 1) * LANES] = value[i * channels : (i + 1) * channels]


def filter_kernel(
    length,
    filter_one,
    filter_two,
    table,
    twist,
    own,
    order,
    spec_one,
    spec_two,
    table_out,
    twist_out,
    own_out,
    order_out,
):
    rows = spec_one.shape[0]
    signals = [read_signal(filter_one, rows), read_signal(filter_two, rows)]
    first, _, second, turns = tables_of(table, twist)
    one, two = forward(signals, first, second, turns)
    spec_one[...] = jnp.concatenate(one, axis=1) * (1.0 / length)
    spec_two[...] = jnp.concatenate(two, axis=1) * (1.0 / length)
    table_out[...] = table[...]
    twist_out[...] = twist[...]
    own_out[...] = own[...]
    order_out[...] = order[...]


def shifted(value, steps, channels):
    if steps == 0:
        return value
    rows, lanes = value.shape
    lane = lax.broadcasted_iota(jnp.int32, value.shape, 1)
    row = lax.broadcasted_iota(jnp.int32, value.shape, 0)
    turned = pltpu.roll(value, steps % lanes, 1)
    if steps > 0:
        carried = jnp.where(row < channels, 0.0, pltpu.roll(turned, channels, 0))
        return jnp.where(lane < steps, carried, turned)
    carried = jnp.where(row >= rows - channels, 0.0, pltpu.roll(turned, rows - channels, 0))
    return jnp.where(lane >= lanes + steps, carried, turned)


def mix_kernel(
    channels,
    scale,
    streams,
    taps,
    spec_one,
    spec_two,
    table,
    twist,
    line,
    short_out,
    product_one,
    product_two,
    *sent_out,
):
    rows = twist.shape[0]
    eight = taps.shape[0]
    first, back, second, twist = tables_of(table, twist)
    if streams.shape[0] == 4 and streams.shape[1] == rows:
        pieces = [streams[s].astype(f32) for s in range(4)]
    else:
        whole = streams[...].astype(f32)
        pieces = [
            whole[:, s * channels : (s + 1) * channels].reshape(rows, LANES) for s in range(4)
        ]
    out_grad = pieces[3]

    def tap(s, k):
        column = jnp.broadcast_to(taps[:, 3 * s + k : 3 * s + k + 1], (eight, LANES))
        column = jnp.broadcast_to(column[None], (rows // eight, eight, LANES))
        return column.reshape(rows, LANES)

    late = [[shifted(pieces[s], k, channels) for k in range(3)] for s in range(3)]
    value, gate_one, gate_two = [
        sum(tap(s, k) * late[s][k] for k in range(3)) for s in range(3)
    ]
    h_one = (spec_one[:, :LANES], spec_one[:, LANES:])
    h_two = (spec_two[:, :LANES], spec_two[:, LANES:])
    value_spec, second_spec = forward([value, out_grad * gate_two], first, second, twist)
    first_mix, grad_first_out = backward(
        [times(h_one, value_spec), conj_times(h_two, second_spec)],
        back,
        second,
        twist,
    )
    first_spec, grad_first_spec = forward(
        [gate_one * first_mix, gate_one * grad_first_out], first, second, twist
    )
    second_mix, grad_value = backward(
        [times(h_two, first_spec), conj_times(h_one, grad_first_spec)],
        back,
        second,
        twist,
    )
    product_one[...] = jnp.concatenate(conj_times(value_spec, grad_first_spec), axis=1)
    product_two[...] = jnp.concatenate(conj_times(first_spec, second_spec), axis=1)
    grads = [grad_value, grad_first_out * first_mix, out_grad * second_mix]
    sent = []
    lane = lax.broadcasted_iota(jnp.int32, (eight, LANES), 1)
    short = jnp.zeros((eight, LANES), f32)
    for s in range(3):
        sent.append(sum(tap(s, k) * shifted(grads[s], -k, channels) for k in range(3)))
        for k in range(3):
            folded = (grads[s] * late[s][k]).reshape(rows // eight, eight, LANES).sum(axis=0)
            total = jnp.sum(folded, axis=1, keepdims=True) * scale
            short = jnp.where(lane == 3 * s + k, total, short)
    sent.append(gate_two * second_mix)
    short_out[...] = short
    if len(sent_out) == 1:
        for s in range(4):
            sent_out[0][s] = sent[s].astype(bf16)
        return
    parts = [part.reshape(rows // channels, channels, LANES) for part in sent]
    packed = jnp.concatenate(parts, axis=1).astype(bf16)
    *sent_out, store = sent_out
    lines, plane = store.shape[:2]
    for i in range(lines):
        store[i] = packed[i * plane : (i + 1) * plane]
    for step in range(lines):
        sent_out[step][...] = store[member(line[0], step)]


def filter_grads_kernel(scale, product_one, product_two, table, twist, *refs):
    count = (len(refs) - 2) // 2
    passed, (grad_one, grad_two, *passed_out) = refs[:count], refs[count:]
    _, back, second, twist = tables_of(table, twist)
    spectra = [(ref[:, :LANES], ref[:, LANES:]) for ref in (product_one, product_two)]
    one, two = backward(spectra, back, second, twist)
    write_signal(grad_one, one * scale)
    write_signal(grad_two, two * scale)
    for source, target in zip(passed, passed_out):
        target[...] = source[...]


def member(at, k):
    return jnp.bitwise_xor(at, k)


def weights_kernel(channels, scale, lines, *refs):
    line, place, short, *refs, partial_out, moved_out = refs
    met, pieces = refs[:lines], refs[lines:]
    plane, width = len(pieces), pieces[0].shape[0] // 2
    height = 4 * channels
    total = jnp.zeros((lines * height, 2 * width), f32)
    step = 2 if plane % 2 == 0 else 1
    for i in range(0, plane, step):
        left = jnp.concatenate(
            [
                jnp.concatenate([m[member(place[0], i + j)] for m in met], axis=0)
                for j in range(step)
            ],
            axis=1,
        )
        right = jnp.concatenate([pieces[i + j][...] for j in range(step)], axis=1)
        total = total + lax.dot_general(
            left, right, (((1,), (1,)), ((), ())), preferred_element_type=f32
        )
    total = total * scale
    size = height * (width // LANES)
    for k in range(lines):
        parts = []
        for h in range(width // LANES):
            low, high = h * LANES, (h + 1) * LANES
            base = k * height
            parts.append(total[base : base + 3 * channels, low:high])
            parts.append(total[base + 3 * channels : base + height, width + low : width + high])
        owner = member(line[0], k)
        spot = pl.ds(pl.multiple_of(owner * size, size), size)
        partial_out[spot] = jnp.concatenate(parts, axis=0).astype(bf16)
    tail = jnp.concatenate([short[...]] * lines, axis=0)
    owner = lax.broadcasted_iota(jnp.int32, tail.shape, 0) // channels
    partial_out[lines * size :] = jnp.where(owner == line[0], tail, 0.0).astype(bf16)
    parts = [m[...].astype(f32)[:, : 3 * channels] for m in met]
    moved_out[...] = jnp.concatenate(parts, axis=1).astype(bf16)


def sum_kernel(*refs):
    *partials, out = refs
    out[...] = sum(part[...].astype(f32) for part in partials).astype(bf16)


def unorder(grad_projected, w_in, order):
    grad_seq = lax.dot_general(
        w_in, grad_projected, (((0,), (0,)), ((), ())), preferred_element_type=f32
    ).astype(bf16)
    return lax.dot_general(
        grad_seq, one_hot(order), (((1,), (1,)), ((), ())), preferred_element_type=f32
    ).astype(bf16)


def moved_kernel(channels, lines, line, back, w_in, order, features_out, store):
    plane, width = back.shape[0], w_in.shape[1]
    share = plane * channels
    whole = back[...].astype(f32)
    for k in range(lines):
        owner = member(line[0], k)
        for s in range(3):
            start = (3 * k + s) * channels
            spot = pl.ds(pl.multiple_of(s * width + owner * share, share), share)
            store[spot] = whole[:, start : start + channels].reshape(share, LANES)
    features_out[...] = unorder(store[...].astype(bf16), w_in[...], order[...])


def finish_kernel(channels, lines, place, *refs):
    *pieces, w_in_out, w_out_out, short_out, out_rows, short_rows = refs
    width = w_out_out.shape[0]
    share = width // lines
    height = 4 * channels
    size = height * (width // LANES)
    for k, piece in enumerate(pieces):
        rows = piece[...].astype(f32)
        for i in range(lines):
            first = pl.multiple_of(i * share + member(place[0], k) * channels, channels)
            for h in range(width // LANES):
                low, high = h * LANES, (h + 1) * LANES
                base = i * size + h * height
                for s in range(3):
                    spot = pl.ds(pl.multiple_of(s * width + first, channels), channels)
                    start = base + s * channels
                    w_in_out[spot, low:high] = rows[start : start + channels]
                start = base + 3 * channels
                out_rows[pl.ds(first, channels), low:high] = rows[start : start + channels]
            start = lines * size + i * channels
            short_rows[pl.ds(first, channels), :] = rows[start : start + channels]
    w_out_out[...] = out_rows[...].T
    short = short_rows[...].T
    for s in range(3):
        short_out[:, s * width : (s + 1) * width] = short[3 * s : 3 * s + 3, :]


def features_kernel(moved, w_in, order, features_out):
    features_out[...] = unorder(moved[...], w_in[...], order[...])


def swapped(value, axis, count, distance):
    return lax.ppermute(value, axis, [(i, i ^ distance) for i in range(count)])


def shape(dims, dtype=f32):
    return jax.ShapeDtypeStruct(dims, dtype)


def local(features, sink_order, cotangent, w_in, short_taps, w_out, filter_one, filter_two):
    width, row_count = features.shape
    lines, plane = lax.axis_size("seq"), lax.axis_size("fft")
    blocks = lines * plane
    channels, length = filter_one.shape
    rows = channels * blocks
    scale = 1.0 / math.sqrt(length)
    powers = all(n > 1 and n & (n - 1) == 0 for n in (lines, plane))
    whole = channels % 8 == 0 and powers
    table, twist = make_tables(blocks, channels)
    eight = channels if whole else 8
    mine = lax.axis_index(AXES)

    def call(kernel, outs, *args, **options):
        return pl.pallas_call(kernel, out_shape=outs, compiler_params=PARAMS, **options)(*args)

    dims = (blocks, 4 * channels, LANES) if whole else (4 * width, LANES)
    streams, own = pl.pallas_call(
        project_kernel,
        out_shape=(shape(dims, bf16), shape((2 * width, row_count), bf16)),
        in_specs=[pl.BlockSpec(memory_space=pl.ANY)] * 5,
        scratch_shapes=[
            pltpu.VMEM(a.shape, a.dtype)
            for a in (features, sink_order, cotangent, w_in, w_out)
        ]
        + [pltpu.SemaphoreType.DMA((5,))],
        compiler_params=pltpu.CompilerParams(vmem_limit_bytes=60 * 1024 * 1024),
    )(features, sink_order, cotangent, w_in, w_out)
    if not whole:
        streams = streams.reshape(4, blocks, channels, LANES).transpose(1, 0, 2, 3)
        streams = streams.reshape(blocks, 4 * channels, LANES)
    arrived = lax.all_to_all(streams, AXES, split_axis=0, concat_axis=0, tiled=True)
    taps = lax.dynamic_slice_in_dim(short_taps.reshape(3, width, 3), mine * channels, channels, 1)
    taps = taps.transpose(1, 0, 2).reshape(channels, 9)
    if not whole:
        taps = jnp.tile(taps, (8 // channels, 1))
        arrived = arrived.reshape(blocks, 4, channels, LANES).transpose(1, 0, 2, 3)
        arrived = arrived.reshape(4, rows, LANES)
        filter_one, filter_two = [
            h.reshape(channels, blocks, LANES).transpose(1, 0, 2).reshape(rows, LANES)
            for h in (filter_one, filter_two)
        ]
    spec = shape((rows, 2 * LANES))
    spec_one, spec_two, table, twist, own, order = call(
        lambda *refs: filter_kernel(length, *refs),
        (
            spec,
            spec,
            shape(table.shape, bf16),
            shape(twist.shape),
            shape(own.shape, bf16),
            shape(sink_order.shape, jnp.int32),
        ),
        filter_one,
        filter_two,
        table,
        twist,
        own,
        sink_order,
    )
    line = lax.axis_index("seq").astype(jnp.int32).reshape(1)
    place = lax.axis_index("fft").astype(jnp.int32).reshape(1)
    scalar = pl.BlockSpec(memory_space=pltpu.SMEM)
    held = pl.BlockSpec(memory_space=pltpu.VMEM)
    chunk = (plane, 4 * channels, LANES)
    dims = [shape(chunk, bf16)] * lines if whole else [shape((4, rows, LANES), bf16)]
    short, product_one, product_two, *sent = call(
        lambda *refs: mix_kernel(channels, scale, *refs),
        (shape((eight, LANES)), spec, spec, *dims),
        arrived,
        taps,
        spec_one,
        spec_two,
        table,
        twist,
        line,
        in_specs=[held] * 6 + [scalar],
        scratch_shapes=[pltpu.VMEM((lines, *chunk), bf16)] if whole else [],
    )
    passed = [short]
    if whole:
        met = [sent[0]] + [swapped(sent[k], "seq", lines, k) for k in range(1, lines)]
        pieces = [swapped(own, "fft", plane, k) for k in (1, *range(2, plane, 2))]
        passed += [met[1], *pieces]
    grad_one, grad_two, short, *passed = call(
        lambda *refs: filter_grads_kernel(scale / length, *refs),
        (
            shape(filter_one.shape),
            shape(filter_two.shape),
            *[shape(a.shape, a.dtype) for a in passed],
        ),
        product_one,
        product_two,
        table,
        twist,
        *passed,
    )
    height = channels * 4 * (width // LANES)
    if whole:
        met[1], beside, *pieces = passed
        pieces = [a for p in pieces for a in (p, swapped(p, "fft", plane, 1))]
        size = lines * height + lines * channels
        partial, moved = call(
            lambda *refs: weights_kernel(channels, scale, lines, *refs),
            (
                shape((size, LANES), bf16),
                shape((plane, 3 * lines * channels, LANES), bf16),
            ),
            line,
            place,
            short,
            *met,
            own,
            beside,
            *pieces,
            in_specs=[scalar] * 2 + [held] * (1 + lines + plane),
        )
        partials = [partial] + [swapped(partial, "seq", lines, k) for k in range(1, lines)]
        back = lax.all_to_all(moved, "fft", split_axis=0, concat_axis=0, tiled=True)
        rows_sum = call(sum_kernel, shape((size, LANES), bf16), *partials)
        grad_features = call(
            lambda *refs: moved_kernel(channels, lines, *refs),
            shape(features.shape, bf16),
            line,
            back,
            w_in,
            order,
            in_specs=[scalar] + [held] * 3,
            scratch_shapes=[pltpu.VMEM((3 * width, LANES), f32)],
        )
        spread = [rows_sum] + [swapped(rows_sum, "fft", plane, k) for k in range(2, plane, 2)]
        spread = [a for piece in spread for a in (piece, swapped(piece, "fft", plane, 1))]
        grad_w_in, grad_w_out, short = call(
            lambda *refs: finish_kernel(channels, lines, *refs),
            (shape((3 * width, width)), shape((width, width)), shape((3, 3 * width))),
            place,
            *spread,
            in_specs=[scalar] + [held] * plane,
            scratch_shapes=[pltpu.VMEM((width, width), f32), pltpu.VMEM((width, LANES), f32)],
        )
        return (grad_features, grad_w_in, grad_w_out, short.T, grad_one, grad_two)
    gathered = lax.all_gather(own, AXES, axis=0, tiled=False)
    sent = sent[0]
    sent = sent.reshape(4, blocks, channels, LANES)
    grad_in = jnp.einsum(
        "sbcp,bwp->scw", sent[:3], gathered[:, :width], preferred_element_type=f32
    )
    grad_out = jnp.einsum(
        "bcp,bwp->cw", sent[3], gathered[:, width:], preferred_element_type=f32
    )
    own = jnp.concatenate([grad_in, grad_out[None]]) * scale
    own = own.reshape(height, LANES)
    short = short.reshape(8 // channels, channels, LANES).sum(axis=0)
    own = jnp.concatenate([own, short]).astype(bf16)
    moved = sent[:3].transpose(1, 0, 2, 3).reshape(blocks, 3 * channels, LANES)
    own = jnp.broadcast_to(own[None], (blocks,) + own.shape)
    packed = jnp.concatenate([moved, own], axis=1)
    back = lax.all_to_all(packed, AXES, split_axis=0, concat_axis=0, tiled=True)
    moved = back[:, : 3 * channels].reshape(blocks, 3, channels, LANES)
    moved = moved.transpose(1, 0, 2, 3).reshape(3 * width, LANES)
    weights = back[:, 3 * channels : 3 * channels + height].astype(f32)
    weights = weights.reshape(blocks, 4, channels, width).transpose(1, 0, 2, 3)
    weights = weights.reshape(4 * width, width)
    short = back[:, 3 * channels + height :, :9].astype(f32).reshape(width, 3, 3)
    short = short.transpose(1, 0, 2).reshape(3 * width, 3)
    grad_features = call(
        features_kernel, shape(features.shape, bf16), moved, w_in, sink_order
    )
    grad_one, grad_two = [
        g.reshape(blocks, channels, LANES).transpose(1, 0, 2).reshape(channels, length)
        for g in (grad_one, grad_two)
    ]
    return (
        grad_features,
        weights[: 3 * width],
        weights[3 * width :].T,
        short,
        grad_one,
        grad_two,
    )


def solution(mesh):
    columns, blocks_first, copied = P(None, AXES), P(AXES, None), P()
    return jax.shard_map(
        local,
        mesh=mesh,
        in_specs=(
            columns,
            blocks_first,
            columns,
            copied,
            copied,
            copied,
            blocks_first,
            blocks_first,
        ),
        out_specs=(columns, copied, copied, copied, blocks_first, blocks_first),
        check_vma=False,
    )
```

```python
import math

import jax
import jax.numpy as jnp
import numpy as np
from jax import lax
from jax.experimental import pallas as pl
from jax.experimental.pallas import tpu as pltpu
from jax.sharding import PartitionSpec as P

AXES = ("seq", "fft")
LANES = 128
bf16 = jnp.bfloat16
f32 = jnp.float32
PARAMS = pltpu.CompilerParams(vmem_limit_bytes=24 * 1024 * 1024)


def halves(table):
    high = table.astype(np.float32).astype(jnp.bfloat16)
    low = (table - high.astype(np.float64)).astype(np.float32).astype(jnp.bfloat16)
    return high, low


def make_tables(count, channels):
    length = count * LANES
    outer = np.arange(count, dtype=np.float64) + 0.25
    inner = np.arange(LANES, dtype=np.float64)
    angle = 2.0 * np.pi * outer[:, None] * outer[None, :] / count
    first = np.kron(np.concatenate([np.cos(angle), np.sin(angle)], axis=0), np.eye(channels))
    turn = 2.0 * np.pi * (inner[:, None] * inner[None, :] % LANES) / LANES
    cos, sin = np.cos(turn), np.sin(turn)
    second = np.block([[cos, -sin], [sin, cos]])
    packed = [half for t in (first, second) for half in halves(t)]
    twist = 2.0 * np.pi * outer[:, None] * (inner[None, :] - LANES / 4) / length
    twist = np.repeat(twist, channels, axis=0)
    twist = np.concatenate([np.cos(twist), -np.sin(twist)], axis=1).astype(np.float32)
    return np.concatenate(packed, axis=0), twist


def tables_of(table, twist):
    rows = twist.shape[0]
    at, found = 0, []
    for size in (2 * rows, 2 * LANES):
        pair = []
        for half in range(2):
            pair.append(table[at : at + size])
            at += size
        found.append(tuple(pair))
    first, second = found
    back = tuple(jnp.concatenate([t[:rows], t[rows:]], axis=1) for t in first)
    return first, back, second, (twist[:, :LANES], twist[:, LANES:])


def split(value):
    high = value.astype(bf16)
    low = (value - high.astype(f32)).astype(bf16)
    return high, low


def dot(left, right):
    return jnp.dot(left, right, preferred_element_type=f32)


def dot_pairs(left, right):
    return dot(left[0], right[0]) + dot(left[0], right[1]) + dot(left[1], right[0])


def forward(signals, first, second, twist):
    rows = signals[0].shape[0]
    stage = dot_pairs(first, split(jnp.concatenate(signals, axis=1)))
    parts = []
    for i in range(len(signals)):
        cos = stage[:rows, i * LANES : (i + 1) * LANES]
        sin = stage[rows:, i * LANES : (i + 1) * LANES]
        parts.append(
            jnp.concatenate(
                [cos * twist[0] + sin * twist[1], cos * twist[1] - sin * twist[0]], axis=1
            )
        )
    spec = dot_pairs(split(jnp.concatenate(parts, axis=0)), second)
    return [
        (spec[i * rows : (i + 1) * rows, :LANES], spec[i * rows : (i + 1) * rows, LANES:])
        for i in range(len(signals))
    ]


def backward(spectra, back, second, twist):
    rows = spectra[0][0].shape[0]
    stacked = jnp.concatenate([jnp.concatenate(pair, axis=1) for pair in spectra], axis=0)
    stage = dot_pairs(split(stacked), second)
    parts = []
    for i in range(len(spectra)):
        re = stage[i * rows : (i + 1) * rows, :LANES]
        im = stage[i * rows : (i + 1) * rows, LANES:]
        parts.append(
            jnp.concatenate(
                [re * twist[0] - im * twist[1], re * twist[1] + im * twist[0]], axis=0
            )
        )
    out = dot_pairs(back, split(jnp.concatenate(parts, axis=1)))
    return [out[:, i * LANES : (i + 1) * LANES] for i in range(len(spectra))]


def times(a, b):
    return (a[0] * b[0] - a[1] * b[1], -(a[0] * b[1] + a[1] * b[0]))


def conj_times(a, b):
    return (a[0] * b[0] + a[1] * b[1], a[1] * b[0] - a[0] * b[1])


def one_hot(order):
    size = order.shape[1]
    place = lax.broadcasted_iota(jnp.int32, (size, size), 0)
    return (place == order).astype(f32).astype(bf16)


def project_kernel(
    features_at,
    order_at,
    cotangent_at,
    w_in_at,
    w_out_at,
    streams_out,
    gather_out,
    features,
    order,
    cotangent,
    w_in,
    w_out,
    done,
):
    copies = [
        pltpu.make_async_copy(source, target, done.at[i])
        for i, (source, target) in enumerate(
            [
                (order_at, order),
                (features_at, features),
                (w_in_at, w_in),
                (cotangent_at, cotangent),
                (w_out_at, w_out),
            ]
        )
    ]
    for copy in copies:
        copy.start()
    width, row_count = features.shape
    copies[0].wait()
    copies[1].wait()
    seq_input = dot(features[...], one_hot(order[...])).astype(bf16)
    copies[2].wait()
    projected = dot(w_in[...], seq_input)
    copies[3].wait()
    copies[4].wait()
    out_grad = lax.dot_general(
        w_out[...], cotangent[...], (((0,), (0,)), ((), ())), preferred_element_type=f32
    )
    if len(streams_out.shape) == 3:
        blocks = streams_out.shape[0]
        parts = [projected[s * width : (s + 1) * width] for s in range(3)] + [out_grad]
        parts = [part.reshape(blocks, width // blocks, row_count) for part in parts]
        streams_out[...] = jnp.concatenate(parts, axis=1).astype(bf16)
    else:
        streams_out[: 3 * width] = projected.astype(bf16)
        streams_out[3 * width :] = out_grad.astype(bf16)
    own = jnp.concatenate([seq_input, cotangent[...]], axis=0)
    gather_out[...] = own


def read_signal(ref, rows):
    if ref.shape[1] == LANES:
        return ref[...]
    return jnp.concatenate(
        [ref[:, i * LANES : (i + 1) * LANES] for i in range(ref.shape[1] // LANES)], axis=0
    )


def write_signal(ref, value):
    if ref.shape[1] == LANES:
        ref[...] = value
        return
    channels = ref.shape[0]
    for i in range(ref.shape[1] // LANES):
        ref[:, i * LANES : (i + 1) * LANES] = value[i * channels : (i + 1) * channels]


def filter_kernel(
    length,
    filter_one,
    filter_two,
    table,
    twist,
    own,
    order,
    spec_one,
    spec_two,
    table_out,
    twist_out,
    own_out,
    order_out,
):
    rows = spec_one.shape[0]
    signals = [read_signal(filter_one, rows), read_signal(filter_two, rows)]
    first, _, second, turns = tables_of(table, twist)
    one, two = forward(signals, first, second, turns)
    spec_one[...] = jnp.concatenate(one, axis=1) * (1.0 / length)
    spec_two[...] = jnp.concatenate(two, axis=1) * (1.0 / length)
    table_out[...] = table[...]
    twist_out[...] = twist[...]
    own_out[...] = own[...]
    order_out[...] = order[...]


def shifted(value, steps, channels):
    if steps == 0:
        return value
    rows, lanes = value.shape
    lane = lax.broadcasted_iota(jnp.int32, value.shape, 1)
    row = lax.broadcasted_iota(jnp.int32, value.shape, 0)
    turned = pltpu.roll(value, steps % lanes, 1)
    if steps > 0:
        carried = jnp.where(row < channels, 0.0, pltpu.roll(turned, channels, 0))
        return jnp.where(lane < steps, carried, turned)
    carried = jnp.where(row >= rows - channels, 0.0, pltpu.roll(turned, rows - channels, 0))
    return jnp.where(lane >= lanes + steps, carried, turned)


def mix_kernel(
    channels,
    scale,
    streams,
    taps,
    spec_one,
    spec_two,
    table,
    twist,
    short_out,
    product_one,
    product_two,
    sent_out,
):
    rows = twist.shape[0]
    eight = taps.shape[0]
    first, back, second, twist = tables_of(table, twist)
    if streams.shape[0] == 4 and streams.shape[1] == rows:
        pieces = [streams[s].astype(f32) for s in range(4)]
    else:
        whole = streams[...].astype(f32)
        pieces = [
            whole[:, s * channels : (s + 1) * channels].reshape(rows, LANES) for s in range(4)
        ]
    out_grad = pieces[3]

    def tap(s, k):
        column = jnp.broadcast_to(taps[:, 3 * s + k : 3 * s + k + 1], (eight, LANES))
        column = jnp.broadcast_to(column[None], (rows // eight, eight, LANES))
        return column.reshape(rows, LANES)

    late = [[shifted(pieces[s], k, channels) for k in range(3)] for s in range(3)]
    value, gate_one, gate_two = [
        sum(tap(s, k) * late[s][k] for k in range(3)) for s in range(3)
    ]
    h_one = (spec_one[:, :LANES], spec_one[:, LANES:])
    h_two = (spec_two[:, :LANES], spec_two[:, LANES:])
    value_spec, second_spec = forward([value, out_grad * gate_two], first, second, twist)
    first_mix, grad_first_out = backward(
        [times(h_one, value_spec), conj_times(h_two, second_spec)],
        back,
        second,
        twist,
    )
    first_spec, grad_first_spec = forward(
        [gate_one * first_mix, gate_one * grad_first_out], first, second, twist
    )
    second_mix, grad_value = backward(
        [times(h_two, first_spec), conj_times(h_one, grad_first_spec)],
        back,
        second,
        twist,
    )
    product_one[...] = jnp.concatenate(conj_times(value_spec, grad_first_spec), axis=1)
    product_two[...] = jnp.concatenate(conj_times(first_spec, second_spec), axis=1)
    grads = [grad_value, grad_first_out * first_mix, out_grad * second_mix]
    sent = []
    lane = lax.broadcasted_iota(jnp.int32, (eight, LANES), 1)
    short = jnp.zeros((eight, LANES), f32)
    for s in range(3):
        sent.append(sum(tap(s, k) * shifted(grads[s], -k, channels) for k in range(3)))
        for k in range(3):
            folded = (grads[s] * late[s][k]).reshape(rows // eight, eight, LANES).sum(axis=0)
            total = jnp.sum(folded, axis=1, keepdims=True) * scale
            short = jnp.where(lane == 3 * s + k, total, short)
    sent.append(gate_two * second_mix)
    short_out[...] = short
    if sent_out.shape[0] == 4 and sent_out.shape[1] == rows:
        for s in range(4):
            sent_out[s] = sent[s].astype(bf16)
    else:
        parts = [part.reshape(rows // channels, channels, LANES) for part in sent]
        sent_out[...] = jnp.concatenate(parts, axis=1).astype(bf16)


def filter_grads_kernel(scale, product_one, product_two, table, twist, *refs):
    count = (len(refs) - 2) // 2
    passed, (grad_one, grad_two, *passed_out) = refs[:count], refs[count:]
    _, back, second, twist = tables_of(table, twist)
    spectra = [(ref[:, :LANES], ref[:, LANES:]) for ref in (product_one, product_two)]
    one, two = backward(spectra, back, second, twist)
    write_signal(grad_one, one * scale)
    write_signal(grad_two, two * scale)
    for source, target in zip(passed, passed_out):
        target[...] = source[...]


def member(at, k):
    return jnp.bitwise_xor(at, k)


def weights_kernel(channels, scale, lines, *refs):
    line, place, short, met, *pieces, partial_out, moved_out = refs
    plane, width = len(pieces), pieces[0].shape[0] // 2
    height = 4 * channels
    total = jnp.zeros((lines * height, 2 * width), f32)
    step = 2 if plane % 2 == 0 else 1
    for i in range(0, plane, step):
        left = jnp.concatenate(
            [
                jnp.concatenate(
                    [met[p * plane + member(place[0], i + j)] for p in range(lines)], axis=0
                )
                for j in range(step)
            ],
            axis=1,
        )
        right = jnp.concatenate([pieces[i + j][...] for j in range(step)], axis=1)
        total = total + lax.dot_general(
            left, right, (((1,), (1,)), ((), ())), preferred_element_type=f32
        )
    total = total * scale
    parts = []
    for k in range(lines):
        for h in range(width // LANES):
            low, high = h * LANES, (h + 1) * LANES
            base = k * height
            parts.append(total[base : base + 3 * channels, low:high])
            parts.append(total[base + 3 * channels : base + height, width + low : width + high])
    tail = jnp.concatenate([short[...]] * lines, axis=0)
    owner = lax.broadcasted_iota(jnp.int32, tail.shape, 0) // channels
    parts.append(jnp.where(owner == line[0], tail, 0.0))
    partial_out[...] = jnp.concatenate(parts, axis=0).astype(bf16)
    parts = [
        met[p * plane : (p + 1) * plane].astype(f32)[:, : 3 * channels] for p in range(lines)
    ]
    moved_out[...] = jnp.concatenate(parts, axis=1).astype(bf16)


def sum_kernel(*refs):
    *partials, out = refs
    out[...] = sum(part[...].astype(f32) for part in partials).astype(bf16)


def unorder(grad_projected, w_in, order):
    grad_seq = lax.dot_general(
        w_in, grad_projected, (((0,), (0,)), ((), ())), preferred_element_type=f32
    ).astype(bf16)
    return lax.dot_general(
        grad_seq, one_hot(order), (((1,), (1,)), ((), ())), preferred_element_type=f32
    ).astype(bf16)


def moved_kernel(channels, lines, back, w_in, order, features_out):
    plane = back.shape[0]
    whole = back[...].astype(f32)
    parts = []
    for s in range(3):
        for line in range(lines):
            start = (3 * line + s) * channels
            parts.append(whole[:, start : start + channels].reshape(plane * channels, LANES))
    grad_projected = jnp.concatenate(parts, axis=0).astype(bf16)
    features_out[...] = unorder(grad_projected, w_in[...], order[...])


def finish_kernel(channels, lines, place, *refs):
    *pieces, w_in_out, w_out_out, short_out, out_rows, short_rows = refs
    width = w_out_out.shape[0]
    share = width // lines
    height = 4 * channels
    size = height * (width // LANES)
    for k, piece in enumerate(pieces):
        rows = piece[...].astype(f32)
        for i in range(lines):
            first = pl.multiple_of(i * share + member(place[0], k) * channels, channels)
            for h in range(width // LANES):
                low, high = h * LANES, (h + 1) * LANES
                base = i * size + h * height
                for s in range(3):
                    spot = pl.ds(pl.multiple_of(s * width + first, channels), channels)
                    start = base + s * channels
                    w_in_out[spot, low:high] = rows[start : start + channels]
                start = base + 3 * channels
                out_rows[pl.ds(first, channels), low:high] = rows[start : start + channels]
            start = lines * size + i * channels
            short_rows[pl.ds(first, channels), :] = rows[start : start + channels]
    w_out_out[...] = out_rows[...].T
    short = short_rows[...].T
    for s in range(3):
        short_out[:, s * width : (s + 1) * width] = short[3 * s : 3 * s + 3, :]


def features_kernel(moved, w_in, order, features_out):
    features_out[...] = unorder(moved[...], w_in[...], order[...])


def swapped(value, axis, count, distance):
    return lax.ppermute(value, axis, [(i, i ^ distance) for i in range(count)])


def shape(dims, dtype=f32):
    return jax.ShapeDtypeStruct(dims, dtype)


def local(features, sink_order, cotangent, w_in, short_taps, w_out, filter_one, filter_two):
    width, row_count = features.shape
    lines, plane = lax.axis_size("seq"), lax.axis_size("fft")
    blocks = lines * plane
    channels, length = filter_one.shape
    rows = channels * blocks
    scale = 1.0 / math.sqrt(length)
    powers = all(n > 1 and n & (n - 1) == 0 for n in (lines, plane))
    whole = channels % 8 == 0 and powers
    table, twist = make_tables(blocks, channels)
    eight = channels if whole else 8
    mine = lax.axis_index(AXES)

    def call(kernel, outs, *args, **options):
        return pl.pallas_call(kernel, out_shape=outs, compiler_params=PARAMS, **options)(*args)

    dims = (blocks, 4 * channels, LANES) if whole else (4 * width, LANES)
    streams, own = pl.pallas_call(
        project_kernel,
        out_shape=(shape(dims, bf16), shape((2 * width, row_count), bf16)),
        in_specs=[pl.BlockSpec(memory_space=pl.ANY)] * 5,
        scratch_shapes=[
            pltpu.VMEM(a.shape, a.dtype)
            for a in (features, sink_order, cotangent, w_in, w_out)
        ]
        + [pltpu.SemaphoreType.DMA((5,))],
        compiler_params=pltpu.CompilerParams(vmem_limit_bytes=60 * 1024 * 1024),
    )(features, sink_order, cotangent, w_in, w_out)
    if not whole:
        streams = streams.reshape(4, blocks, channels, LANES).transpose(1, 0, 2, 3)
        streams = streams.reshape(blocks, 4 * channels, LANES)
    arrived = lax.all_to_all(streams, AXES, split_axis=0, concat_axis=0, tiled=True)
    taps = lax.dynamic_slice_in_dim(short_taps.reshape(3, width, 3), mine * channels, channels, 1)
    taps = taps.transpose(1, 0, 2).reshape(channels, 9)
    if not whole:
        taps = jnp.tile(taps, (8 // channels, 1))
        arrived = arrived.reshape(blocks, 4, channels, LANES).transpose(1, 0, 2, 3)
        arrived = arrived.reshape(4, rows, LANES)
        filter_one, filter_two = [
            h.reshape(channels, blocks, LANES).transpose(1, 0, 2).reshape(rows, LANES)
            for h in (filter_one, filter_two)
        ]
    spec = shape((rows, 2 * LANES))
    spec_one, spec_two, table, twist, own, order = call(
        lambda *refs: filter_kernel(length, *refs),
        (
            spec,
            spec,
            shape(table.shape, bf16),
            shape(twist.shape),
            shape(own.shape, bf16),
            shape(sink_order.shape, jnp.int32),
        ),
        filter_one,
        filter_two,
        table,
        twist,
        own,
        sink_order,
    )
    line = lax.axis_index("seq").astype(jnp.int32).reshape(1)
    place = lax.axis_index("fft").astype(jnp.int32).reshape(1)
    scalar = pl.BlockSpec(memory_space=pltpu.SMEM)
    held = pl.BlockSpec(memory_space=pltpu.VMEM)
    dims = (blocks, 4 * channels, LANES) if whole else (4, rows, LANES)
    short, product_one, product_two, sent = call(
        lambda *refs: mix_kernel(channels, scale, *refs),
        (shape((eight, LANES)), spec, spec, shape(dims, bf16)),
        arrived,
        taps,
        spec_one,
        spec_two,
        table,
        twist,
    )
    passed = [short]
    if whole:
        met = lax.all_to_all(sent, "seq", split_axis=0, concat_axis=0, tiled=True)
        passed += [swapped(own, "fft", plane, k) for k in range(2, plane, 2)]
    grad_one, grad_two, short, *passed = call(
        lambda *refs: filter_grads_kernel(scale / length, *refs),
        (
            shape(filter_one.shape),
            shape(filter_two.shape),
            *[shape(a.shape, a.dtype) for a in passed],
        ),
        product_one,
        product_two,
        table,
        twist,
        *passed,
    )
    height = channels * 4 * (width // LANES)
    if whole:
        pieces = [a for p in (own, *passed) for a in (p, swapped(p, "fft", plane, 1))]
        size = lines * height + lines * channels
        partial, moved = call(
            lambda *refs: weights_kernel(channels, scale, lines, *refs),
            (
                shape((size, LANES), bf16),
                shape((plane, 3 * lines * channels, LANES), bf16),
            ),
            line,
            place,
            short,
            met,
            *pieces,
            in_specs=[scalar] * 2 + [held] * (2 + plane),
        )
        partials = [partial] + [swapped(partial, "seq", lines, k) for k in range(1, lines)]
        back = lax.all_to_all(moved, "fft", split_axis=0, concat_axis=0, tiled=True)
        rows_sum = call(sum_kernel, shape((size, LANES), bf16), *partials)
        grad_features = call(
            lambda *refs: moved_kernel(channels, lines, *refs),
            shape(features.shape, bf16),
            back,
            w_in,
            order,
        )
        spread = [rows_sum] + [swapped(rows_sum, "fft", plane, k) for k in range(2, plane, 2)]
        spread = [a for piece in spread for a in (piece, swapped(piece, "fft", plane, 1))]
        grad_w_in, grad_w_out, short = call(
            lambda *refs: finish_kernel(channels, lines, *refs),
            (shape((3 * width, width)), shape((width, width)), shape((3, 3 * width))),
            place,
            *spread,
            in_specs=[scalar] + [held] * plane,
            scratch_shapes=[pltpu.VMEM((width, width), f32), pltpu.VMEM((width, LANES), f32)],
        )
        return (grad_features, grad_w_in, grad_w_out, short.T, grad_one, grad_two)
    gathered = lax.all_gather(own, AXES, axis=0, tiled=False)
    sent = sent.reshape(4, blocks, channels, LANES)
    grad_in = jnp.einsum(
        "sbcp,bwp->scw", sent[:3], gathered[:, :width], preferred_element_type=f32
    )
    grad_out = jnp.einsum(
        "bcp,bwp->cw", sent[3], gathered[:, width:], preferred_element_type=f32
    )
    own = jnp.concatenate([grad_in, grad_out[None]]) * scale
    own = own.reshape(height, LANES)
    short = short.reshape(8 // channels, channels, LANES).sum(axis=0)
    own = jnp.concatenate([own, short]).astype(bf16)
    moved = sent[:3].transpose(1, 0, 2, 3).reshape(blocks, 3 * channels, LANES)
    own = jnp.broadcast_to(own[None], (blocks,) + own.shape)
    packed = jnp.concatenate([moved, own], axis=1)
    back = lax.all_to_all(packed, AXES, split_axis=0, concat_axis=0, tiled=True)
    moved = back[:, : 3 * channels].reshape(blocks, 3, channels, LANES)
    moved = moved.transpose(1, 0, 2, 3).reshape(3 * width, LANES)
    weights = back[:, 3 * channels : 3 * channels + height].astype(f32)
    weights = weights.reshape(blocks, 4, channels, width).transpose(1, 0, 2, 3)
    weights = weights.reshape(4 * width, width)
    short = back[:, 3 * channels + height :, :9].astype(f32).reshape(width, 3, 3)
    short = short.transpose(1, 0, 2).reshape(3 * width, 3)
    grad_features = call(
        features_kernel, shape(features.shape, bf16), moved, w_in, sink_order
    )
    grad_one, grad_two = [
        g.reshape(blocks, channels, LANES).transpose(1, 0, 2).reshape(channels, length)
        for g in (grad_one, grad_two)
    ]
    return (
        grad_features,
        weights[: 3 * width],
        weights[3 * width :].T,
        short,
        grad_one,
        grad_two,
    )


def solution(mesh):
    columns, blocks_first, copied = P(None, AXES), P(AXES, None), P()
    return jax.shard_map(
        local,
        mesh=mesh,
        in_specs=(
            columns,
            blocks_first,
            columns,
            copied,
            copied,
            copied,
            blocks_first,
            blocks_first,
        ),
        out_specs=(columns, copied, copied, copied, blocks_first, blocks_first),
        check_vma=False,
    )
```

```python
import math

import jax
import jax.numpy as jnp
import numpy as np
from jax import lax
from jax.experimental import pallas as pl
from jax.experimental.pallas import tpu as pltpu
from jax.sharding import PartitionSpec as P

AXES = ("seq", "fft")
LANES = 128
bf16 = jnp.bfloat16
f32 = jnp.float32
PARAMS = pltpu.CompilerParams(vmem_limit_bytes=24 * 1024 * 1024)


def halves(table):
    high = table.astype(np.float32).astype(jnp.bfloat16)
    low = (table - high.astype(np.float64)).astype(np.float32).astype(jnp.bfloat16)
    return high, low


def make_tables(count, channels):
    length = count * LANES
    outer = np.arange(count, dtype=np.float64) + 0.25
    inner = np.arange(LANES, dtype=np.float64)
    angle = 2.0 * np.pi * outer[:, None] * outer[None, :] / count
    first = np.kron(np.concatenate([np.cos(angle), np.sin(angle)], axis=0), np.eye(channels))
    turn = 2.0 * np.pi * (inner[:, None] * inner[None, :] % LANES) / LANES
    cos, sin = np.cos(turn), np.sin(turn)
    second = np.block([[cos, -sin], [sin, cos]])
    packed = [half for t in (first, second) for half in halves(t)]
    twist = 2.0 * np.pi * outer[:, None] * (inner[None, :] - LANES / 4) / length
    twist = np.repeat(twist, channels, axis=0)
    twist = np.concatenate([np.cos(twist), -np.sin(twist)], axis=1).astype(np.float32)
    return np.concatenate(packed, axis=0), twist


def tables_of(table, twist):
    rows = twist.shape[0]
    at, found = 0, []
    for size in (2 * rows, 2 * LANES):
        pair = []
        for half in range(2):
            pair.append(table[at : at + size])
            at += size
        found.append(tuple(pair))
    first, second = found
    back = tuple(jnp.concatenate([t[:rows], t[rows:]], axis=1) for t in first)
    return first, back, second, (twist[:, :LANES], twist[:, LANES:])


def split(value):
    high = value.astype(bf16)
    low = (value - high.astype(f32)).astype(bf16)
    return high, low


def dot(left, right):
    return jnp.dot(left, right, preferred_element_type=f32)


def dot_pairs(left, right):
    return dot(left[0], right[0]) + dot(left[0], right[1]) + dot(left[1], right[0])


def forward(signals, first, second, twist):
    rows = signals[0].shape[0]
    stage = dot_pairs(first, split(jnp.concatenate(signals, axis=1)))
    parts = []
    for i in range(len(signals)):
        cos = stage[:rows, i * LANES : (i + 1) * LANES]
        sin = stage[rows:, i * LANES : (i + 1) * LANES]
        parts.append(
            jnp.concatenate(
                [cos * twist[0] + sin * twist[1], cos * twist[1] - sin * twist[0]], axis=1
            )
        )
    spec = dot_pairs(split(jnp.concatenate(parts, axis=0)), second)
    return [
        (spec[i * rows : (i + 1) * rows, :LANES], spec[i * rows : (i + 1) * rows, LANES:])
        for i in range(len(signals))
    ]


def backward(spectra, back, second, twist):
    rows = spectra[0][0].shape[0]
    stacked = jnp.concatenate([jnp.concatenate(pair, axis=1) for pair in spectra], axis=0)
    stage = dot_pairs(split(stacked), second)
    parts = []
    for i in range(len(spectra)):
        re = stage[i * rows : (i + 1) * rows, :LANES]
        im = stage[i * rows : (i + 1) * rows, LANES:]
        parts.append(
            jnp.concatenate(
                [re * twist[0] - im * twist[1], re * twist[1] + im * twist[0]], axis=0
            )
        )
    out = dot_pairs(back, split(jnp.concatenate(parts, axis=1)))
    return [out[:, i * LANES : (i + 1) * LANES] for i in range(len(spectra))]


def times(a, b):
    return (a[0] * b[0] - a[1] * b[1], -(a[0] * b[1] + a[1] * b[0]))


def conj_times(a, b):
    return (a[0] * b[0] + a[1] * b[1], a[1] * b[0] - a[0] * b[1])


def one_hot(order):
    size = order.shape[1]
    place = lax.broadcasted_iota(jnp.int32, (size, size), 0)
    return (place == order).astype(f32).astype(bf16)


def project_kernel(
    features_at,
    order_at,
    cotangent_at,
    w_in_at,
    w_out_at,
    streams_out,
    gather_out,
    features,
    order,
    cotangent,
    w_in,
    w_out,
    done,
):
    copies = [
        pltpu.make_async_copy(source, target, done.at[i])
        for i, (source, target) in enumerate(
            [
                (order_at, order),
                (features_at, features),
                (w_in_at, w_in),
                (cotangent_at, cotangent),
                (w_out_at, w_out),
            ]
        )
    ]
    for copy in copies:
        copy.start()
    width, row_count = features.shape
    copies[0].wait()
    copies[1].wait()
    seq_input = dot(features[...], one_hot(order[...])).astype(bf16)
    copies[2].wait()
    projected = dot(w_in[...], seq_input)
    copies[3].wait()
    copies[4].wait()
    out_grad = lax.dot_general(
        w_out[...], cotangent[...], (((0,), (0,)), ((), ())), preferred_element_type=f32
    )
    if len(streams_out.shape) == 3:
        blocks = streams_out.shape[0]
        parts = [projected[s * width : (s + 1) * width] for s in range(3)] + [out_grad]
        parts = [part.reshape(blocks, width // blocks, row_count) for part in parts]
        streams_out[...] = jnp.concatenate(parts, axis=1).astype(bf16)
    else:
        streams_out[: 3 * width] = projected.astype(bf16)
        streams_out[3 * width :] = out_grad.astype(bf16)
    own = jnp.concatenate([seq_input, cotangent[...]], axis=0)
    gather_out[...] = own


def read_signal(ref, rows):
    if ref.shape[1] == LANES:
        return ref[...]
    return jnp.concatenate(
        [ref[:, i * LANES : (i + 1) * LANES] for i in range(ref.shape[1] // LANES)], axis=0
    )


def write_signal(ref, value):
    if ref.shape[1] == LANES:
        ref[...] = value
        return
    channels = ref.shape[0]
    for i in range(ref.shape[1] // LANES):
        ref[:, i * LANES : (i + 1) * LANES] = value[i * channels : (i + 1) * channels]


def filter_kernel(
    length,
    filter_one,
    filter_two,
    table,
    twist,
    order,
    spec_one,
    spec_two,
    table_out,
    twist_out,
    order_out,
):
    rows = spec_one.shape[0]
    signals = [read_signal(filter_one, rows), read_signal(filter_two, rows)]
    first, _, second, turns = tables_of(table, twist)
    one, two = forward(signals, first, second, turns)
    spec_one[...] = jnp.concatenate(one, axis=1) * (1.0 / length)
    spec_two[...] = jnp.concatenate(two, axis=1) * (1.0 / length)
    table_out[...] = table[...]
    twist_out[...] = twist[...]
    order_out[...] = order[...]


def pass_kernel(after, *refs):
    count = len(refs) // 2
    for source, target in zip(refs[:count], refs[count:]):
        target[...] = source[...]


def shifted(value, steps, channels):
    if steps == 0:
        return value
    rows, lanes = value.shape
    lane = lax.broadcasted_iota(jnp.int32, value.shape, 1)
    row = lax.broadcasted_iota(jnp.int32, value.shape, 0)
    turned = pltpu.roll(value, steps % lanes, 1)
    if steps > 0:
        carried = jnp.where(row < channels, 0.0, pltpu.roll(turned, channels, 0))
        return jnp.where(lane < steps, carried, turned)
    carried = jnp.where(row >= rows - channels, 0.0, pltpu.roll(turned, rows - channels, 0))
    return jnp.where(lane >= lanes + steps, carried, turned)


def mix_kernel(
    channels,
    scale,
    streams,
    taps,
    spec_one,
    spec_two,
    table,
    twist,
    line,
    short_out,
    product_one,
    product_two,
    *sent_out,
):
    rows = twist.shape[0]
    eight = taps.shape[0]
    first, back, second, twist = tables_of(table, twist)
    if streams.shape[0] == 4 and streams.shape[1] == rows:
        pieces = [streams[s].astype(f32) for s in range(4)]
    else:
        whole = streams[...].astype(f32)
        pieces = [
            whole[:, s * channels : (s + 1) * channels].reshape(rows, LANES) for s in range(4)
        ]
    out_grad = pieces[3]

    def tap(s, k):
        column = jnp.broadcast_to(taps[:, 3 * s + k : 3 * s + k + 1], (eight, LANES))
        column = jnp.broadcast_to(column[None], (rows // eight, eight, LANES))
        return column.reshape(rows, LANES)

    late = [[shifted(pieces[s], k, channels) for k in range(3)] for s in range(3)]
    value, gate_one, gate_two = [
        sum(tap(s, k) * late[s][k] for k in range(3)) for s in range(3)
    ]
    h_one = (spec_one[:, :LANES], spec_one[:, LANES:])
    h_two = (spec_two[:, :LANES], spec_two[:, LANES:])
    value_spec, second_spec = forward([value, out_grad * gate_two], first, second, twist)
    first_mix, grad_first_out = backward(
        [times(h_one, value_spec), conj_times(h_two, second_spec)],
        back,
        second,
        twist,
    )
    first_spec, grad_first_spec = forward(
        [gate_one * first_mix, gate_one * grad_first_out], first, second, twist
    )
    second_mix, grad_value = backward(
        [times(h_two, first_spec), conj_times(h_one, grad_first_spec)],
        back,
        second,
        twist,
    )
    product_one[...] = jnp.concatenate(conj_times(value_spec, grad_first_spec), axis=1)
    product_two[...] = jnp.concatenate(conj_times(first_spec, second_spec), axis=1)
    grads = [grad_value, grad_first_out * first_mix, out_grad * second_mix]
    sent = []
    lane = lax.broadcasted_iota(jnp.int32, (eight, LANES), 1)
    short = jnp.zeros((eight, LANES), f32)
    for s in range(3):
        sent.append(sum(tap(s, k) * shifted(grads[s], -k, channels) for k in range(3)))
        for k in range(3):
            folded = (grads[s] * late[s][k]).reshape(rows // eight, eight, LANES).sum(axis=0)
            total = jnp.sum(folded, axis=1, keepdims=True) * scale
            short = jnp.where(lane == 3 * s + k, total, short)
    sent.append(gate_two * second_mix)
    short_out[...] = short
    if len(sent_out) == 1:
        for s in range(4):
            sent_out[0][s] = sent[s].astype(bf16)
        return
    parts = [part.reshape(rows // channels, channels, LANES) for part in sent]
    packed = jnp.concatenate(parts, axis=1).astype(bf16)
    *sent_out, store = sent_out
    lines, plane = store.shape[:2]
    for i in range(lines):
        store[i] = packed[i * plane : (i + 1) * plane]
    for step in range(lines):
        sent_out[step][...] = store[lax.rem(line[0] + step, lines)]


def filter_grads_kernel(
    scale, product_one, product_two, table, twist, short, grad_one, grad_two, short_out
):
    _, back, second, twist = tables_of(table, twist)
    spectra = [(ref[:, :LANES], ref[:, LANES:]) for ref in (product_one, product_two)]
    one, two = backward(spectra, back, second, twist)
    write_signal(grad_one, one * scale)
    write_signal(grad_two, two * scale)
    short_out[...] = short[...]


def member(at, k):
    return jnp.bitwise_xor(at, k)


def weights_kernel(channels, scale, lines, *refs):
    line, place, short, *refs, partial_out, moved_out = refs
    met, pieces = refs[:lines], refs[lines:]
    plane, width = len(pieces), pieces[0].shape[0] // 2
    height = 4 * channels
    total = jnp.zeros((lines * height, 2 * width), f32)
    step = 2 if plane % 2 == 0 else 1
    for i in range(0, plane, step):
        left = jnp.concatenate(
            [
                jnp.concatenate([m[member(place[0], i + j)] for m in met], axis=0)
                for j in range(step)
            ],
            axis=1,
        )
        right = jnp.concatenate([pieces[i + j][...] for j in range(step)], axis=1)
        total = total + lax.dot_general(
            left, right, (((1,), (1,)), ((), ())), preferred_element_type=f32
        )
    total = total * scale
    size = height * (width // LANES)
    for k in range(lines):
        parts = []
        for h in range(width // LANES):
            low, high = h * LANES, (h + 1) * LANES
            base = k * height
            parts.append(total[base : base + 3 * channels, low:high])
            parts.append(total[base + 3 * channels : base + height, width + low : width + high])
        owner = lax.rem(line[0] + lines - k, lines)
        spot = pl.ds(pl.multiple_of(owner * size, size), size)
        partial_out[spot] = jnp.concatenate(parts, axis=0).astype(bf16)
    tail = jnp.concatenate([short[...]] * lines, axis=0)
    owner = lax.broadcasted_iota(jnp.int32, tail.shape, 0) // channels
    partial_out[lines * size :] = jnp.where(owner == line[0], tail, 0.0).astype(bf16)
    parts = [m[...].astype(f32)[:, : 3 * channels] for m in met]
    moved_out[...] = jnp.concatenate(parts, axis=1).astype(bf16)


def sum_kernel(*refs):
    *partials, out = refs
    out[...] = sum(part[...].astype(f32) for part in partials).astype(bf16)


def unorder(grad_projected, w_in, order):
    grad_seq = lax.dot_general(
        w_in, grad_projected, (((0,), (0,)), ((), ())), preferred_element_type=f32
    ).astype(bf16)
    return lax.dot_general(
        grad_seq, one_hot(order), (((1,), (1,)), ((), ())), preferred_element_type=f32
    ).astype(bf16)


def moved_kernel(channels, lines, line, back, w_in, order, features_out, store):
    plane, width = back.shape[0], w_in.shape[1]
    share = plane * channels
    whole = back[...].astype(f32)
    for k in range(lines):
        owner = lax.rem(line[0] + lines - k, lines)
        for s in range(3):
            start = (3 * k + s) * channels
            spot = pl.ds(pl.multiple_of(s * width + owner * share, share), share)
            store[spot] = whole[:, start : start + channels].reshape(share, LANES)
    features_out[...] = unorder(store[...].astype(bf16), w_in[...], order[...])


def finish_kernel(channels, lines, place, *refs):
    *pieces, w_in_out, w_out_out, short_out, out_rows, short_rows = refs
    width = w_out_out.shape[0]
    share = width // lines
    height = 4 * channels
    size = height * (width // LANES)
    for k, piece in enumerate(pieces):
        rows = piece[...].astype(f32)
        for i in range(lines):
            first = pl.multiple_of(i * share + member(place[0], k) * channels, channels)
            for h in range(width // LANES):
                low, high = h * LANES, (h + 1) * LANES
                base = i * size + h * height
                for s in range(3):
                    spot = pl.ds(pl.multiple_of(s * width + first, channels), channels)
                    start = base + s * channels
                    w_in_out[spot, low:high] = rows[start : start + channels]
                start = base + 3 * channels
                out_rows[pl.ds(first, channels), low:high] = rows[start : start + channels]
            start = lines * size + i * channels
            short_rows[pl.ds(first, channels), :] = rows[start : start + channels]
    w_out_out[...] = out_rows[...].T
    short = short_rows[...].T
    for s in range(3):
        short_out[:, s * width : (s + 1) * width] = short[3 * s : 3 * s + 3, :]


def features_kernel(moved, w_in, order, features_out):
    features_out[...] = unorder(moved[...], w_in[...], order[...])


def swapped(value, plane, distance):
    return lax.ppermute(value, "fft", [(i, i ^ distance) for i in range(plane)])


def spread(value, plane):
    pieces = [value if k == 0 else swapped(value, plane, k) for k in range(0, plane, 2)]
    return [piece for own in pieces for piece in (own, swapped(own, plane, 1))]


def shape(dims, dtype=f32):
    return jax.ShapeDtypeStruct(dims, dtype)


def local(features, sink_order, cotangent, w_in, short_taps, w_out, filter_one, filter_two):
    width, row_count = features.shape
    lines, plane = lax.axis_size("seq"), lax.axis_size("fft")
    blocks = lines * plane
    channels, length = filter_one.shape
    rows = channels * blocks
    scale = 1.0 / math.sqrt(length)
    whole = channels % 8 == 0 and plane % 2 == 0 and plane & (plane - 1) == 0
    table, twist = make_tables(blocks, channels)
    eight = channels if whole else 8
    mine = lax.axis_index(AXES)

    def call(kernel, outs, *args, **options):
        return pl.pallas_call(kernel, out_shape=outs, compiler_params=PARAMS, **options)(*args)

    dims = (blocks, 4 * channels, LANES) if whole else (4 * width, LANES)
    streams, own = pl.pallas_call(
        project_kernel,
        out_shape=(shape(dims, bf16), shape((2 * width, row_count), bf16)),
        in_specs=[pl.BlockSpec(memory_space=pl.ANY)] * 5,
        scratch_shapes=[
            pltpu.VMEM(a.shape, a.dtype)
            for a in (features, sink_order, cotangent, w_in, w_out)
        ]
        + [pltpu.SemaphoreType.DMA((5,))],
        compiler_params=pltpu.CompilerParams(vmem_limit_bytes=60 * 1024 * 1024),
    )(features, sink_order, cotangent, w_in, w_out)
    if not whole:
        streams = streams.reshape(4, blocks, channels, LANES).transpose(1, 0, 2, 3)
        streams = streams.reshape(blocks, 4 * channels, LANES)
    arrived = lax.all_to_all(streams, AXES, split_axis=0, concat_axis=0, tiled=True)
    taps = lax.dynamic_slice_in_dim(short_taps.reshape(3, width, 3), mine * channels, channels, 1)
    taps = taps.transpose(1, 0, 2).reshape(channels, 9)
    if not whole:
        taps = jnp.tile(taps, (8 // channels, 1))
        arrived = arrived.reshape(blocks, 4, channels, LANES).transpose(1, 0, 2, 3)
        arrived = arrived.reshape(4, rows, LANES)
        filter_one, filter_two = [
            h.reshape(channels, blocks, LANES).transpose(1, 0, 2).reshape(rows, LANES)
            for h in (filter_one, filter_two)
        ]
    spec = shape((rows, 2 * LANES))
    spec_one, spec_two, table, twist, order = call(
        lambda *refs: filter_kernel(length, *refs),
        (
            spec,
            spec,
            shape(table.shape, bf16),
            shape(twist.shape),
            shape(sink_order.shape, jnp.int32),
        ),
        filter_one,
        filter_two,
        table,
        twist,
        sink_order,
    )
    if whole:
        pieces = [swapped(own, plane, k) for k in range(2, plane, 2)]
        pieces = call(pass_kernel, [shape(own.shape, bf16)] * len(pieces), order, *pieces)
    line = lax.axis_index("seq").astype(jnp.int32).reshape(1)
    place = lax.axis_index("fft").astype(jnp.int32).reshape(1)
    scalar = pl.BlockSpec(memory_space=pltpu.SMEM)
    held = pl.BlockSpec(memory_space=pltpu.VMEM)
    chunk = (plane, 4 * channels, LANES)
    dims = [shape(chunk, bf16)] * lines if whole else [shape((4, rows, LANES), bf16)]
    short, product_one, product_two, *sent = call(
        lambda *refs: mix_kernel(channels, scale, *refs),
        (shape((eight, LANES)), spec, spec, *dims),
        arrived,
        taps,
        spec_one,
        spec_two,
        table,
        twist,
        line,
        in_specs=[held] * 6 + [scalar],
        scratch_shapes=[pltpu.VMEM((lines, *chunk), bf16)] if whole else [],
    )
    grad_one, grad_two, short = call(
        lambda *refs: filter_grads_kernel(scale / length, *refs),
        (shape(filter_one.shape), shape(filter_two.shape), shape(short.shape)),
        product_one,
        product_two,
        table,
        twist,
        short,
    )
    height = channels * 4 * (width // LANES)
    if whole:
        def ahead(value, steps):
            pairs = [(i, (i + steps) % lines) for i in range(lines)]
            return lax.ppermute(value, "seq", pairs)

        met = [sent[0]] + [ahead(sent[k], k) for k in range(1, lines)]
        size = lines * height + lines * channels
        partial, moved = call(
            lambda *refs: weights_kernel(channels, scale, lines, *refs),
            (
                shape((size, LANES), bf16),
                shape((plane, 3 * lines * channels, LANES), bf16),
            ),
            line,
            place,
            short,
            *met,
            *[a for p in (own, *pieces) for a in (p, swapped(p, plane, 1))],
            in_specs=[scalar] * 2 + [held] * (1 + lines + plane),
        )
        partials = [partial] + [ahead(partial, k) for k in range(1, lines)]
        back = lax.all_to_all(moved, "fft", split_axis=0, concat_axis=0, tiled=True)
        grad_features = call(
            lambda *refs: moved_kernel(channels, lines, *refs),
            shape(features.shape, bf16),
            line,
            back,
            w_in,
            order,
            in_specs=[scalar] + [held] * 3,
            scratch_shapes=[pltpu.VMEM((3 * width, LANES), f32)],
        )
        rows_sum = call(sum_kernel, shape((size, LANES), bf16), *partials)
        grad_w_in, grad_w_out, short = call(
            lambda *refs: finish_kernel(channels, lines, *refs),
            (shape((3 * width, width)), shape((width, width)), shape((3, 3 * width))),
            place,
            *spread(rows_sum, plane),
            in_specs=[scalar] + [held] * plane,
            scratch_shapes=[pltpu.VMEM((width, width), f32), pltpu.VMEM((width, LANES), f32)],
        )
        return (grad_features, grad_w_in, grad_w_out, short.T, grad_one, grad_two)
    gathered = lax.all_gather(own, AXES, axis=0, tiled=False)
    sent = sent[0]
    sent = sent.reshape(4, blocks, channels, LANES)
    grad_in = jnp.einsum(
        "sbcp,bwp->scw", sent[:3], gathered[:, :width], preferred_element_type=f32
    )
    grad_out = jnp.einsum(
        "bcp,bwp->cw", sent[3], gathered[:, width:], preferred_element_type=f32
    )
    own = jnp.concatenate([grad_in, grad_out[None]]) * scale
    own = own.reshape(height, LANES)
    short = short.reshape(8 // channels, channels, LANES).sum(axis=0)
    own = jnp.concatenate([own, short]).astype(bf16)
    moved = sent[:3].transpose(1, 0, 2, 3).reshape(blocks, 3 * channels, LANES)
    own = jnp.broadcast_to(own[None], (blocks,) + own.shape)
    packed = jnp.concatenate([moved, own], axis=1)
    back = lax.all_to_all(packed, AXES, split_axis=0, concat_axis=0, tiled=True)
    moved = back[:, : 3 * channels].reshape(blocks, 3, channels, LANES)
    moved = moved.transpose(1, 0, 2, 3).reshape(3 * width, LANES)
    weights = back[:, 3 * channels : 3 * channels + height].astype(f32)
    weights = weights.reshape(blocks, 4, channels, width).transpose(1, 0, 2, 3)
    weights = weights.reshape(4 * width, width)
    short = back[:, 3 * channels + height :, :9].astype(f32).reshape(width, 3, 3)
    short = short.transpose(1, 0, 2).reshape(3 * width, 3)
    grad_features = call(
        features_kernel, shape(features.shape, bf16), moved, w_in, sink_order
    )
    grad_one, grad_two = [
        g.reshape(blocks, channels, LANES).transpose(1, 0, 2).reshape(channels, length)
        for g in (grad_one, grad_two)
    ]
    return (
        grad_features,
        weights[: 3 * width],
        weights[3 * width :].T,
        short,
        grad_one,
        grad_two,
    )


def solution(mesh):
    columns, blocks_first, copied = P(None, AXES), P(AXES, None), P()
    return jax.shard_map(
        local,
        mesh=mesh,
        in_specs=(
            columns,
            blocks_first,
            columns,
            copied,
            copied,
            copied,
            blocks_first,
            blocks_first,
        ),
        out_specs=(columns, copied, copied, copied, blocks_first, blocks_first),
        check_vma=False,
    )
```

```python
import math

import jax
import jax.numpy as jnp
import numpy as np
from jax import lax
from jax.experimental import pallas as pl
from jax.experimental.pallas import tpu as pltpu
from jax.sharding import PartitionSpec as P

AXES = ("seq", "fft")
LANES = 128
bf16 = jnp.bfloat16
f32 = jnp.float32
PARAMS = pltpu.CompilerParams(vmem_limit_bytes=24 * 1024 * 1024)


def halves(table):
    high = table.astype(np.float32).astype(jnp.bfloat16)
    low = (table - high.astype(np.float64)).astype(np.float32).astype(jnp.bfloat16)
    return high, low


def make_tables(count, channels):
    length = count * LANES
    outer = np.arange(count, dtype=np.float64) + 0.25
    inner = np.arange(LANES, dtype=np.float64)
    angle = 2.0 * np.pi * outer[:, None] * outer[None, :] / count
    first = np.kron(np.concatenate([np.cos(angle), np.sin(angle)], axis=0), np.eye(channels))
    turn = 2.0 * np.pi * (inner[:, None] * inner[None, :] % LANES) / LANES
    cos, sin = np.cos(turn), np.sin(turn)
    second = np.block([[cos, -sin], [sin, cos]])
    packed = [half for t in (first, second) for half in halves(t)]
    twist = 2.0 * np.pi * outer[:, None] * (inner[None, :] - LANES / 4) / length
    twist = np.repeat(twist, channels, axis=0)
    twist = np.concatenate([np.cos(twist), -np.sin(twist)], axis=1).astype(np.float32)
    return np.concatenate(packed, axis=0), twist


def tables_of(table, twist):
    rows = twist.shape[0]
    at, found = 0, []
    for size in (2 * rows, 2 * LANES):
        pair = []
        for half in range(2):
            pair.append(table[at : at + size])
            at += size
        found.append(tuple(pair))
    first, second = found
    back = tuple(jnp.concatenate([t[:rows], t[rows:]], axis=1) for t in first)
    return first, back, second, (twist[:, :LANES], twist[:, LANES:])


def split(value):
    high = value.astype(bf16)
    low = (value - high.astype(f32)).astype(bf16)
    return high, low


def dot(left, right):
    return jnp.dot(left, right, preferred_element_type=f32)


def dot_pairs(left, right):
    deep_left = jnp.concatenate([left[0], left[0], left[1]], axis=1)
    deep_right = jnp.concatenate([right[0], right[1], right[0]], axis=0)
    return dot(deep_left, deep_right)


def forward(signals, first, second, twist):
    rows = signals[0].shape[0]
    stage = dot_pairs(first, split(jnp.concatenate(signals, axis=1)))
    parts = []
    for i in range(len(signals)):
        cos = stage[:rows, i * LANES : (i + 1) * LANES]
        sin = stage[rows:, i * LANES : (i + 1) * LANES]
        parts.append(
            jnp.concatenate(
                [cos * twist[0] + sin * twist[1], cos * twist[1] - sin * twist[0]], axis=1
            )
        )
    spec = dot_pairs(split(jnp.concatenate(parts, axis=0)), second)
    return [
        (spec[i * rows : (i + 1) * rows, :LANES], spec[i * rows : (i + 1) * rows, LANES:])
        for i in range(len(signals))
    ]


def backward(spectra, back, second, twist):
    rows = spectra[0][0].shape[0]
    stacked = jnp.concatenate([jnp.concatenate(pair, axis=1) for pair in spectra], axis=0)
    stage = dot_pairs(split(stacked), second)
    parts = []
    for i in range(len(spectra)):
        re = stage[i * rows : (i + 1) * rows, :LANES]
        im = stage[i * rows : (i + 1) * rows, LANES:]
        parts.append(
            jnp.concatenate(
                [re * twist[0] - im * twist[1], re * twist[1] + im * twist[0]], axis=0
            )
        )
    out = dot_pairs(back, split(jnp.concatenate(parts, axis=1)))
    return [out[:, i * LANES : (i + 1) * LANES] for i in range(len(spectra))]


def times(a, b):
    return (a[0] * b[0] - a[1] * b[1], -(a[0] * b[1] + a[1] * b[0]))


def conj_times(a, b):
    return (a[0] * b[0] + a[1] * b[1], a[1] * b[0] - a[0] * b[1])


def one_hot(order):
    size = order.shape[1]
    place = lax.broadcasted_iota(jnp.int32, (size, size), 0)
    return (place == order).astype(f32).astype(bf16)


def project_kernel(
    features_at,
    order_at,
    cotangent_at,
    w_in_at,
    w_out_at,
    streams_out,
    gather_out,
    features,
    order,
    cotangent,
    w_in,
    w_out,
    done,
):
    copies = [
        pltpu.make_async_copy(source, target, done.at[i])
        for i, (source, target) in enumerate(
            [
                (order_at, order),
                (features_at, features),
                (w_in_at, w_in),
                (cotangent_at, cotangent),
                (w_out_at, w_out),
            ]
        )
    ]
    for copy in copies:
        copy.start()
    width, row_count = features.shape
    copies[0].wait()
    copies[1].wait()
    seq_input = dot(features[...], one_hot(order[...])).astype(bf16)
    copies[2].wait()
    projected = dot(w_in[...], seq_input)
    copies[3].wait()
    copies[4].wait()
    out_grad = lax.dot_general(
        w_out[...], cotangent[...], (((0,), (0,)), ((), ())), preferred_element_type=f32
    )
    if len(streams_out.shape) == 3:
        blocks = streams_out.shape[0]
        parts = [projected[s * width : (s + 1) * width] for s in range(3)] + [out_grad]
        parts = [part.reshape(blocks, width // blocks, row_count) for part in parts]
        streams_out[...] = jnp.concatenate(parts, axis=1).astype(bf16)
    else:
        streams_out[: 3 * width] = projected.astype(bf16)
        streams_out[3 * width :] = out_grad.astype(bf16)
    own = jnp.concatenate([seq_input, cotangent[...]], axis=0)
    gather_out[...] = own


def read_signal(ref, rows):
    if ref.shape[1] == LANES:
        return ref[...]
    return jnp.concatenate(
        [ref[:, i * LANES : (i + 1) * LANES] for i in range(ref.shape[1] // LANES)], axis=0
    )


def write_signal(ref, value):
    if ref.shape[1] == LANES:
        ref[...] = value
        return
    channels = ref.shape[0]
    for i in range(ref.shape[1] // LANES):
        ref[:, i * LANES : (i + 1) * LANES] = value[i * channels : (i + 1) * channels]


def filter_kernel(
    length,
    filter_one,
    filter_two,
    table,
    twist,
    order,
    spec_one,
    spec_two,
    table_out,
    twist_out,
    order_out,
):
    rows = spec_one.shape[0]
    signals = [read_signal(filter_one, rows), read_signal(filter_two, rows)]
    first, _, second, turns = tables_of(table, twist)
    one, two = forward(signals, first, second, turns)
    spec_one[...] = jnp.concatenate(one, axis=1) * (1.0 / length)
    spec_two[...] = jnp.concatenate(two, axis=1) * (1.0 / length)
    table_out[...] = table[...]
    twist_out[...] = twist[...]
    order_out[...] = order[...]


def pass_kernel(after, *refs):
    count = len(refs) // 2
    for source, target in zip(refs[:count], refs[count:]):
        target[...] = source[...]


def shifted(value, steps, channels):
    if steps == 0:
        return value
    rows, lanes = value.shape
    lane = lax.broadcasted_iota(jnp.int32, value.shape, 1)
    row = lax.broadcasted_iota(jnp.int32, value.shape, 0)
    turned = pltpu.roll(value, steps % lanes, 1)
    if steps > 0:
        carried = jnp.where(row < channels, 0.0, pltpu.roll(turned, channels, 0))
        return jnp.where(lane < steps, carried, turned)
    carried = jnp.where(row >= rows - channels, 0.0, pltpu.roll(turned, rows - channels, 0))
    return jnp.where(lane >= lanes + steps, carried, turned)


def mix_kernel(
    channels,
    scale,
    streams,
    taps,
    spec_one,
    spec_two,
    table,
    twist,
    line,
    short_out,
    product_one,
    product_two,
    *sent_out,
):
    rows = twist.shape[0]
    eight = taps.shape[0]
    first, back, second, twist = tables_of(table, twist)
    if streams.shape[0] == 4 and streams.shape[1] == rows:
        pieces = [streams[s].astype(f32) for s in range(4)]
    else:
        whole = streams[...].astype(f32)
        pieces = [
            whole[:, s * channels : (s + 1) * channels].reshape(rows, LANES) for s in range(4)
        ]
    out_grad = pieces[3]

    def tap(s, k):
        column = jnp.broadcast_to(taps[:, 3 * s + k : 3 * s + k + 1], (eight, LANES))
        column = jnp.broadcast_to(column[None], (rows // eight, eight, LANES))
        return column.reshape(rows, LANES)

    late = [[shifted(pieces[s], k, channels) for k in range(3)] for s in range(3)]
    value, gate_one, gate_two = [
        sum(tap(s, k) * late[s][k] for k in range(3)) for s in range(3)
    ]
    h_one = (spec_one[:, :LANES], spec_one[:, LANES:])
    h_two = (spec_two[:, :LANES], spec_two[:, LANES:])
    value_spec, second_spec = forward([value, out_grad * gate_two], first, second, twist)
    first_mix, grad_first_out = backward(
        [times(h_one, value_spec), conj_times(h_two, second_spec)],
        back,
        second,
        twist,
    )
    first_spec, grad_first_spec = forward(
        [gate_one * first_mix, gate_one * grad_first_out], first, second, twist
    )
    second_mix, grad_value = backward(
        [times(h_two, first_spec), conj_times(h_one, grad_first_spec)],
        back,
        second,
        twist,
    )
    product_one[...] = jnp.concatenate(conj_times(value_spec, grad_first_spec), axis=1)
    product_two[...] = jnp.concatenate(conj_times(first_spec, second_spec), axis=1)
    grads = [grad_value, grad_first_out * first_mix, out_grad * second_mix]
    sent = []
    lane = lax.broadcasted_iota(jnp.int32, (eight, LANES), 1)
    short = jnp.zeros((eight, LANES), f32)
    for s in range(3):
        sent.append(sum(tap(s, k) * shifted(grads[s], -k, channels) for k in range(3)))
        for k in range(3):
            folded = (grads[s] * late[s][k]).reshape(rows // eight, eight, LANES).sum(axis=0)
            total = jnp.sum(folded, axis=1, keepdims=True) * scale
            short = jnp.where(lane == 3 * s + k, total, short)
    sent.append(gate_two * second_mix)
    short_out[...] = short
    if len(sent_out) == 1:
        for s in range(4):
            sent_out[0][s] = sent[s].astype(bf16)
        return
    parts = [part.reshape(rows // channels, channels, LANES) for part in sent]
    packed = jnp.concatenate(parts, axis=1).astype(bf16)
    *sent_out, store = sent_out
    lines, plane = store.shape[:2]
    for i in range(lines):
        store[i] = packed[i * plane : (i + 1) * plane]
    for step in range(lines):
        sent_out[step][...] = store[lax.rem(line[0] + step, lines)]


def filter_grads_kernel(
    scale, product_one, product_two, table, twist, short, grad_one, grad_two, short_out
):
    _, back, second, twist = tables_of(table, twist)
    spectra = [(ref[:, :LANES], ref[:, LANES:]) for ref in (product_one, product_two)]
    one, two = backward(spectra, back, second, twist)
    write_signal(grad_one, one * scale)
    write_signal(grad_two, two * scale)
    short_out[...] = short[...]


def member(at, k):
    return jnp.bitwise_xor(at, k)


def weights_kernel(channels, scale, lines, *refs):
    line, place, short, *refs, partial_out, moved_out = refs
    met, pieces = refs[:lines], refs[lines:]
    plane, width = len(pieces), pieces[0].shape[0] // 2
    height = 4 * channels
    total = jnp.zeros((lines * height, 2 * width), f32)
    step = 2 if plane % 2 == 0 else 1
    for i in range(0, plane, step):
        left = jnp.concatenate(
            [
                jnp.concatenate([m[member(place[0], i + j)] for m in met], axis=0)
                for j in range(step)
            ],
            axis=1,
        )
        right = jnp.concatenate([pieces[i + j][...] for j in range(step)], axis=1)
        total = total + lax.dot_general(
            left, right, (((1,), (1,)), ((), ())), preferred_element_type=f32
        )
    total = total * scale
    size = height * (width // LANES)
    for k in range(lines):
        parts = []
        for h in range(width // LANES):
            low, high = h * LANES, (h + 1) * LANES
            base = k * height
            parts.append(total[base : base + 3 * channels, low:high])
            parts.append(total[base + 3 * channels : base + height, width + low : width + high])
        owner = lax.rem(line[0] + lines - k, lines)
        spot = pl.ds(pl.multiple_of(owner * size, size), size)
        partial_out[spot] = jnp.concatenate(parts, axis=0).astype(bf16)
    tail = jnp.concatenate([short[...]] * lines, axis=0)
    owner = lax.broadcasted_iota(jnp.int32, tail.shape, 0) // channels
    partial_out[lines * size :] = jnp.where(owner == line[0], tail, 0.0).astype(bf16)
    parts = [m[...].astype(f32)[:, : 3 * channels] for m in met]
    moved_out[...] = jnp.concatenate(parts, axis=1).astype(bf16)


def sum_kernel(*refs):
    *partials, out = refs
    out[...] = sum(part[...].astype(f32) for part in partials).astype(bf16)


def unorder(grad_projected, w_in, order):
    grad_seq = lax.dot_general(
        w_in, grad_projected, (((0,), (0,)), ((), ())), preferred_element_type=f32
    ).astype(bf16)
    return lax.dot_general(
        grad_seq, one_hot(order), (((1,), (1,)), ((), ())), preferred_element_type=f32
    ).astype(bf16)


def moved_kernel(channels, lines, line, back, w_in, order, features_out, store):
    plane, width = back.shape[0], w_in.shape[1]
    share = plane * channels
    whole = back[...].astype(f32)
    for k in range(lines):
        owner = lax.rem(line[0] + lines - k, lines)
        for s in range(3):
            start = (3 * k + s) * channels
            spot = pl.ds(pl.multiple_of(s * width + owner * share, share), share)
            store[spot] = whole[:, start : start + channels].reshape(share, LANES)
    features_out[...] = unorder(store[...].astype(bf16), w_in[...], order[...])


def finish_kernel(channels, lines, place, *refs):
    *pieces, w_in_out, w_out_out, short_out, out_rows, short_rows = refs
    width = w_out_out.shape[0]
    share = width // lines
    height = 4 * channels
    size = height * (width // LANES)
    for k, piece in enumerate(pieces):
        rows = piece[...].astype(f32)
        for i in range(lines):
            first = pl.multiple_of(i * share + member(place[0], k) * channels, channels)
            for h in range(width // LANES):
                low, high = h * LANES, (h + 1) * LANES
                base = i * size + h * height
                for s in range(3):
                    spot = pl.ds(pl.multiple_of(s * width + first, channels), channels)
                    start = base + s * channels
                    w_in_out[spot, low:high] = rows[start : start + channels]
                start = base + 3 * channels
                out_rows[pl.ds(first, channels), low:high] = rows[start : start + channels]
            start = lines * size + i * channels
            short_rows[pl.ds(first, channels), :] = rows[start : start + channels]
    w_out_out[...] = out_rows[...].T
    short = short_rows[...].T
    for s in range(3):
        short_out[:, s * width : (s + 1) * width] = short[3 * s : 3 * s + 3, :]


def features_kernel(moved, w_in, order, features_out):
    features_out[...] = unorder(moved[...], w_in[...], order[...])


def swapped(value, plane, distance):
    return lax.ppermute(value, "fft", [(i, i ^ distance) for i in range(plane)])


def spread(value, plane):
    pieces = [value if k == 0 else swapped(value, plane, k) for k in range(0, plane, 2)]
    return [piece for own in pieces for piece in (own, swapped(own, plane, 1))]


def shape(dims, dtype=f32):
    return jax.ShapeDtypeStruct(dims, dtype)


def local(features, sink_order, cotangent, w_in, short_taps, w_out, filter_one, filter_two):
    width, row_count = features.shape
    lines, plane = lax.axis_size("seq"), lax.axis_size("fft")
    blocks = lines * plane
    channels, length = filter_one.shape
    rows = channels * blocks
    scale = 1.0 / math.sqrt(length)
    whole = channels % 8 == 0 and plane % 2 == 0 and plane & (plane - 1) == 0
    table, twist = make_tables(blocks, channels)
    eight = channels if whole else 8
    mine = lax.axis_index(AXES)

    def call(kernel, outs, *args, **options):
        return pl.pallas_call(kernel, out_shape=outs, compiler_params=PARAMS, **options)(*args)

    dims = (blocks, 4 * channels, LANES) if whole else (4 * width, LANES)
    streams, own = pl.pallas_call(
        project_kernel,
        out_shape=(shape(dims, bf16), shape((2 * width, row_count), bf16)),
        in_specs=[pl.BlockSpec(memory_space=pl.ANY)] * 5,
        scratch_shapes=[
            pltpu.VMEM(a.shape, a.dtype)
            for a in (features, sink_order, cotangent, w_in, w_out)
        ]
        + [pltpu.SemaphoreType.DMA((5,))],
        compiler_params=pltpu.CompilerParams(vmem_limit_bytes=60 * 1024 * 1024),
    )(features, sink_order, cotangent, w_in, w_out)
    if not whole:
        streams = streams.reshape(4, blocks, channels, LANES).transpose(1, 0, 2, 3)
        streams = streams.reshape(blocks, 4 * channels, LANES)
    arrived = lax.all_to_all(streams, AXES, split_axis=0, concat_axis=0, tiled=True)
    taps = lax.dynamic_slice_in_dim(short_taps.reshape(3, width, 3), mine * channels, channels, 1)
    taps = taps.transpose(1, 0, 2).reshape(channels, 9)
    if not whole:
        taps = jnp.tile(taps, (8 // channels, 1))
        arrived = arrived.reshape(blocks, 4, channels, LANES).transpose(1, 0, 2, 3)
        arrived = arrived.reshape(4, rows, LANES)
        filter_one, filter_two = [
            h.reshape(channels, blocks, LANES).transpose(1, 0, 2).reshape(rows, LANES)
            for h in (filter_one, filter_two)
        ]
    spec = shape((rows, 2 * LANES))
    spec_one, spec_two, table, twist, order = call(
        lambda *refs: filter_kernel(length, *refs),
        (
            spec,
            spec,
            shape(table.shape, bf16),
            shape(twist.shape),
            shape(sink_order.shape, jnp.int32),
        ),
        filter_one,
        filter_two,
        table,
        twist,
        sink_order,
    )
    line = lax.axis_index("seq").astype(jnp.int32).reshape(1)
    place = lax.axis_index("fft").astype(jnp.int32).reshape(1)
    scalar = pl.BlockSpec(memory_space=pltpu.SMEM)
    held = pl.BlockSpec(memory_space=pltpu.VMEM)
    chunk = (plane, 4 * channels, LANES)
    dims = [shape(chunk, bf16)] * lines if whole else [shape((4, rows, LANES), bf16)]
    short, product_one, product_two, *sent = call(
        lambda *refs: mix_kernel(channels, scale, *refs),
        (shape((eight, LANES)), spec, spec, *dims),
        arrived,
        taps,
        spec_one,
        spec_two,
        table,
        twist,
        line,
        in_specs=[held] * 6 + [scalar],
        scratch_shapes=[pltpu.VMEM((lines, *chunk), bf16)] if whole else [],
    )
    if whole:
        pieces = [swapped(own, plane, k) for k in (1, *range(2, plane, 2))]
        beside, *pieces = call(
            pass_kernel, [shape(own.shape, bf16)] * len(pieces), short, *pieces
        )
        pieces = [own, beside] + [a for p in pieces for a in (p, swapped(p, plane, 1))]
    grad_one, grad_two, short = call(
        lambda *refs: filter_grads_kernel(scale / length, *refs),
        (shape(filter_one.shape), shape(filter_two.shape), shape(short.shape)),
        product_one,
        product_two,
        table,
        twist,
        short,
    )
    height = channels * 4 * (width // LANES)
    if whole:
        def ahead(value, steps):
            pairs = [(i, (i + steps) % lines) for i in range(lines)]
            return lax.ppermute(value, "seq", pairs)

        met = [sent[0]] + [ahead(sent[k], k) for k in range(1, lines)]
        size = lines * height + lines * channels
        partial, moved = call(
            lambda *refs: weights_kernel(channels, scale, lines, *refs),
            (
                shape((size, LANES), bf16),
                shape((plane, 3 * lines * channels, LANES), bf16),
            ),
            line,
            place,
            short,
            *met,
            *pieces,
            in_specs=[scalar] * 2 + [held] * (1 + lines + plane),
        )
        partials = [partial] + [ahead(partial, k) for k in range(1, lines)]
        back = lax.all_to_all(moved, "fft", split_axis=0, concat_axis=0, tiled=True)
        grad_features = call(
            lambda *refs: moved_kernel(channels, lines, *refs),
            shape(features.shape, bf16),
            line,
            back,
            w_in,
            order,
            in_specs=[scalar] + [held] * 3,
            scratch_shapes=[pltpu.VMEM((3 * width, LANES), f32)],
        )
        rows_sum = call(sum_kernel, shape((size, LANES), bf16), *partials)
        grad_w_in, grad_w_out, short = call(
            lambda *refs: finish_kernel(channels, lines, *refs),
            (shape((3 * width, width)), shape((width, width)), shape((3, 3 * width))),
            place,
            *spread(rows_sum, plane),
            in_specs=[scalar] + [held] * plane,
            scratch_shapes=[pltpu.VMEM((width, width), f32), pltpu.VMEM((width, LANES), f32)],
        )
        return (grad_features, grad_w_in, grad_w_out, short.T, grad_one, grad_two)
    gathered = lax.all_gather(own, AXES, axis=0, tiled=False)
    sent = sent[0]
    sent = sent.reshape(4, blocks, channels, LANES)
    grad_in = jnp.einsum(
        "sbcp,bwp->scw", sent[:3], gathered[:, :width], preferred_element_type=f32
    )
    grad_out = jnp.einsum(
        "bcp,bwp->cw", sent[3], gathered[:, width:], preferred_element_type=f32
    )
    own = jnp.concatenate([grad_in, grad_out[None]]) * scale
    own = own.reshape(height, LANES)
    short = short.reshape(8 // channels, channels, LANES).sum(axis=0)
    own = jnp.concatenate([own, short]).astype(bf16)
    moved = sent[:3].transpose(1, 0, 2, 3).reshape(blocks, 3 * channels, LANES)
    own = jnp.broadcast_to(own[None], (blocks,) + own.shape)
    packed = jnp.concatenate([moved, own], axis=1)
    back = lax.all_to_all(packed, AXES, split_axis=0, concat_axis=0, tiled=True)
    moved = back[:, : 3 * channels].reshape(blocks, 3, channels, LANES)
    moved = moved.transpose(1, 0, 2, 3).reshape(3 * width, LANES)
    weights = back[:, 3 * channels : 3 * channels + height].astype(f32)
    weights = weights.reshape(blocks, 4, channels, width).transpose(1, 0, 2, 3)
    weights = weights.reshape(4 * width, width)
    short = back[:, 3 * channels + height :, :9].astype(f32).reshape(width, 3, 3)
    short = short.transpose(1, 0, 2).reshape(3 * width, 3)
    grad_features = call(
        features_kernel, shape(features.shape, bf16), moved, w_in, sink_order
    )
    grad_one, grad_two = [
        g.reshape(blocks, channels, LANES).transpose(1, 0, 2).reshape(channels, length)
        for g in (grad_one, grad_two)
    ]
    return (
        grad_features,
        weights[: 3 * width],
        weights[3 * width :].T,
        short,
        grad_one,
        grad_two,
    )


def solution(mesh):
    columns, blocks_first, copied = P(None, AXES), P(AXES, None), P()
    return jax.shard_map(
        local,
        mesh=mesh,
        in_specs=(
            columns,
            blocks_first,
            columns,
            copied,
            copied,
            copied,
            blocks_first,
            blocks_first,
        ),
        out_specs=(columns, copied, copied, copied, blocks_first, blocks_first),
        check_vma=False,
    )
```

```python
import math

import jax
import jax.numpy as jnp
import numpy as np
from jax import lax
from jax.experimental import pallas as pl
from jax.experimental.pallas import tpu as pltpu
from jax.sharding import PartitionSpec as P

AXES = ("seq", "fft")
LANES = 128
bf16 = jnp.bfloat16
f32 = jnp.float32
PARAMS = pltpu.CompilerParams(vmem_limit_bytes=24 * 1024 * 1024)


def halves(table):
    high = table.astype(np.float32).astype(jnp.bfloat16)
    low = (table - high.astype(np.float64)).astype(np.float32).astype(jnp.bfloat16)
    return high, low


def make_tables(count, channels):
    length = count * LANES
    outer = np.arange(count, dtype=np.float64) + 0.25
    inner = np.arange(LANES, dtype=np.float64)
    angle = 2.0 * np.pi * outer[:, None] * outer[None, :] / count
    first = np.kron(np.concatenate([np.cos(angle), np.sin(angle)], axis=0), np.eye(channels))
    turn = 2.0 * np.pi * (inner[:, None] * inner[None, :] % LANES) / LANES
    cos, sin = np.cos(turn), np.sin(turn)
    second = np.block([[cos, -sin], [sin, cos]])
    packed = [half for t in (first, second) for half in halves(t)]
    twist = 2.0 * np.pi * outer[:, None] * (inner[None, :] - LANES / 4) / length
    twist = np.repeat(twist, channels, axis=0)
    twist = np.concatenate([np.cos(twist), -np.sin(twist)], axis=1).astype(np.float32)
    return np.concatenate(packed, axis=0), twist


def tables_of(table, twist):
    rows = twist.shape[0]
    at, found = 0, []
    for size in (2 * rows, 2 * LANES):
        pair = []
        for half in range(2):
            pair.append(table[at : at + size])
            at += size
        found.append(tuple(pair))
    first, second = found
    back = tuple(jnp.concatenate([t[:rows], t[rows:]], axis=1) for t in first)
    return first, back, second, (twist[:, :LANES], twist[:, LANES:])


def split(value):
    high = value.astype(bf16)
    low = (value - high.astype(f32)).astype(bf16)
    return high, low


def dot(left, right):
    return jnp.dot(left, right, preferred_element_type=f32)


def dot_pairs(left, right):
    deep_left = jnp.concatenate([left[0], left[0], left[1]], axis=1)
    deep_right = jnp.concatenate([right[0], right[1], right[0]], axis=0)
    return dot(deep_left, deep_right)


def forward(signals, first, second, twist):
    rows = signals[0].shape[0]
    stage = dot_pairs(first, split(jnp.concatenate(signals, axis=1)))
    parts = []
    for i in range(len(signals)):
        cos = stage[:rows, i * LANES : (i + 1) * LANES]
        sin = stage[rows:, i * LANES : (i + 1) * LANES]
        parts.append(
            jnp.concatenate(
                [cos * twist[0] + sin * twist[1], cos * twist[1] - sin * twist[0]], axis=1
            )
        )
    spec = dot_pairs(split(jnp.concatenate(parts, axis=0)), second)
    return [
        (spec[i * rows : (i + 1) * rows, :LANES], spec[i * rows : (i + 1) * rows, LANES:])
        for i in range(len(signals))
    ]


def backward(spectra, back, second, twist):
    rows = spectra[0][0].shape[0]
    stacked = jnp.concatenate([jnp.concatenate(pair, axis=1) for pair in spectra], axis=0)
    stage = dot_pairs(split(stacked), second)
    parts = []
    for i in range(len(spectra)):
        re = stage[i * rows : (i + 1) * rows, :LANES]
        im = stage[i * rows : (i + 1) * rows, LANES:]
        parts.append(
            jnp.concatenate(
                [re * twist[0] - im * twist[1], re * twist[1] + im * twist[0]], axis=0
            )
        )
    out = dot_pairs(back, split(jnp.concatenate(parts, axis=1)))
    return [out[:, i * LANES : (i + 1) * LANES] for i in range(len(spectra))]


def times(a, b):
    return (a[0] * b[0] - a[1] * b[1], -(a[0] * b[1] + a[1] * b[0]))


def conj_times(a, b):
    return (a[0] * b[0] + a[1] * b[1], a[1] * b[0] - a[0] * b[1])


def one_hot(order):
    size = order.shape[1]
    place = lax.broadcasted_iota(jnp.int32, (size, size), 0)
    return (place == order).astype(f32).astype(bf16)


def project_kernel(
    features_at,
    order_at,
    cotangent_at,
    w_in_at,
    w_out_at,
    streams_out,
    gather_out,
    features,
    order,
    cotangent,
    w_in,
    w_out,
    done,
):
    copies = [
        pltpu.make_async_copy(source, target, done.at[i])
        for i, (source, target) in enumerate(
            [
                (order_at, order),
                (features_at, features),
                (w_in_at, w_in),
                (cotangent_at, cotangent),
                (w_out_at, w_out),
            ]
        )
    ]
    for copy in copies:
        copy.start()
    width, row_count = features.shape
    copies[0].wait()
    copies[1].wait()
    seq_input = dot(features[...], one_hot(order[...])).astype(bf16)
    copies[2].wait()
    projected = dot(w_in[...], seq_input)
    copies[3].wait()
    copies[4].wait()
    out_grad = lax.dot_general(
        w_out[...], cotangent[...], (((0,), (0,)), ((), ())), preferred_element_type=f32
    )
    if len(streams_out.shape) == 3:
        blocks = streams_out.shape[0]
        parts = [projected[s * width : (s + 1) * width] for s in range(3)] + [out_grad]
        parts = [part.reshape(blocks, width // blocks, row_count) for part in parts]
        streams_out[...] = jnp.concatenate(parts, axis=1).astype(bf16)
    else:
        streams_out[: 3 * width] = projected.astype(bf16)
        streams_out[3 * width :] = out_grad.astype(bf16)
    own = jnp.concatenate([seq_input, cotangent[...]], axis=0)
    gather_out[...] = own


def read_signal(ref, rows):
    if ref.shape[1] == LANES:
        return ref[...]
    return jnp.concatenate(
        [ref[:, i * LANES : (i + 1) * LANES] for i in range(ref.shape[1] // LANES)], axis=0
    )


def write_signal(ref, value):
    if ref.shape[1] == LANES:
        ref[...] = value
        return
    channels = ref.shape[0]
    for i in range(ref.shape[1] // LANES):
        ref[:, i * LANES : (i + 1) * LANES] = value[i * channels : (i + 1) * channels]


def filter_kernel(
    length,
    filter_one,
    filter_two,
    table,
    twist,
    order,
    spec_one,
    spec_two,
    table_out,
    twist_out,
    order_out,
):
    rows = spec_one.shape[0]
    signals = [read_signal(filter_one, rows), read_signal(filter_two, rows)]
    first, _, second, turns = tables_of(table, twist)
    one, two = forward(signals, first, second, turns)
    spec_one[...] = jnp.concatenate(one, axis=1) * (1.0 / length)
    spec_two[...] = jnp.concatenate(two, axis=1) * (1.0 / length)
    table_out[...] = table[...]
    twist_out[...] = twist[...]
    order_out[...] = order[...]


def stack_kernel(after, *refs):
    *sources, out = refs
    for i, source in enumerate(sources):
        out[i] = source[...]


def shifted(value, steps, channels):
    if steps == 0:
        return value
    rows, lanes = value.shape
    lane = lax.broadcasted_iota(jnp.int32, value.shape, 1)
    row = lax.broadcasted_iota(jnp.int32, value.shape, 0)
    turned = pltpu.roll(value, steps % lanes, 1)
    if steps > 0:
        carried = jnp.where(row < channels, 0.0, pltpu.roll(turned, channels, 0))
        return jnp.where(lane < steps, carried, turned)
    carried = jnp.where(row >= rows - channels, 0.0, pltpu.roll(turned, rows - channels, 0))
    return jnp.where(lane >= lanes + steps, carried, turned)


def mix_kernel(
    channels,
    scale,
    streams,
    taps,
    spec_one,
    spec_two,
    table,
    twist,
    line,
    short_out,
    product_one,
    product_two,
    *sent_out,
):
    rows = twist.shape[0]
    eight = taps.shape[0]
    first, back, second, twist = tables_of(table, twist)
    if streams.shape[0] == 4 and streams.shape[1] == rows:
        pieces = [streams[s].astype(f32) for s in range(4)]
    else:
        whole = streams[...].astype(f32)
        pieces = [
            whole[:, s * channels : (s + 1) * channels].reshape(rows, LANES) for s in range(4)
        ]
    out_grad = pieces[3]

    def tap(s, k):
        column = jnp.broadcast_to(taps[:, 3 * s + k : 3 * s + k + 1], (eight, LANES))
        column = jnp.broadcast_to(column[None], (rows // eight, eight, LANES))
        return column.reshape(rows, LANES)

    late = [[shifted(pieces[s], k, channels) for k in range(3)] for s in range(3)]
    value, gate_one, gate_two = [
        sum(tap(s, k) * late[s][k] for k in range(3)) for s in range(3)
    ]
    h_one = (spec_one[:, :LANES], spec_one[:, LANES:])
    h_two = (spec_two[:, :LANES], spec_two[:, LANES:])
    value_spec, second_spec = forward([value, out_grad * gate_two], first, second, twist)
    first_mix, grad_first_out = backward(
        [times(h_one, value_spec), conj_times(h_two, second_spec)],
        back,
        second,
        twist,
    )
    first_spec, grad_first_spec = forward(
        [gate_one * first_mix, gate_one * grad_first_out], first, second, twist
    )
    second_mix, grad_value = backward(
        [times(h_two, first_spec), conj_times(h_one, grad_first_spec)],
        back,
        second,
        twist,
    )
    product_one[...] = jnp.concatenate(conj_times(value_spec, grad_first_spec), axis=1)
    product_two[...] = jnp.concatenate(conj_times(first_spec, second_spec), axis=1)
    grads = [grad_value, grad_first_out * first_mix, out_grad * second_mix]
    sent = []
    lane = lax.broadcasted_iota(jnp.int32, (eight, LANES), 1)
    short = jnp.zeros((eight, LANES), f32)
    for s in range(3):
        sent.append(sum(tap(s, k) * shifted(grads[s], -k, channels) for k in range(3)))
        for k in range(3):
            folded = (grads[s] * late[s][k]).reshape(rows // eight, eight, LANES).sum(axis=0)
            total = jnp.sum(folded, axis=1, keepdims=True) * scale
            short = jnp.where(lane == 3 * s + k, total, short)
    sent.append(gate_two * second_mix)
    short_out[...] = short
    if len(sent_out) == 1:
        for s in range(4):
            sent_out[0][s] = sent[s].astype(bf16)
        return
    parts = [part.reshape(rows // channels, channels, LANES) for part in sent]
    packed = jnp.concatenate(parts, axis=1).astype(bf16)
    *sent_out, store = sent_out
    lines, plane = store.shape[:2]
    for i in range(lines):
        store[i] = packed[i * plane : (i + 1) * plane]
    for step in range(lines):
        sent_out[step][...] = store[lax.rem(line[0] + step, lines)]


def filter_grads_kernel(
    scale, product_one, product_two, table, twist, short, grad_one, grad_two, short_out
):
    _, back, second, twist = tables_of(table, twist)
    spectra = [(ref[:, :LANES], ref[:, LANES:]) for ref in (product_one, product_two)]
    one, two = backward(spectra, back, second, twist)
    write_signal(grad_one, one * scale)
    write_signal(grad_two, two * scale)
    short_out[...] = short[...]


def member(at, k):
    return jnp.bitwise_xor(at, k)


def weights_kernel(channels, scale, lines, *refs):
    line, place, short, *refs, partial_out, moved_out = refs
    met, (own, beside, across, over) = refs[:lines], refs[lines:]
    pieces = [own[...], beside[...]]
    for i in range(across.shape[0]):
        pieces += [across[i], over[i]]
    plane, width = len(pieces), own.shape[0] // 2
    height = 4 * channels
    total = jnp.zeros((lines * height, 2 * width), f32)
    step = 2 if plane % 2 == 0 else 1
    for i in range(0, plane, step):
        left = jnp.concatenate(
            [
                jnp.concatenate([m[member(place[0], i + j)] for m in met], axis=0)
                for j in range(step)
            ],
            axis=1,
        )
        right = jnp.concatenate([pieces[i + j] for j in range(step)], axis=1)
        total = total + lax.dot_general(
            left, right, (((1,), (1,)), ((), ())), preferred_element_type=f32
        )
    total = total * scale
    size = height * (width // LANES)
    for k in range(lines):
        parts = []
        for h in range(width // LANES):
            low, high = h * LANES, (h + 1) * LANES
            base = k * height
            parts.append(total[base : base + 3 * channels, low:high])
            parts.append(total[base + 3 * channels : base + height, width + low : width + high])
        owner = lax.rem(line[0] + lines - k, lines)
        spot = pl.ds(pl.multiple_of(owner * size, size), size)
        partial_out[spot] = jnp.concatenate(parts, axis=0).astype(bf16)
    tail = jnp.concatenate([short[...]] * lines, axis=0)
    owner = lax.broadcasted_iota(jnp.int32, tail.shape, 0) // channels
    partial_out[lines * size :] = jnp.where(owner == line[0], tail, 0.0).astype(bf16)
    parts = [m[...].astype(f32)[:, : 3 * channels] for m in met]
    moved_out[...] = jnp.concatenate(parts, axis=1).astype(bf16)


def sum_kernel(*refs):
    *partials, out = refs
    out[...] = sum(part[...].astype(f32) for part in partials).astype(bf16)


def unorder(grad_projected, w_in, order):
    grad_seq = lax.dot_general(
        w_in, grad_projected, (((0,), (0,)), ((), ())), preferred_element_type=f32
    ).astype(bf16)
    return lax.dot_general(
        grad_seq, one_hot(order), (((1,), (1,)), ((), ())), preferred_element_type=f32
    ).astype(bf16)


def moved_kernel(channels, lines, line, back, w_in, order, features_out, store):
    plane, width = back.shape[0], w_in.shape[1]
    share = plane * channels
    whole = back[...].astype(f32)
    for k in range(lines):
        owner = lax.rem(line[0] + lines - k, lines)
        for s in range(3):
            start = (3 * k + s) * channels
            spot = pl.ds(pl.multiple_of(s * width + owner * share, share), share)
            store[spot] = whole[:, start : start + channels].reshape(share, LANES)
    features_out[...] = unorder(store[...].astype(bf16), w_in[...], order[...])


def finish_kernel(channels, lines, place, *refs):
    *pieces, w_in_out, w_out_out, short_out, out_rows, short_rows = refs
    width = w_out_out.shape[0]
    share = width // lines
    height = 4 * channels
    size = height * (width // LANES)
    for k, piece in enumerate(pieces):
        rows = piece[...].astype(f32)
        for i in range(lines):
            first = pl.multiple_of(i * share + member(place[0], k) * channels, channels)
            for h in range(width // LANES):
                low, high = h * LANES, (h + 1) * LANES
                base = i * size + h * height
                for s in range(3):
                    spot = pl.ds(pl.multiple_of(s * width + first, channels), channels)
                    start = base + s * channels
                    w_in_out[spot, low:high] = rows[start : start + channels]
                start = base + 3 * channels
                out_rows[pl.ds(first, channels), low:high] = rows[start : start + channels]
            start = lines * size + i * channels
            short_rows[pl.ds(first, channels), :] = rows[start : start + channels]
    w_out_out[...] = out_rows[...].T
    short = short_rows[...].T
    for s in range(3):
        short_out[:, s * width : (s + 1) * width] = short[3 * s : 3 * s + 3, :]


def features_kernel(moved, w_in, order, features_out):
    features_out[...] = unorder(moved[...], w_in[...], order[...])


def swapped(value, plane, distance):
    return lax.ppermute(value, "fft", [(i, i ^ distance) for i in range(plane)])


def spread(value, plane):
    pieces = [value if k == 0 else swapped(value, plane, k) for k in range(0, plane, 2)]
    return [piece for own in pieces for piece in (own, swapped(own, plane, 1))]


def shape(dims, dtype=f32):
    return jax.ShapeDtypeStruct(dims, dtype)


def local(features, sink_order, cotangent, w_in, short_taps, w_out, filter_one, filter_two):
    width, row_count = features.shape
    lines, plane = lax.axis_size("seq"), lax.axis_size("fft")
    blocks = lines * plane
    channels, length = filter_one.shape
    rows = channels * blocks
    scale = 1.0 / math.sqrt(length)
    whole = channels % 8 == 0 and plane % 2 == 0 and plane & (plane - 1) == 0
    table, twist = make_tables(blocks, channels)
    eight = channels if whole else 8
    mine = lax.axis_index(AXES)

    def call(kernel, outs, *args, **options):
        return pl.pallas_call(kernel, out_shape=outs, compiler_params=PARAMS, **options)(*args)

    dims = (blocks, 4 * channels, LANES) if whole else (4 * width, LANES)
    streams, own = pl.pallas_call(
        project_kernel,
        out_shape=(shape(dims, bf16), shape((2 * width, row_count), bf16)),
        in_specs=[pl.BlockSpec(memory_space=pl.ANY)] * 5,
        scratch_shapes=[
            pltpu.VMEM(a.shape, a.dtype)
            for a in (features, sink_order, cotangent, w_in, w_out)
        ]
        + [pltpu.SemaphoreType.DMA((5,))],
        compiler_params=pltpu.CompilerParams(vmem_limit_bytes=60 * 1024 * 1024),
    )(features, sink_order, cotangent, w_in, w_out)
    if not whole:
        streams = streams.reshape(4, blocks, channels, LANES).transpose(1, 0, 2, 3)
        streams = streams.reshape(blocks, 4 * channels, LANES)
    arrived = lax.all_to_all(streams, AXES, split_axis=0, concat_axis=0, tiled=True)
    taps = lax.dynamic_slice_in_dim(short_taps.reshape(3, width, 3), mine * channels, channels, 1)
    taps = taps.transpose(1, 0, 2).reshape(channels, 9)
    if not whole:
        taps = jnp.tile(taps, (8 // channels, 1))
        arrived = arrived.reshape(blocks, 4, channels, LANES).transpose(1, 0, 2, 3)
        arrived = arrived.reshape(4, rows, LANES)
        filter_one, filter_two = [
            h.reshape(channels, blocks, LANES).transpose(1, 0, 2).reshape(rows, LANES)
            for h in (filter_one, filter_two)
        ]
    spec = shape((rows, 2 * LANES))
    spec_one, spec_two, table, twist, order = call(
        lambda *refs: filter_kernel(length, *refs),
        (
            spec,
            spec,
            shape(table.shape, bf16),
            shape(twist.shape),
            shape(sink_order.shape, jnp.int32),
        ),
        filter_one,
        filter_two,
        table,
        twist,
        sink_order,
    )
    line = lax.axis_index("seq").astype(jnp.int32).reshape(1)
    place = lax.axis_index("fft").astype(jnp.int32).reshape(1)
    scalar = pl.BlockSpec(memory_space=pltpu.SMEM)
    held = pl.BlockSpec(memory_space=pltpu.VMEM)
    chunk = (plane, 4 * channels, LANES)
    dims = [shape(chunk, bf16)] * lines if whole else [shape((4, rows, LANES), bf16)]
    short, product_one, product_two, *sent = call(
        lambda *refs: mix_kernel(channels, scale, *refs),
        (shape((eight, LANES)), spec, spec, *dims),
        arrived,
        taps,
        spec_one,
        spec_two,
        table,
        twist,
        line,
        in_specs=[held] * 6 + [scalar],
        scratch_shapes=[pltpu.VMEM((lines, *chunk), bf16)] if whole else [],
    )
    if whole:
        across = [swapped(own, plane, k) for k in range(2, plane, 2)]
        across = call(stack_kernel, shape((len(across), *own.shape), bf16), short, *across)
        pieces = (own, swapped(own, plane, 1), across, swapped(across, plane, 1))
    grad_one, grad_two, short = call(
        lambda *refs: filter_grads_kernel(scale / length, *refs),
        (shape(filter_one.shape), shape(filter_two.shape), shape(short.shape)),
        product_one,
        product_two,
        table,
        twist,
        short,
    )
    height = channels * 4 * (width // LANES)
    if whole:
        def ahead(value, steps):
            pairs = [(i, (i + steps) % lines) for i in range(lines)]
            return lax.ppermute(value, "seq", pairs)

        met = [sent[0]] + [ahead(sent[k], k) for k in range(1, lines)]
        size = lines * height + lines * channels
        partial, moved = call(
            lambda *refs: weights_kernel(channels, scale, lines, *refs),
            (
                shape((size, LANES), bf16),
                shape((plane, 3 * lines * channels, LANES), bf16),
            ),
            line,
            place,
            short,
            *met,
            *pieces,
            in_specs=[scalar] * 2 + [held] * (1 + lines + len(pieces)),
        )
        partials = [partial] + [ahead(partial, k) for k in range(1, lines)]
        back = lax.all_to_all(moved, "fft", split_axis=0, concat_axis=0, tiled=True)
        grad_features = call(
            lambda *refs: moved_kernel(channels, lines, *refs),
            shape(features.shape, bf16),
            line,
            back,
            w_in,
            order,
            in_specs=[scalar] + [held] * 3,
            scratch_shapes=[pltpu.VMEM((3 * width, LANES), f32)],
        )
        rows_sum = call(sum_kernel, shape((size, LANES), bf16), *partials)
        grad_w_in, grad_w_out, short = call(
            lambda *refs: finish_kernel(channels, lines, *refs),
            (shape((3 * width, width)), shape((width, width)), shape((3, 3 * width))),
            place,
            *spread(rows_sum, plane),
            in_specs=[scalar] + [held] * plane,
            scratch_shapes=[pltpu.VMEM((width, width), f32), pltpu.VMEM((width, LANES), f32)],
        )
        return (grad_features, grad_w_in, grad_w_out, short.T, grad_one, grad_two)
    gathered = lax.all_gather(own, AXES, axis=0, tiled=False)
    sent = sent[0]
    sent = sent.reshape(4, blocks, channels, LANES)
    grad_in = jnp.einsum(
        "sbcp,bwp->scw", sent[:3], gathered[:, :width], preferred_element_type=f32
    )
    grad_out = jnp.einsum(
        "bcp,bwp->cw", sent[3], gathered[:, width:], preferred_element_type=f32
    )
    own = jnp.concatenate([grad_in, grad_out[None]]) * scale
    own = own.reshape(height, LANES)
    short = short.reshape(8 // channels, channels, LANES).sum(axis=0)
    own = jnp.concatenate([own, short]).astype(bf16)
    moved = sent[:3].transpose(1, 0, 2, 3).reshape(blocks, 3 * channels, LANES)
    own = jnp.broadcast_to(own[None], (blocks,) + own.shape)
    packed = jnp.concatenate([moved, own], axis=1)
    back = lax.all_to_all(packed, AXES, split_axis=0, concat_axis=0, tiled=True)
    moved = back[:, : 3 * channels].reshape(blocks, 3, channels, LANES)
    moved = moved.transpose(1, 0, 2, 3).reshape(3 * width, LANES)
    weights = back[:, 3 * channels : 3 * channels + height].astype(f32)
    weights = weights.reshape(blocks, 4, channels, width).transpose(1, 0, 2, 3)
    weights = weights.reshape(4 * width, width)
    short = back[:, 3 * channels + height :, :9].astype(f32).reshape(width, 3, 3)
    short = short.transpose(1, 0, 2).reshape(3 * width, 3)
    grad_features = call(
        features_kernel, shape(features.shape, bf16), moved, w_in, sink_order
    )
    grad_one, grad_two = [
        g.reshape(blocks, channels, LANES).transpose(1, 0, 2).reshape(channels, length)
        for g in (grad_one, grad_two)
    ]
    return (
        grad_features,
        weights[: 3 * width],
        weights[3 * width :].T,
        short,
        grad_one,
        grad_two,
    )


def solution(mesh):
    columns, blocks_first, copied = P(None, AXES), P(AXES, None), P()
    return jax.shard_map(
        local,
        mesh=mesh,
        in_specs=(
            columns,
            blocks_first,
            columns,
            copied,
            copied,
            copied,
            blocks_first,
            blocks_first,
        ),
        out_specs=(columns, copied, copied, copied, blocks_first, blocks_first),
        check_vma=False,
    )
```

```python
import math

import jax
import jax.numpy as jnp
import numpy as np
from jax import lax
from jax.experimental import pallas as pl
from jax.experimental.pallas import tpu as pltpu
from jax.sharding import PartitionSpec as P

AXES = ("seq", "fft")
LANES = 128
bf16 = jnp.bfloat16
f32 = jnp.float32
PARAMS = pltpu.CompilerParams(vmem_limit_bytes=24 * 1024 * 1024)


def halves(table):
    high = table.astype(np.float32).astype(jnp.bfloat16)
    low = (table - high.astype(np.float64)).astype(np.float32).astype(jnp.bfloat16)
    return high, low


def make_tables(count, channels):
    length = count * LANES
    outer = np.arange(count, dtype=np.float64) + 0.25
    inner = np.arange(LANES, dtype=np.float64)
    angle = 2.0 * np.pi * outer[:, None] * outer[None, :] / count
    first = np.kron(np.concatenate([np.cos(angle), np.sin(angle)], axis=0), np.eye(channels))
    turn = 2.0 * np.pi * (inner[:, None] * inner[None, :] % LANES) / LANES
    cos, sin = np.cos(turn), np.sin(turn)
    second = np.block([[cos, -sin], [sin, cos]])
    packed = [half for t in (first, second) for half in halves(t)]
    twist = 2.0 * np.pi * outer[:, None] * (inner[None, :] - LANES / 4) / length
    twist = np.repeat(twist, channels, axis=0)
    twist = np.concatenate([np.cos(twist), -np.sin(twist)], axis=1).astype(np.float32)
    return np.concatenate(packed, axis=0), twist


def tables_of(table, twist):
    rows = twist.shape[0]
    at, found = 0, []
    for size in (2 * rows, 2 * LANES):
        pair = []
        for half in range(2):
            pair.append(table[at : at + size])
            at += size
        found.append(tuple(pair))
    first, second = found
    back = tuple(jnp.concatenate([t[:rows], t[rows:]], axis=1) for t in first)
    return first, back, second, (twist[:, :LANES], twist[:, LANES:])


def split(value):
    high = value.astype(bf16)
    low = (value - high.astype(f32)).astype(bf16)
    return high, low


def dot(left, right):
    return jnp.dot(left, right, preferred_element_type=f32)


def dot_pairs(left, right):
    deep_left = jnp.concatenate([left[0], left[0], left[1]], axis=1)
    deep_right = jnp.concatenate([right[0], right[1], right[0]], axis=0)
    return dot(deep_left, deep_right)


def forward(signals, first, second, twist):
    rows = signals[0].shape[0]
    stage = dot_pairs(first, split(jnp.concatenate(signals, axis=1)))
    parts = []
    for i in range(len(signals)):
        cos = stage[:rows, i * LANES : (i + 1) * LANES]
        sin = stage[rows:, i * LANES : (i + 1) * LANES]
        parts.append(
            jnp.concatenate(
                [cos * twist[0] + sin * twist[1], cos * twist[1] - sin * twist[0]], axis=1
            )
        )
    specs = [dot_pairs(split(part), second) for part in parts]
    return [(spec[:, :LANES], spec[:, LANES:]) for spec in specs]


def backward(spectra, back, second, twist):
    parts = []
    for pair in spectra:
        stage = dot_pairs(split(jnp.concatenate(pair, axis=1)), second)
        re, im = stage[:, :LANES], stage[:, LANES:]
        parts.append(
            jnp.concatenate(
                [re * twist[0] - im * twist[1], re * twist[1] + im * twist[0]], axis=0
            )
        )
    out = dot_pairs(back, split(jnp.concatenate(parts, axis=1)))
    return [out[:, i * LANES : (i + 1) * LANES] for i in range(len(spectra))]


def times(a, b):
    return (a[0] * b[0] - a[1] * b[1], -(a[0] * b[1] + a[1] * b[0]))


def conj_times(a, b):
    return (a[0] * b[0] + a[1] * b[1], a[1] * b[0] - a[0] * b[1])


def one_hot(order):
    size = order.shape[1]
    place = lax.broadcasted_iota(jnp.int32, (size, size), 0)
    return (place == order).astype(f32).astype(bf16)


def project_kernel(
    features_at,
    order_at,
    cotangent_at,
    w_in_at,
    w_out_at,
    streams_out,
    gather_out,
    features,
    order,
    cotangent,
    w_in,
    w_out,
    done,
):
    copies = [
        pltpu.make_async_copy(source, target, done.at[i])
        for i, (source, target) in enumerate(
            [
                (order_at, order),
                (features_at, features),
                (w_in_at, w_in),
                (cotangent_at, cotangent),
                (w_out_at, w_out),
            ]
        )
    ]
    for copy in copies:
        copy.start()
    width, row_count = features.shape
    copies[0].wait()
    copies[1].wait()
    seq_input = dot(features[...], one_hot(order[...])).astype(bf16)
    copies[2].wait()
    projected = dot(w_in[...], seq_input)
    copies[3].wait()
    copies[4].wait()
    out_grad = lax.dot_general(
        w_out[...], cotangent[...], (((0,), (0,)), ((), ())), preferred_element_type=f32
    )
    if len(streams_out.shape) == 3:
        blocks = streams_out.shape[0]
        parts = [projected[s * width : (s + 1) * width] for s in range(3)] + [out_grad]
        parts = [part.reshape(blocks, width // blocks, row_count) for part in parts]
        streams_out[...] = jnp.concatenate(parts, axis=1).astype(bf16)
    else:
        streams_out[: 3 * width] = projected.astype(bf16)
        streams_out[3 * width :] = out_grad.astype(bf16)
    own = jnp.concatenate([seq_input, cotangent[...]], axis=0)
    gather_out[...] = own


def read_signal(ref, rows):
    if ref.shape[1] == LANES:
        return ref[...]
    return jnp.concatenate(
        [ref[:, i * LANES : (i + 1) * LANES] for i in range(ref.shape[1] // LANES)], axis=0
    )


def write_signal(ref, value):
    if ref.shape[1] == LANES:
        ref[...] = value
        return
    channels = ref.shape[0]
    for i in range(ref.shape[1] // LANES):
        ref[:, i * LANES : (i + 1) * LANES] = value[i * channels : (i + 1) * channels]


def filter_kernel(
    length,
    filter_one,
    filter_two,
    table,
    twist,
    order,
    spec_one,
    spec_two,
    table_out,
    twist_out,
    order_out,
):
    rows = spec_one.shape[0]
    signals = [read_signal(filter_one, rows), read_signal(filter_two, rows)]
    first, _, second, turns = tables_of(table, twist)
    one, two = forward(signals, first, second, turns)
    spec_one[...] = jnp.concatenate(one, axis=1) * (1.0 / length)
    spec_two[...] = jnp.concatenate(two, axis=1) * (1.0 / length)
    table_out[...] = table[...]
    twist_out[...] = twist[...]
    order_out[...] = order[...]


def stack_kernel(after, *refs):
    *sources, out = refs
    for i, source in enumerate(sources):
        out[i] = source[...]


def shifted(value, steps, channels):
    if steps == 0:
        return value
    rows, lanes = value.shape
    lane = lax.broadcasted_iota(jnp.int32, value.shape, 1)
    row = lax.broadcasted_iota(jnp.int32, value.shape, 0)
    turned = pltpu.roll(value, steps % lanes, 1)
    if steps > 0:
        carried = jnp.where(row < channels, 0.0, pltpu.roll(turned, channels, 0))
        return jnp.where(lane < steps, carried, turned)
    carried = jnp.where(row >= rows - channels, 0.0, pltpu.roll(turned, rows - channels, 0))
    return jnp.where(lane >= lanes + steps, carried, turned)


def mix_kernel(
    channels,
    scale,
    streams,
    taps,
    spec_one,
    spec_two,
    table,
    twist,
    line,
    short_out,
    product_one,
    product_two,
    *sent_out,
):
    rows = twist.shape[0]
    eight = taps.shape[0]
    first, back, second, twist = tables_of(table, twist)
    if streams.shape[0] == 4 and streams.shape[1] == rows:
        pieces = [streams[s].astype(f32) for s in range(4)]
    else:
        whole = streams[...].astype(f32)
        pieces = [
            whole[:, s * channels : (s + 1) * channels].reshape(rows, LANES) for s in range(4)
        ]
    out_grad = pieces[3]

    def tap(s, k):
        column = jnp.broadcast_to(taps[:, 3 * s + k : 3 * s + k + 1], (eight, LANES))
        column = jnp.broadcast_to(column[None], (rows // eight, eight, LANES))
        return column.reshape(rows, LANES)

    late = [[shifted(pieces[s], k, channels) for k in range(3)] for s in range(3)]
    value, gate_one, gate_two = [
        sum(tap(s, k) * late[s][k] for k in range(3)) for s in range(3)
    ]
    h_one = (spec_one[:, :LANES], spec_one[:, LANES:])
    h_two = (spec_two[:, :LANES], spec_two[:, LANES:])
    value_spec, second_spec = forward([value, out_grad * gate_two], first, second, twist)
    first_mix, grad_first_out = backward(
        [times(h_one, value_spec), conj_times(h_two, second_spec)],
        back,
        second,
        twist,
    )
    first_spec, grad_first_spec = forward(
        [gate_one * first_mix, gate_one * grad_first_out], first, second, twist
    )
    second_mix, grad_value = backward(
        [times(h_two, first_spec), conj_times(h_one, grad_first_spec)],
        back,
        second,
        twist,
    )
    product_one[...] = jnp.concatenate(conj_times(value_spec, grad_first_spec), axis=1)
    product_two[...] = jnp.concatenate(conj_times(first_spec, second_spec), axis=1)
    grads = [grad_value, grad_first_out * first_mix, out_grad * second_mix]
    sent = []
    lane = lax.broadcasted_iota(jnp.int32, (eight, LANES), 1)
    short = jnp.zeros((eight, LANES), f32)
    for s in range(3):
        sent.append(sum(tap(s, k) * shifted(grads[s], -k, channels) for k in range(3)))
        for k in range(3):
            folded = (grads[s] * late[s][k]).reshape(rows // eight, eight, LANES).sum(axis=0)
            total = jnp.sum(folded, axis=1, keepdims=True) * scale
            short = jnp.where(lane == 3 * s + k, total, short)
    sent.append(gate_two * second_mix)
    short_out[...] = short
    if len(sent_out) == 1:
        for s in range(4):
            sent_out[0][s] = sent[s].astype(bf16)
        return
    parts = [part.reshape(rows // channels, channels, LANES) for part in sent]
    packed = jnp.concatenate(parts, axis=1).astype(bf16)
    *sent_out, store = sent_out
    lines, plane = store.shape[:2]
    for i in range(lines):
        store[i] = packed[i * plane : (i + 1) * plane]
    for step in range(lines):
        sent_out[step][...] = store[lax.rem(line[0] + step, lines)]


def filter_grads_kernel(
    scale, product_one, product_two, table, twist, short, grad_one, grad_two, short_out
):
    _, back, second, twist = tables_of(table, twist)
    spectra = [(ref[:, :LANES], ref[:, LANES:]) for ref in (product_one, product_two)]
    one, two = backward(spectra, back, second, twist)
    write_signal(grad_one, one * scale)
    write_signal(grad_two, two * scale)
    short_out[...] = short[...]


def member(at, k):
    return jnp.bitwise_xor(at, k)


def weights_kernel(channels, scale, lines, *refs):
    line, place, short, *met, across, over, partial_out = refs
    pieces = [over[0], across[0]]
    for i in range(1, across.shape[0]):
        pieces += [across[i], over[i]]
    plane, width = len(pieces), across.shape[1] // 2
    height = 4 * channels
    total = jnp.zeros((lines * height, 2 * width), f32)
    step = 2 if plane % 2 == 0 else 1
    for i in range(0, plane, step):
        left = jnp.concatenate(
            [
                jnp.concatenate([m[member(place[0], i + j)] for m in met], axis=0)
                for j in range(step)
            ],
            axis=1,
        )
        right = jnp.concatenate([pieces[i + j] for j in range(step)], axis=1)
        total = total + lax.dot_general(
            left, right, (((1,), (1,)), ((), ())), preferred_element_type=f32
        )
    total = total * scale
    size = height * (width // LANES)
    for k in range(lines):
        parts = []
        for h in range(width // LANES):
            low, high = h * LANES, (h + 1) * LANES
            base = k * height
            parts.append(total[base : base + 3 * channels, low:high])
            parts.append(total[base + 3 * channels : base + height, width + low : width + high])
        owner = lax.rem(line[0] + lines - k, lines)
        spot = pl.ds(pl.multiple_of(owner * size, size), size)
        partial_out[spot] = jnp.concatenate(parts, axis=0).astype(bf16)
    tail = jnp.concatenate([short[...]] * lines, axis=0)
    owner = lax.broadcasted_iota(jnp.int32, tail.shape, 0) // channels
    partial_out[lines * size :] = jnp.where(owner == line[0], tail, 0.0).astype(bf16)


def return_kernel(channels, *refs):
    *met, after, moved_out = refs
    parts = [m[...].astype(f32)[:, : 3 * channels] for m in met]
    moved_out[...] = jnp.concatenate(parts, axis=1).astype(bf16)


def sum_kernel(*refs):
    *partials, out = refs
    out[...] = sum(part[...].astype(f32) for part in partials).astype(bf16)


def unorder(grad_projected, w_in, order):
    grad_seq = lax.dot_general(
        w_in, grad_projected, (((0,), (0,)), ((), ())), preferred_element_type=f32
    ).astype(bf16)
    return lax.dot_general(
        grad_seq, one_hot(order), (((1,), (1,)), ((), ())), preferred_element_type=f32
    ).astype(bf16)


def moved_kernel(channels, lines, line, back, w_in, order, features_out, store):
    plane, width = back.shape[0], w_in.shape[1]
    share = plane * channels
    whole = back[...].astype(f32)
    for k in range(lines):
        owner = lax.rem(line[0] + lines - k, lines)
        for s in range(3):
            start = (3 * k + s) * channels
            spot = pl.ds(pl.multiple_of(s * width + owner * share, share), share)
            store[spot] = whole[:, start : start + channels].reshape(share, LANES)
    features_out[...] = unorder(store[...].astype(bf16), w_in[...], order[...])


def finish_kernel(channels, lines, place, *refs):
    *pieces, w_in_out, w_out_out, short_out, out_rows, short_rows = refs
    width = w_out_out.shape[0]
    share = width // lines
    height = 4 * channels
    size = height * (width // LANES)
    for k, piece in enumerate(pieces):
        rows = piece[...].astype(f32)
        for i in range(lines):
            first = pl.multiple_of(i * share + member(place[0], k) * channels, channels)
            for h in range(width // LANES):
                low, high = h * LANES, (h + 1) * LANES
                base = i * size + h * height
                for s in range(3):
                    spot = pl.ds(pl.multiple_of(s * width + first, channels), channels)
                    start = base + s * channels
                    w_in_out[spot, low:high] = rows[start : start + channels]
                start = base + 3 * channels
                out_rows[pl.ds(first, channels), low:high] = rows[start : start + channels]
            start = lines * size + i * channels
            short_rows[pl.ds(first, channels), :] = rows[start : start + channels]
    w_out_out[...] = out_rows[...].T
    short = short_rows[...].T
    for s in range(3):
        short_out[:, s * width : (s + 1) * width] = short[3 * s : 3 * s + 3, :]


def features_kernel(moved, w_in, order, features_out):
    features_out[...] = unorder(moved[...], w_in[...], order[...])


def swapped(value, plane, distance):
    return lax.ppermute(value, "fft", [(i, i ^ distance) for i in range(plane)])


def spread(value, plane):
    pieces = [value if k == 0 else swapped(value, plane, k) for k in range(0, plane, 2)]
    return [piece for own in pieces for piece in (own, swapped(own, plane, 1))]


def shape(dims, dtype=f32):
    return jax.ShapeDtypeStruct(dims, dtype)


def local(features, sink_order, cotangent, w_in, short_taps, w_out, filter_one, filter_two):
    width, row_count = features.shape
    lines, plane = lax.axis_size("seq"), lax.axis_size("fft")
    blocks = lines * plane
    channels, length = filter_one.shape
    rows = channels * blocks
    scale = 1.0 / math.sqrt(length)
    whole = channels % 8 == 0 and plane % 2 == 0 and plane & (plane - 1) == 0
    table, twist = make_tables(blocks, channels)
    eight = channels if whole else 8
    mine = lax.axis_index(AXES)

    def call(kernel, outs, *args, **options):
        return pl.pallas_call(kernel, out_shape=outs, compiler_params=PARAMS, **options)(*args)

    dims = (blocks, 4 * channels, LANES) if whole else (4 * width, LANES)
    streams, own = pl.pallas_call(
        project_kernel,
        out_shape=(shape(dims, bf16), shape((2 * width, row_count), bf16)),
        in_specs=[pl.BlockSpec(memory_space=pl.ANY)] * 5,
        scratch_shapes=[
            pltpu.VMEM(a.shape, a.dtype)
            for a in (features, sink_order, cotangent, w_in, w_out)
        ]
        + [pltpu.SemaphoreType.DMA((5,))],
        compiler_params=pltpu.CompilerParams(vmem_limit_bytes=60 * 1024 * 1024),
    )(features, sink_order, cotangent, w_in, w_out)
    if not whole:
        streams = streams.reshape(4, blocks, channels, LANES).transpose(1, 0, 2, 3)
        streams = streams.reshape(blocks, 4 * channels, LANES)
    arrived = lax.all_to_all(streams, AXES, split_axis=0, concat_axis=0, tiled=True)
    taps = lax.dynamic_slice_in_dim(short_taps.reshape(3, width, 3), mine * channels, channels, 1)
    taps = taps.transpose(1, 0, 2).reshape(channels, 9)
    if not whole:
        taps = jnp.tile(taps, (8 // channels, 1))
        arrived = arrived.reshape(blocks, 4, channels, LANES).transpose(1, 0, 2, 3)
        arrived = arrived.reshape(4, rows, LANES)
        filter_one, filter_two = [
            h.reshape(channels, blocks, LANES).transpose(1, 0, 2).reshape(rows, LANES)
            for h in (filter_one, filter_two)
        ]
    spec = shape((rows, 2 * LANES))
    spec_one, spec_two, table, twist, order = call(
        lambda *refs: filter_kernel(length, *refs),
        (
            spec,
            spec,
            shape(table.shape, bf16),
            shape(twist.shape),
            shape(sink_order.shape, jnp.int32),
        ),
        filter_one,
        filter_two,
        table,
        twist,
        sink_order,
    )
    line = lax.axis_index("seq").astype(jnp.int32).reshape(1)
    place = lax.axis_index("fft").astype(jnp.int32).reshape(1)
    scalar = pl.BlockSpec(memory_space=pltpu.SMEM)
    held = pl.BlockSpec(memory_space=pltpu.VMEM)
    chunk = (plane, 4 * channels, LANES)
    dims = [shape(chunk, bf16)] * lines if whole else [shape((4, rows, LANES), bf16)]
    short, product_one, product_two, *sent = call(
        lambda *refs: mix_kernel(channels, scale, *refs),
        (shape((eight, LANES)), spec, spec, *dims),
        arrived,
        taps,
        spec_one,
        spec_two,
        table,
        twist,
        line,
        in_specs=[held] * 6 + [scalar],
        scratch_shapes=[pltpu.VMEM((lines, *chunk), bf16)] if whole else [],
    )
    if whole:
        across = [swapped(own, plane, k) for k in (1, *range(2, plane, 2))]
        across = call(stack_kernel, shape((len(across), *own.shape), bf16), short, *across)
        pieces = (across, swapped(across, plane, 1))
    grad_one, grad_two, short = call(
        lambda *refs: filter_grads_kernel(scale / length, *refs),
        (shape(filter_one.shape), shape(filter_two.shape), shape(short.shape)),
        product_one,
        product_two,
        table,
        twist,
        short,
    )
    height = channels * 4 * (width // LANES)
    if whole:
        def ahead(value, steps):
            pairs = [(i, (i + steps) % lines) for i in range(lines)]
            return lax.ppermute(value, "seq", pairs)

        met = [sent[0]] + [ahead(sent[k], k) for k in range(1, lines)]
        size = lines * height + lines * channels
        partial = call(
            lambda *refs: weights_kernel(channels, scale, lines, *refs),
            shape((size, LANES), bf16),
            line,
            place,
            short,
            *met,
            *pieces,
            in_specs=[scalar] * 2 + [held] * (1 + lines + len(pieces)),
        )
        moved = call(
            lambda *refs: return_kernel(channels, *refs),
            shape((plane, 3 * lines * channels, LANES), bf16),
            *met,
            partial,
        )
        partials = [partial] + [ahead(partial, k) for k in range(1, lines)]
        back = lax.all_to_all(moved, "fft", split_axis=0, concat_axis=0, tiled=True)
        grad_features = call(
            lambda *refs: moved_kernel(channels, lines, *refs),
            shape(features.shape, bf16),
            line,
            back,
            w_in,
            order,
            in_specs=[scalar] + [held] * 3,
            scratch_shapes=[pltpu.VMEM((3 * width, LANES), f32)],
        )
        rows_sum = call(sum_kernel, shape((size, LANES), bf16), *partials)
        grad_w_in, grad_w_out, short = call(
            lambda *refs: finish_kernel(channels, lines, *refs),
            (shape((3 * width, width)), shape((width, width)), shape((3, 3 * width))),
            place,
            *spread(rows_sum, plane),
            in_specs=[scalar] + [held] * plane,
            scratch_shapes=[pltpu.VMEM((width, width), f32), pltpu.VMEM((width, LANES), f32)],
        )
        return (grad_features, grad_w_in, grad_w_out, short.T, grad_one, grad_two)
    gathered = lax.all_gather(own, AXES, axis=0, tiled=False)
    sent = sent[0]
    sent = sent.reshape(4, blocks, channels, LANES)
    grad_in = jnp.einsum(
        "sbcp,bwp->scw", sent[:3], gathered[:, :width], preferred_element_type=f32
    )
    grad_out = jnp.einsum(
        "bcp,bwp->cw", sent[3], gathered[:, width:], preferred_element_type=f32
    )
    own = jnp.concatenate([grad_in, grad_out[None]]) * scale
    own = own.reshape(height, LANES)
    short = short.reshape(8 // channels, channels, LANES).sum(axis=0)
    own = jnp.concatenate([own, short]).astype(bf16)
    moved = sent[:3].transpose(1, 0, 2, 3).reshape(blocks, 3 * channels, LANES)
    own = jnp.broadcast_to(own[None], (blocks,) + own.shape)
    packed = jnp.concatenate([moved, own], axis=1)
    back = lax.all_to_all(packed, AXES, split_axis=0, concat_axis=0, tiled=True)
    moved = back[:, : 3 * channels].reshape(blocks, 3, channels, LANES)
    moved = moved.transpose(1, 0, 2, 3).reshape(3 * width, LANES)
    weights = back[:, 3 * channels : 3 * channels + height].astype(f32)
    weights = weights.reshape(blocks, 4, channels, width).transpose(1, 0, 2, 3)
    weights = weights.reshape(4 * width, width)
    short = back[:, 3 * channels + height :, :9].astype(f32).reshape(width, 3, 3)
    short = short.transpose(1, 0, 2).reshape(3 * width, 3)
    grad_features = call(
        features_kernel, shape(features.shape, bf16), moved, w_in, sink_order
    )
    grad_one, grad_two = [
        g.reshape(blocks, channels, LANES).transpose(1, 0, 2).reshape(channels, length)
        for g in (grad_one, grad_two)
    ]
    return (
        grad_features,
        weights[: 3 * width],
        weights[3 * width :].T,
        short,
        grad_one,
        grad_two,
    )


def solution(mesh):
    columns, blocks_first, copied = P(None, AXES), P(AXES, None), P()
    return jax.shard_map(
        local,
        mesh=mesh,
        in_specs=(
            columns,
            blocks_first,
            columns,
            copied,
            copied,
            copied,
            blocks_first,
            blocks_first,
        ),
        out_specs=(columns, copied, copied, copied, blocks_first, blocks_first),
        check_vma=False,
    )
```

```python
import math

import jax
import jax.numpy as jnp
import numpy as np
from jax import lax
from jax.experimental import pallas as pl
from jax.experimental.pallas import tpu as pltpu
from jax.sharding import PartitionSpec as P

AXES = ("seq", "fft")
LANES = 128
TAPS = 16
bf16 = jnp.bfloat16
f32 = jnp.float32
PARAMS = pltpu.CompilerParams(vmem_limit_bytes=24 * 1024 * 1024)


def halves(table):
    high = table.astype(np.float32).astype(jnp.bfloat16)
    low = (table - high.astype(np.float64)).astype(np.float32).astype(jnp.bfloat16)
    return high, low


def make_tables(count, channels):
    length = count * LANES
    outer = np.arange(count, dtype=np.float64) + 0.25
    inner = np.arange(LANES, dtype=np.float64)
    angle = 2.0 * np.pi * outer[:, None] * outer[None, :] / count
    first = np.kron(np.concatenate([np.cos(angle), np.sin(angle)], axis=0), np.eye(channels))
    turn = 2.0 * np.pi * (inner[:, None] * inner[None, :] % LANES) / LANES
    cos, sin = np.cos(turn), np.sin(turn)
    second = np.block([[cos, -sin], [sin, cos]])
    packed = [half for t in (first, second) for half in halves(t)]
    twist = 2.0 * np.pi * outer[:, None] * (inner[None, :] - LANES / 4) / length
    twist = np.repeat(twist, channels, axis=0)
    twist = np.concatenate([np.cos(twist), -np.sin(twist)], axis=1).astype(np.float32)
    return np.concatenate(packed, axis=0), twist


def tables_of(table, twist):
    rows = twist.shape[0]
    at, found = 0, []
    for size in (2 * rows, 2 * LANES):
        pair = []
        for half in range(2):
            pair.append(table[at : at + size])
            at += size
        found.append(tuple(pair))
    first, second = found
    back = tuple(jnp.concatenate([t[:rows], t[rows:]], axis=1) for t in first)
    return first, back, second, (twist[:, :LANES], twist[:, LANES:])


def split(value):
    high = value.astype(bf16)
    low = (value - high.astype(f32)).astype(bf16)
    return high, low


def dot(left, right):
    return jnp.dot(left, right, preferred_element_type=f32)


def dot_pairs(left, right):
    deep_left = jnp.concatenate([left[0], left[0], left[1]], axis=1)
    deep_right = jnp.concatenate([right[0], right[1], right[0]], axis=0)
    return dot(deep_left, deep_right)


def forward(signals, first, second, twist):
    rows = signals[0].shape[0]
    stage = dot_pairs(first, split(jnp.concatenate(signals, axis=1)))
    parts = []
    for i in range(len(signals)):
        cos = stage[:rows, i * LANES : (i + 1) * LANES]
        sin = stage[rows:, i * LANES : (i + 1) * LANES]
        parts.append(
            jnp.concatenate(
                [cos * twist[0] + sin * twist[1], cos * twist[1] - sin * twist[0]], axis=1
            )
        )
    specs = [dot_pairs(split(part), second) for part in parts]
    return [(spec[:, :LANES], spec[:, LANES:]) for spec in specs]


def backward(spectra, back, second, twist):
    parts = []
    for pair in spectra:
        stage = dot_pairs(split(jnp.concatenate(pair, axis=1)), second)
        re, im = stage[:, :LANES], stage[:, LANES:]
        parts.append(
            jnp.concatenate(
                [re * twist[0] - im * twist[1], re * twist[1] + im * twist[0]], axis=0
            )
        )
    out = dot_pairs(back, split(jnp.concatenate(parts, axis=1)))
    return [out[:, i * LANES : (i + 1) * LANES] for i in range(len(spectra))]


def times(a, b):
    return (a[0] * b[0] - a[1] * b[1], -(a[0] * b[1] + a[1] * b[0]))


def conj_times(a, b):
    return (a[0] * b[0] + a[1] * b[1], a[1] * b[0] - a[0] * b[1])


def one_hot(order):
    size = order.shape[1]
    place = lax.broadcasted_iota(jnp.int32, (size, size), 0)
    return (place == order).astype(f32).astype(bf16)


def project_kernel(
    features_at,
    order_at,
    cotangent_at,
    w_in_at,
    w_out_at,
    streams_out,
    gather_out,
    features,
    order,
    cotangent,
    w_in,
    w_out,
    done,
):
    copies = [
        pltpu.make_async_copy(source, target, done.at[i])
        for i, (source, target) in enumerate(
            [
                (order_at, order),
                (features_at, features),
                (w_in_at, w_in),
                (cotangent_at, cotangent),
                (w_out_at, w_out),
            ]
        )
    ]
    for copy in copies:
        copy.start()
    width, row_count = features.shape
    copies[0].wait()
    copies[1].wait()
    seq_input = dot(features[...], one_hot(order[...])).astype(bf16)
    copies[2].wait()
    projected = dot(w_in[...], seq_input)
    copies[3].wait()
    copies[4].wait()
    out_grad = lax.dot_general(
        w_out[...], cotangent[...], (((0,), (0,)), ((), ())), preferred_element_type=f32
    )
    if len(streams_out.shape) == 3:
        blocks = streams_out.shape[0]
        parts = [projected[s * width : (s + 1) * width] for s in range(3)] + [out_grad]
        parts = [part.reshape(blocks, width // blocks, row_count) for part in parts]
        streams_out[...] = jnp.concatenate(parts, axis=1).astype(bf16)
    else:
        streams_out[: 3 * width] = projected.astype(bf16)
        streams_out[3 * width :] = out_grad.astype(bf16)
    own = jnp.concatenate([seq_input, cotangent[...]], axis=0)
    gather_out[...] = own


def read_signal(ref, rows):
    if ref.shape[1] == LANES:
        return ref[...]
    return jnp.concatenate(
        [ref[:, i * LANES : (i + 1) * LANES] for i in range(ref.shape[1] // LANES)], axis=0
    )


def write_signal(ref, value):
    if ref.shape[1] == LANES:
        ref[...] = value
        return
    channels = ref.shape[0]
    for i in range(ref.shape[1] // LANES):
        ref[:, i * LANES : (i + 1) * LANES] = value[i * channels : (i + 1) * channels]


def filter_kernel(
    length,
    filter_one,
    filter_two,
    table,
    twist,
    order,
    spec_one,
    spec_two,
    table_out,
    twist_out,
    order_out,
):
    rows = spec_one.shape[0]
    signals = [read_signal(filter_one, rows), read_signal(filter_two, rows)]
    first, _, second, turns = tables_of(table, twist)
    one, two = forward(signals, first, second, turns)
    spec_one[...] = jnp.concatenate(one, axis=1) * (1.0 / length)
    spec_two[...] = jnp.concatenate(two, axis=1) * (1.0 / length)
    table_out[...] = table[...]
    twist_out[...] = twist[...]
    order_out[...] = order[...]


def stack_kernel(after, *refs):
    *sources, out = refs
    for i, source in enumerate(sources):
        out[i] = source[...]


def shifted(value, steps, channels):
    if steps == 0:
        return value
    rows, lanes = value.shape
    lane = lax.broadcasted_iota(jnp.int32, value.shape, 1)
    row = lax.broadcasted_iota(jnp.int32, value.shape, 0)
    turned = pltpu.roll(value, steps % lanes, 1)
    if steps > 0:
        carried = jnp.where(row < channels, 0.0, pltpu.roll(turned, channels, 0))
        return jnp.where(lane < steps, carried, turned)
    carried = jnp.where(row >= rows - channels, 0.0, pltpu.roll(turned, rows - channels, 0))
    return jnp.where(lane >= lanes + steps, carried, turned)


def mix_kernel(
    channels,
    scale,
    streams,
    taps,
    spec_one,
    spec_two,
    table,
    twist,
    line,
    short_out,
    product_one,
    product_two,
    *sent_out,
):
    rows = twist.shape[0]
    eight = taps.shape[0]
    first, back, second, twist = tables_of(table, twist)
    if streams.shape[0] == 4 and streams.shape[1] == rows:
        pieces = [streams[s].astype(f32) for s in range(4)]
    else:
        whole = streams[...].astype(f32)
        pieces = [
            whole[:, s * channels : (s + 1) * channels].reshape(rows, LANES) for s in range(4)
        ]
    out_grad = pieces[3]

    def tap(s, k):
        column = jnp.broadcast_to(taps[:, 3 * s + k : 3 * s + k + 1], (eight, LANES))
        column = jnp.broadcast_to(column[None], (rows // eight, eight, LANES))
        return column.reshape(rows, LANES)

    late = [[shifted(pieces[s], k, channels) for k in range(3)] for s in range(3)]
    value, gate_one, gate_two = [
        sum(tap(s, k) * late[s][k] for k in range(3)) for s in range(3)
    ]
    h_one = (spec_one[:, :LANES], spec_one[:, LANES:])
    h_two = (spec_two[:, :LANES], spec_two[:, LANES:])

    def spectrum(signal):
        return forward([signal], first, second, twist)[0]

    def signal_of(spec):
        return backward([spec], back, second, twist)[0]

    value_spec, second_spec = spectrum(value), spectrum(out_grad * gate_two)
    first_mix = signal_of(times(h_one, value_spec))
    grad_first_out = signal_of(conj_times(h_two, second_spec))
    first_spec = spectrum(gate_one * first_mix)
    grad_first_spec = spectrum(gate_one * grad_first_out)
    second_mix = signal_of(times(h_two, first_spec))
    grad_value = signal_of(conj_times(h_one, grad_first_spec))
    product_one[...] = jnp.concatenate(conj_times(value_spec, grad_first_spec), axis=1)
    product_two[...] = jnp.concatenate(conj_times(first_spec, second_spec), axis=1)
    grads = [grad_value, grad_first_out * first_mix, out_grad * second_mix]
    sent = []
    lane = lax.broadcasted_iota(jnp.int32, (eight, LANES), 1)
    short = jnp.zeros((eight, LANES), f32)
    for s in range(3):
        sent.append(sum(tap(s, k) * shifted(grads[s], -k, channels) for k in range(3)))
        for k in range(3):
            folded = (grads[s] * late[s][k]).reshape(rows // eight, eight, LANES).sum(axis=0)
            total = jnp.sum(folded, axis=1, keepdims=True) * scale
            short = jnp.where(lane == 3 * s + k, total, short)
    sent.append(gate_two * second_mix)
    short_out[...] = short
    if len(sent_out) == 1:
        for s in range(4):
            sent_out[0][s] = sent[s].astype(bf16)
        return
    parts = [part.reshape(rows // channels, channels, LANES) for part in sent]
    packed = jnp.concatenate(parts, axis=1).astype(bf16)
    *sent_out, store = sent_out
    lines, plane = store.shape[:2]
    for i in range(lines):
        store[i] = packed[i * plane : (i + 1) * plane]
    for step in range(lines):
        sent_out[step][...] = store[lax.rem(line[0] + step, lines)]


def filter_grads_kernel(
    scale, product_one, product_two, table, twist, short, grad_one, grad_two, short_out
):
    _, back, second, twist = tables_of(table, twist)
    spectra = [(ref[:, :LANES], ref[:, LANES:]) for ref in (product_one, product_two)]
    one, two = backward(spectra, back, second, twist)
    write_signal(grad_one, one * scale)
    write_signal(grad_two, two * scale)
    short_out[...] = short[...]


def member(at, k):
    return jnp.bitwise_xor(at, k)


def weights_kernel(channels, scale, lines, *refs):
    line, place, short, *met, across, over, partial_out = refs
    pieces = [over[0], across[0]]
    for i in range(1, across.shape[0]):
        pieces += [across[i], over[i]]
    plane, width = len(pieces), across.shape[1] // 2
    height = 4 * channels
    total = jnp.zeros((lines * height, 2 * width), f32)
    step = 2 if plane % 2 == 0 else 1
    for i in range(0, plane, step):
        left = jnp.concatenate(
            [
                jnp.concatenate([m[member(place[0], i + j)] for m in met], axis=0)
                for j in range(step)
            ],
            axis=1,
        )
        right = jnp.concatenate([pieces[i + j] for j in range(step)], axis=1)
        total = total + lax.dot_general(
            left, right, (((1,), (1,)), ((), ())), preferred_element_type=f32
        )
    total = total * scale
    size = height * (width // LANES)
    for k in range(lines):
        parts = []
        for h in range(width // LANES):
            low, high = h * LANES, (h + 1) * LANES
            base = k * height
            parts.append(total[base : base + 3 * channels, low:high])
            parts.append(total[base + 3 * channels : base + height, width + low : width + high])
        owner = lax.rem(line[0] + lines - k, lines)
        spot = pl.ds(pl.multiple_of(owner * size, size), size)
        partial_out[spot] = jnp.concatenate(parts, axis=0).astype(bf16)
    tail = pltpu.roll(short[...], line[0] * TAPS, 1)
    tail = jnp.concatenate([tail, jnp.zeros_like(tail)], axis=0)
    partial_out[lines * size :] = tail.astype(bf16)


def return_kernel(channels, *refs):
    *met, after, moved_out = refs
    parts = [m[...].astype(f32)[:, : 3 * channels] for m in met]
    moved_out[...] = jnp.concatenate(parts, axis=1).astype(bf16)


def sum_kernel(*refs):
    *partials, out = refs
    out[...] = sum(part[...].astype(f32) for part in partials).astype(bf16)


def unorder(grad_projected, w_in, order):
    grad_seq = lax.dot_general(
        w_in, grad_projected, (((0,), (0,)), ((), ())), preferred_element_type=f32
    ).astype(bf16)
    return lax.dot_general(
        grad_seq, one_hot(order), (((1,), (1,)), ((), ())), preferred_element_type=f32
    ).astype(bf16)


def moved_kernel(channels, lines, line, back, w_in, order, features_out, store):
    plane, width = back.shape[0], w_in.shape[1]
    share = plane * channels
    whole = back[...].astype(f32)
    for k in range(lines):
        owner = lax.rem(line[0] + lines - k, lines)
        for s in range(3):
            start = (3 * k + s) * channels
            spot = pl.ds(pl.multiple_of(s * width + owner * share, share), share)
            store[spot] = whole[:, start : start + channels].reshape(share, LANES)
    features_out[...] = unorder(store[...].astype(bf16), w_in[...], order[...])


def finish_kernel(channels, lines, place, *refs):
    *pieces, w_in_out, w_out_out, short_out, out_rows, short_rows = refs
    width = w_out_out.shape[0]
    share = width // lines
    height = 4 * channels
    size = height * (width // LANES)
    for k, piece in enumerate(pieces):
        rows = piece[...].astype(f32)
        for i in range(lines):
            first = pl.multiple_of(i * share + member(place[0], k) * channels, channels)
            for h in range(width // LANES):
                low, high = h * LANES, (h + 1) * LANES
                base = i * size + h * height
                for s in range(3):
                    spot = pl.ds(pl.multiple_of(s * width + first, channels), channels)
                    start = base + s * channels
                    w_in_out[spot, low:high] = rows[start : start + channels]
                start = base + 3 * channels
                out_rows[pl.ds(first, channels), low:high] = rows[start : start + channels]
            start = lines * size
            short_rows[pl.ds(first, channels), :] = pltpu.roll(
                rows[start : start + channels], (LANES - i * TAPS) % LANES, 1
            )
    w_out_out[...] = out_rows[...].T
    short = short_rows[...].T
    for s in range(3):
        short_out[:, s * width : (s + 1) * width] = short[3 * s : 3 * s + 3, :]


def features_kernel(moved, w_in, order, features_out):
    features_out[...] = unorder(moved[...], w_in[...], order[...])


def swapped(value, plane, distance):
    return lax.ppermute(value, "fft", [(i, i ^ distance) for i in range(plane)])


def spread(value, plane):
    pieces = [value if k == 0 else swapped(value, plane, k) for k in range(0, plane, 2)]
    return [piece for own in pieces for piece in (own, swapped(own, plane, 1))]


def shape(dims, dtype=f32):
    return jax.ShapeDtypeStruct(dims, dtype)


def local(features, sink_order, cotangent, w_in, short_taps, w_out, filter_one, filter_two):
    width, row_count = features.shape
    lines, plane = lax.axis_size("seq"), lax.axis_size("fft")
    blocks = lines * plane
    channels, length = filter_one.shape
    rows = channels * blocks
    scale = 1.0 / math.sqrt(length)
    whole = channels % 8 == 0 and plane % 2 == 0 and plane & (plane - 1) == 0
    table, twist = make_tables(blocks, channels)
    eight = channels if whole else 8
    mine = lax.axis_index(AXES)

    def call(kernel, outs, *args, **options):
        return pl.pallas_call(kernel, out_shape=outs, compiler_params=PARAMS, **options)(*args)

    dims = (blocks, 4 * channels, LANES) if whole else (4 * width, LANES)
    streams, own = pl.pallas_call(
        project_kernel,
        out_shape=(shape(dims, bf16), shape((2 * width, row_count), bf16)),
        in_specs=[pl.BlockSpec(memory_space=pl.ANY)] * 5,
        scratch_shapes=[
            pltpu.VMEM(a.shape, a.dtype)
            for a in (features, sink_order, cotangent, w_in, w_out)
        ]
        + [pltpu.SemaphoreType.DMA((5,))],
        compiler_params=pltpu.CompilerParams(vmem_limit_bytes=60 * 1024 * 1024),
    )(features, sink_order, cotangent, w_in, w_out)
    if not whole:
        streams = streams.reshape(4, blocks, channels, LANES).transpose(1, 0, 2, 3)
        streams = streams.reshape(blocks, 4 * channels, LANES)
    arrived = lax.all_to_all(streams, AXES, split_axis=0, concat_axis=0, tiled=True)
    taps = lax.dynamic_slice_in_dim(short_taps.reshape(3, width, 3), mine * channels, channels, 1)
    taps = taps.transpose(1, 0, 2).reshape(channels, 9)
    if not whole:
        taps = jnp.tile(taps, (8 // channels, 1))
        arrived = arrived.reshape(blocks, 4, channels, LANES).transpose(1, 0, 2, 3)
        arrived = arrived.reshape(4, rows, LANES)
        filter_one, filter_two = [
            h.reshape(channels, blocks, LANES).transpose(1, 0, 2).reshape(rows, LANES)
            for h in (filter_one, filter_two)
        ]
    spec = shape((rows, 2 * LANES))
    spec_one, spec_two, table, twist, order = call(
        lambda *refs: filter_kernel(length, *refs),
        (
            spec,
            spec,
            shape(table.shape, bf16),
            shape(twist.shape),
            shape(sink_order.shape, jnp.int32),
        ),
        filter_one,
        filter_two,
        table,
        twist,
        sink_order,
    )
    line = lax.axis_index("seq").astype(jnp.int32).reshape(1)
    place = lax.axis_index("fft").astype(jnp.int32).reshape(1)
    scalar = pl.BlockSpec(memory_space=pltpu.SMEM)
    held = pl.BlockSpec(memory_space=pltpu.VMEM)
    chunk = (plane, 4 * channels, LANES)
    dims = [shape(chunk, bf16)] * lines if whole else [shape((4, rows, LANES), bf16)]
    short, product_one, product_two, *sent = call(
        lambda *refs: mix_kernel(channels, scale, *refs),
        (shape((eight, LANES)), spec, spec, *dims),
        arrived,
        taps,
        spec_one,
        spec_two,
        table,
        twist,
        line,
        in_specs=[held] * 6 + [scalar],
        scratch_shapes=[pltpu.VMEM((lines, *chunk), bf16)] if whole else [],
    )
    if whole:
        across = [swapped(own, plane, k) for k in (1, *range(2, plane, 2))]
        across = call(stack_kernel, shape((len(across), *own.shape), bf16), short, *across)
        pieces = (across, swapped(across, plane, 1))
    grad_one, grad_two, short = call(
        lambda *refs: filter_grads_kernel(scale / length, *refs),
        (shape(filter_one.shape), shape(filter_two.shape), shape(short.shape)),
        product_one,
        product_two,
        table,
        twist,
        short,
    )
    height = channels * 4 * (width // LANES)
    if whole:
        def ahead(value, steps):
            pairs = [(i, (i + steps) % lines) for i in range(lines)]
            return lax.ppermute(value, "seq", pairs)

        met = [sent[0]] + [ahead(sent[k], k) for k in range(1, lines)]
        size = lines * height + 2 * channels
        partial = call(
            lambda *refs: weights_kernel(channels, scale, lines, *refs),
            shape((size, LANES), bf16),
            line,
            place,
            short,
            *met,
            *pieces,
            in_specs=[scalar] * 2 + [held] * (1 + lines + len(pieces)),
        )
        moved = call(
            lambda *refs: return_kernel(channels, *refs),
            shape((plane, 3 * lines * channels, LANES), bf16),
            *met,
            partial,
        )
        partials = [partial] + [ahead(partial, k) for k in range(1, lines)]
        back = lax.all_to_all(moved, "fft", split_axis=0, concat_axis=0, tiled=True)
        grad_features = call(
            lambda *refs: moved_kernel(channels, lines, *refs),
            shape(features.shape, bf16),
            line,
            back,
            w_in,
            order,
            in_specs=[scalar] + [held] * 3,
            scratch_shapes=[pltpu.VMEM((3 * width, LANES), f32)],
        )
        rows_sum = call(sum_kernel, shape((size, LANES), bf16), *partials)
        grad_w_in, grad_w_out, short = call(
            lambda *refs: finish_kernel(channels, lines, *refs),
            (shape((3 * width, width)), shape((width, width)), shape((3, 3 * width))),
            place,
            *spread(rows_sum, plane),
            in_specs=[scalar] + [held] * plane,
            scratch_shapes=[pltpu.VMEM((width, width), f32), pltpu.VMEM((width, LANES), f32)],
        )
        return (grad_features, grad_w_in, grad_w_out, short.T, grad_one, grad_two)
    gathered = lax.all_gather(own, AXES, axis=0, tiled=False)
    sent = sent[0]
    sent = sent.reshape(4, blocks, channels, LANES)
    grad_in = jnp.einsum(
        "sbcp,bwp->scw", sent[:3], gathered[:, :width], preferred_element_type=f32
    )
    grad_out = jnp.einsum(
        "bcp,bwp->cw", sent[3], gathered[:, width:], preferred_element_type=f32
    )
    own = jnp.concatenate([grad_in, grad_out[None]]) * scale
    own = own.reshape(height, LANES)
    short = short.reshape(8 // channels, channels, LANES).sum(axis=0)
    own = jnp.concatenate([own, short]).astype(bf16)
    moved = sent[:3].transpose(1, 0, 2, 3).reshape(blocks, 3 * channels, LANES)
    own = jnp.broadcast_to(own[None], (blocks,) + own.shape)
    packed = jnp.concatenate([moved, own], axis=1)
    back = lax.all_to_all(packed, AXES, split_axis=0, concat_axis=0, tiled=True)
    moved = back[:, : 3 * channels].reshape(blocks, 3, channels, LANES)
    moved = moved.transpose(1, 0, 2, 3).reshape(3 * width, LANES)
    weights = back[:, 3 * channels : 3 * channels + height].astype(f32)
    weights = weights.reshape(blocks, 4, channels, width).transpose(1, 0, 2, 3)
    weights = weights.reshape(4 * width, width)
    short = back[:, 3 * channels + height :, :9].astype(f32).reshape(width, 3, 3)
    short = short.transpose(1, 0, 2).reshape(3 * width, 3)
    grad_features = call(
        features_kernel, shape(features.shape, bf16), moved, w_in, sink_order
    )
    grad_one, grad_two = [
        g.reshape(blocks, channels, LANES).transpose(1, 0, 2).reshape(channels, length)
        for g in (grad_one, grad_two)
    ]
    return (
        grad_features,
        weights[: 3 * width],
        weights[3 * width :].T,
        short,
        grad_one,
        grad_two,
    )


def solution(mesh):
    columns, blocks_first, copied = P(None, AXES), P(AXES, None), P()
    return jax.shard_map(
        local,
        mesh=mesh,
        in_specs=(
            columns,
            blocks_first,
            columns,
            copied,
            copied,
            copied,
            blocks_first,
            blocks_first,
        ),
        out_specs=(columns, copied, copied, copied, blocks_first, blocks_first),
        check_vma=False,
    )
```

```python
import math

import jax
import jax.numpy as jnp
import numpy as np
from jax import lax
from jax.experimental import pallas as pl
from jax.experimental.pallas import tpu as pltpu
from jax.sharding import PartitionSpec as P

AXES = ("seq", "fft")
LANES = 128
TAPS = 16
bf16 = jnp.bfloat16
f32 = jnp.float32
PARAMS = pltpu.CompilerParams(vmem_limit_bytes=24 * 1024 * 1024)


def halves(table):
    high = table.astype(np.float32).astype(jnp.bfloat16)
    low = (table - high.astype(np.float64)).astype(np.float32).astype(jnp.bfloat16)
    return high, low


def make_tables(count, channels):
    length = count * LANES
    outer = np.arange(count, dtype=np.float64) + 0.25
    inner = np.arange(LANES, dtype=np.float64)
    angle = 2.0 * np.pi * outer[:, None] * outer[None, :] / count
    first = np.kron(np.concatenate([np.cos(angle), np.sin(angle)], axis=0), np.eye(channels))
    turn = 2.0 * np.pi * (inner[:, None] * inner[None, :] % LANES) / LANES
    cos, sin = np.cos(turn), np.sin(turn)
    second = np.block([[cos, -sin], [sin, cos]])
    packed = [half for t in (first, second) for half in halves(t)]
    twist = 2.0 * np.pi * outer[:, None] * (inner[None, :] - LANES / 4) / length
    twist = np.repeat(twist, channels, axis=0)
    twist = np.concatenate([np.cos(twist), -np.sin(twist)], axis=1).astype(np.float32)
    return np.concatenate(packed, axis=0), twist


def tables_of(table, twist):
    rows = twist.shape[0]
    at, found = 0, []
    for size in (2 * rows, 2 * LANES):
        pair = []
        for half in range(2):
            pair.append(table[at : at + size])
            at += size
        found.append(tuple(pair))
    first, second = found
    back = tuple(jnp.concatenate([t[:rows], t[rows:]], axis=1) for t in first)
    return first, back, second, (twist[:, :LANES], twist[:, LANES:])


def split(value):
    high = value.astype(bf16)
    low = (value - high.astype(f32)).astype(bf16)
    return high, low


def dot(left, right):
    return jnp.dot(left, right, preferred_element_type=f32)


def dot_pairs(left, right):
    deep_left = jnp.concatenate([left[0], left[0], left[1]], axis=1)
    deep_right = jnp.concatenate([right[0], right[1], right[0]], axis=0)
    return dot(deep_left, deep_right)


def forward(signals, first, second, twist):
    rows = signals[0].shape[0]
    stage = dot_pairs(first, split(jnp.concatenate(signals, axis=1)))
    parts = []
    for i in range(len(signals)):
        cos = stage[:rows, i * LANES : (i + 1) * LANES]
        sin = stage[rows:, i * LANES : (i + 1) * LANES]
        parts.append(
            jnp.concatenate(
                [cos * twist[0] + sin * twist[1], cos * twist[1] - sin * twist[0]], axis=1
            )
        )
    specs = [dot_pairs(split(part), second) for part in parts]
    return [(spec[:, :LANES], spec[:, LANES:]) for spec in specs]


def backward(spectra, back, second, twist):
    parts = []
    for pair in spectra:
        stage = dot_pairs(split(jnp.concatenate(pair, axis=1)), second)
        re, im = stage[:, :LANES], stage[:, LANES:]
        parts.append(
            jnp.concatenate(
                [re * twist[0] - im * twist[1], re * twist[1] + im * twist[0]], axis=0
            )
        )
    out = dot_pairs(back, split(jnp.concatenate(parts, axis=1)))
    return [out[:, i * LANES : (i + 1) * LANES] for i in range(len(spectra))]


def times(a, b):
    return (a[0] * b[0] - a[1] * b[1], -(a[0] * b[1] + a[1] * b[0]))


def conj_times(a, b):
    return (a[0] * b[0] + a[1] * b[1], a[1] * b[0] - a[0] * b[1])


def one_hot(order):
    size = order.shape[1]
    place = lax.broadcasted_iota(jnp.int32, (size, size), 0)
    return (place == order).astype(f32).astype(bf16)


def project_kernel(
    features_at,
    order_at,
    cotangent_at,
    w_in_at,
    w_out_at,
    streams_out,
    gather_out,
    features,
    order,
    cotangent,
    w_in,
    w_out,
    done,
):
    copies = [
        pltpu.make_async_copy(source, target, done.at[i])
        for i, (source, target) in enumerate(
            [
                (order_at, order),
                (features_at, features),
                (w_in_at, w_in),
                (cotangent_at, cotangent),
                (w_out_at, w_out),
            ]
        )
    ]
    for copy in copies:
        copy.start()
    width, row_count = features.shape
    copies[0].wait()
    copies[1].wait()
    seq_input = dot(features[...], one_hot(order[...])).astype(bf16)
    copies[2].wait()
    projected = dot(w_in[...], seq_input)
    copies[3].wait()
    copies[4].wait()
    out_grad = lax.dot_general(
        w_out[...], cotangent[...], (((0,), (0,)), ((), ())), preferred_element_type=f32
    )
    if len(streams_out.shape) == 3:
        blocks = streams_out.shape[0]
        parts = [projected[s * width : (s + 1) * width] for s in range(3)] + [out_grad]
        parts = [part.reshape(blocks, width // blocks, row_count) for part in parts]
        streams_out[...] = jnp.concatenate(parts, axis=1).astype(bf16)
    else:
        streams_out[: 3 * width] = projected.astype(bf16)
        streams_out[3 * width :] = out_grad.astype(bf16)
    own = jnp.concatenate([seq_input, cotangent[...]], axis=0)
    gather_out[...] = own


def read_signal(ref, rows):
    if ref.shape[1] == LANES:
        return ref[...]
    return jnp.concatenate(
        [ref[:, i * LANES : (i + 1) * LANES] for i in range(ref.shape[1] // LANES)], axis=0
    )


def write_signal(ref, value):
    if ref.shape[1] == LANES:
        ref[...] = value
        return
    channels = ref.shape[0]
    for i in range(ref.shape[1] // LANES):
        ref[:, i * LANES : (i + 1) * LANES] = value[i * channels : (i + 1) * channels]


def filter_kernel(
    length,
    filter_one,
    filter_two,
    table,
    twist,
    order,
    spec_one,
    spec_two,
    table_out,
    twist_out,
    order_out,
):
    rows = spec_one.shape[0]
    signals = [read_signal(filter_one, rows), read_signal(filter_two, rows)]
    first, _, second, turns = tables_of(table, twist)
    one, two = forward(signals, first, second, turns)
    spec_one[...] = jnp.concatenate(one, axis=1) * (1.0 / length)
    spec_two[...] = jnp.concatenate(two, axis=1) * (1.0 / length)
    table_out[...] = table[...]
    twist_out[...] = twist[...]
    order_out[...] = order[...]


def stack_kernel(after, *refs):
    *sources, out = refs
    for i, source in enumerate(sources):
        out[i] = source[...]


def shifted(value, steps, channels):
    if steps == 0:
        return value
    rows, lanes = value.shape
    lane = lax.broadcasted_iota(jnp.int32, value.shape, 1)
    row = lax.broadcasted_iota(jnp.int32, value.shape, 0)
    turned = pltpu.roll(value, steps % lanes, 1)
    if steps > 0:
        carried = jnp.where(row < channels, 0.0, pltpu.roll(turned, channels, 0))
        return jnp.where(lane < steps, carried, turned)
    carried = jnp.where(row >= rows - channels, 0.0, pltpu.roll(turned, rows - channels, 0))
    return jnp.where(lane >= lanes + steps, carried, turned)


def mix_kernel(
    channels,
    scale,
    streams,
    taps,
    spec_one,
    spec_two,
    table,
    twist,
    line,
    short_out,
    product_one,
    product_two,
    *sent_out,
):
    rows = twist.shape[0]
    eight = taps.shape[0]
    first, back, second, twist = tables_of(table, twist)
    if streams.shape[0] == 4 and streams.shape[1] == rows:
        pieces = [streams[s].astype(f32) for s in range(4)]
    else:
        whole = streams[...].astype(f32)
        pieces = [
            whole[:, s * channels : (s + 1) * channels].reshape(rows, LANES) for s in range(4)
        ]
    out_grad = pieces[3]

    def tap(s, k):
        column = jnp.broadcast_to(taps[:, 3 * s + k : 3 * s + k + 1], (eight, LANES))
        column = jnp.broadcast_to(column[None], (rows // eight, eight, LANES))
        return column.reshape(rows, LANES)

    late = [[shifted(pieces[s], k, channels) for k in range(3)] for s in range(3)]
    value, gate_one, gate_two = [
        sum(tap(s, k) * late[s][k] for k in range(3)) for s in range(3)
    ]
    h_one = (spec_one[:, :LANES], spec_one[:, LANES:])
    h_two = (spec_two[:, :LANES], spec_two[:, LANES:])
    value_spec, second_spec = forward([value, out_grad * gate_two], first, second, twist)
    first_mix, grad_first_out = backward(
        [times(h_one, value_spec), conj_times(h_two, second_spec)],
        back,
        second,
        twist,
    )
    first_spec, grad_first_spec = forward(
        [gate_one * first_mix, gate_one * grad_first_out], first, second, twist
    )
    second_mix, grad_value = backward(
        [times(h_two, first_spec), conj_times(h_one, grad_first_spec)],
        back,
        second,
        twist,
    )
    product_one[...] = jnp.concatenate(conj_times(value_spec, grad_first_spec), axis=1)
    product_two[...] = jnp.concatenate(conj_times(first_spec, second_spec), axis=1)
    grads = [grad_value, grad_first_out * first_mix, out_grad * second_mix]
    sent = []
    lane = lax.broadcasted_iota(jnp.int32, (eight, LANES), 1)
    short = jnp.zeros((eight, LANES), f32)
    for s in range(3):
        sent.append(sum(tap(s, k) * shifted(grads[s], -k, channels) for k in range(3)))
        for k in range(3):
            folded = (grads[s] * late[s][k]).reshape(rows // eight, eight, LANES).sum(axis=0)
            total = jnp.sum(folded, axis=1, keepdims=True) * scale
            short = jnp.where(lane == 3 * s + k, total, short)
    sent.append(gate_two * second_mix)
    short_out[...] = short
    if len(sent_out) == 1:
        for s in range(4):
            sent_out[0][s] = sent[s].astype(bf16)
        return
    parts = [part.reshape(rows // channels, channels, LANES) for part in sent]
    packed = jnp.concatenate(parts, axis=1).astype(bf16)
    *sent_out, store = sent_out
    lines, plane = store.shape[:2]
    for i in range(lines):
        store[i] = packed[i * plane : (i + 1) * plane]
    for step in range(lines):
        sent_out[step][...] = store[lax.rem(line[0] + step, lines)]


def filter_grads_kernel(
    scale, product_one, product_two, table, twist, short, grad_one, grad_two, short_out
):
    _, back, second, twist = tables_of(table, twist)
    spectra = [(ref[:, :LANES], ref[:, LANES:]) for ref in (product_one, product_two)]
    one, two = backward(spectra, back, second, twist)
    write_signal(grad_one, one * scale)
    write_signal(grad_two, two * scale)
    short_out[...] = short[...]


def member(at, k):
    return jnp.bitwise_xor(at, k)


def weights_kernel(channels, scale, lines, *refs):
    line, place, short, *met, across, over, partial_out = refs
    pieces = [over[0], across[0]]
    for i in range(1, across.shape[0]):
        pieces += [across[i], over[i]]
    plane, width = len(pieces), across.shape[1] // 2
    height = 4 * channels
    total = jnp.zeros((lines * height, 2 * width), f32)
    step = 2 if plane % 2 == 0 else 1
    for i in range(0, plane, step):
        left = jnp.concatenate(
            [
                jnp.concatenate([m[member(place[0], i + j)] for m in met], axis=0)
                for j in range(step)
            ],
            axis=1,
        )
        right = jnp.concatenate([pieces[i + j] for j in range(step)], axis=1)
        total = total + lax.dot_general(
            left, right, (((1,), (1,)), ((), ())), preferred_element_type=f32
        )
    total = total * scale
    size = height * (width // LANES)
    for k in range(lines):
        parts = []
        for h in range(width // LANES):
            low, high = h * LANES, (h + 1) * LANES
            base = k * height
            parts.append(total[base : base + 3 * channels, low:high])
            parts.append(total[base + 3 * channels : base + height, width + low : width + high])
        owner = lax.rem(line[0] + lines - k, lines)
        spot = pl.ds(pl.multiple_of(owner * size, size), size)
        partial_out[spot] = jnp.concatenate(parts, axis=0).astype(bf16)
    tail = pltpu.roll(short[...], line[0] * TAPS, 1)
    tail = jnp.concatenate([tail, jnp.zeros_like(tail)], axis=0)
    partial_out[lines * size :] = tail.astype(bf16)


def return_kernel(channels, *refs):
    *met, after, moved_out = refs
    parts = [m[...].astype(f32)[:, : 3 * channels] for m in met]
    moved_out[...] = jnp.concatenate(parts, axis=1).astype(bf16)


def sum_kernel(*refs):
    *partials, out = refs
    out[...] = sum(part[...].astype(f32) for part in partials).astype(bf16)


def unorder(grad_projected, w_in, order):
    grad_seq = lax.dot_general(
        w_in, grad_projected, (((0,), (0,)), ((), ())), preferred_element_type=f32
    ).astype(bf16)
    return lax.dot_general(
        grad_seq, one_hot(order), (((1,), (1,)), ((), ())), preferred_element_type=f32
    ).astype(bf16)


def moved_kernel(channels, lines, line, back, w_in, order, features_out, store):
    plane, width = back.shape[0], w_in.shape[1]
    share = plane * channels
    whole = back[...].astype(f32)
    for k in range(lines):
        owner = lax.rem(line[0] + lines - k, lines)
        for s in range(3):
            start = (3 * k + s) * channels
            spot = pl.ds(pl.multiple_of(s * width + owner * share, share), share)
            store[spot] = whole[:, start : start + channels].reshape(share, LANES)
    features_out[...] = unorder(store[...].astype(bf16), w_in[...], order[...])


def finish_kernel(channels, lines, place, *refs):
    *pieces, w_in_out, w_out_out, short_out, out_rows, short_rows = refs
    width = w_out_out.shape[0]
    share = width // lines
    height = 4 * channels
    size = height * (width // LANES)
    for k, piece in enumerate(pieces):
        rows = piece[...].astype(f32)
        for i in range(lines):
            first = pl.multiple_of(i * share + member(place[0], k) * channels, channels)
            for h in range(width // LANES):
                low, high = h * LANES, (h + 1) * LANES
                base = i * size + h * height
                for s in range(3):
                    spot = pl.ds(pl.multiple_of(s * width + first, channels), channels)
                    start = base + s * channels
                    w_in_out[spot, low:high] = rows[start : start + channels]
                start = base + 3 * channels
                out_rows[pl.ds(first, channels), low:high] = rows[start : start + channels]
            start = lines * size
            short_rows[pl.ds(first, channels), :] = pltpu.roll(
                rows[start : start + channels], (LANES - i * TAPS) % LANES, 1
            )
    w_out_out[...] = out_rows[...].T
    short = short_rows[...].T
    for s in range(3):
        short_out[:, s * width : (s + 1) * width] = short[3 * s : 3 * s + 3, :]


def features_kernel(moved, w_in, order, features_out):
    features_out[...] = unorder(moved[...], w_in[...], order[...])


def swapped(value, plane, distance):
    return lax.ppermute(value, "fft", [(i, i ^ distance) for i in range(plane)])


def spread(value, plane):
    pieces = [value if k == 0 else swapped(value, plane, k) for k in range(0, plane, 2)]
    return [piece for own in pieces for piece in (own, swapped(own, plane, 1))]


def shape(dims, dtype=f32):
    return jax.ShapeDtypeStruct(dims, dtype)


def local(features, sink_order, cotangent, w_in, short_taps, w_out, filter_one, filter_two):
    width, row_count = features.shape
    lines, plane = lax.axis_size("seq"), lax.axis_size("fft")
    blocks = lines * plane
    channels, length = filter_one.shape
    rows = channels * blocks
    scale = 1.0 / math.sqrt(length)
    whole = channels % 8 == 0 and plane % 2 == 0 and plane & (plane - 1) == 0
    table, twist = make_tables(blocks, channels)
    eight = channels if whole else 8
    mine = lax.axis_index(AXES)

    def call(kernel, outs, *args, **options):
        return pl.pallas_call(kernel, out_shape=outs, compiler_params=PARAMS, **options)(*args)

    dims = (blocks, 4 * channels, LANES) if whole else (4 * width, LANES)
    streams, own = pl.pallas_call(
        project_kernel,
        out_shape=(shape(dims, bf16), shape((2 * width, row_count), bf16)),
        in_specs=[pl.BlockSpec(memory_space=pl.ANY)] * 5,
        scratch_shapes=[
            pltpu.VMEM(a.shape, a.dtype)
            for a in (features, sink_order, cotangent, w_in, w_out)
        ]
        + [pltpu.SemaphoreType.DMA((5,))],
        compiler_params=pltpu.CompilerParams(vmem_limit_bytes=60 * 1024 * 1024),
    )(features, sink_order, cotangent, w_in, w_out)
    if not whole:
        streams = streams.reshape(4, blocks, channels, LANES).transpose(1, 0, 2, 3)
        streams = streams.reshape(blocks, 4 * channels, LANES)
    arrived = lax.all_to_all(streams, AXES, split_axis=0, concat_axis=0, tiled=True)
    taps = lax.dynamic_slice_in_dim(short_taps.reshape(3, width, 3), mine * channels, channels, 1)
    taps = taps.transpose(1, 0, 2).reshape(channels, 9)
    if not whole:
        taps = jnp.tile(taps, (8 // channels, 1))
        arrived = arrived.reshape(blocks, 4, channels, LANES).transpose(1, 0, 2, 3)
        arrived = arrived.reshape(4, rows, LANES)
        filter_one, filter_two = [
            h.reshape(channels, blocks, LANES).transpose(1, 0, 2).reshape(rows, LANES)
            for h in (filter_one, filter_two)
        ]
    spec = shape((rows, 2 * LANES))
    spec_one, spec_two, table, twist, order = call(
        lambda *refs: filter_kernel(length, *refs),
        (
            spec,
            spec,
            shape(table.shape, bf16),
            shape(twist.shape),
            shape(sink_order.shape, jnp.int32),
        ),
        filter_one,
        filter_two,
        table,
        twist,
        sink_order,
    )
    line = lax.axis_index("seq").astype(jnp.int32).reshape(1)
    place = lax.axis_index("fft").astype(jnp.int32).reshape(1)
    scalar = pl.BlockSpec(memory_space=pltpu.SMEM)
    held = pl.BlockSpec(memory_space=pltpu.VMEM)
    chunk = (plane, 4 * channels, LANES)
    dims = [shape(chunk, bf16)] * lines if whole else [shape((4, rows, LANES), bf16)]
    short, product_one, product_two, *sent = call(
        lambda *refs: mix_kernel(channels, scale, *refs),
        (shape((eight, LANES)), spec, spec, *dims),
        arrived,
        taps,
        spec_one,
        spec_two,
        table,
        twist,
        line,
        in_specs=[held] * 6 + [scalar],
        scratch_shapes=[pltpu.VMEM((lines, *chunk), bf16)] if whole else [],
    )
    if whole:
        across = [swapped(own, plane, k) for k in (1, *range(2, plane, 2))]
        across = call(stack_kernel, shape((len(across), *own.shape), bf16), short, *across)
        pieces = (across, swapped(across, plane, 1))
    grad_one, grad_two, short = call(
        lambda *refs: filter_grads_kernel(scale / length, *refs),
        (shape(filter_one.shape), shape(filter_two.shape), shape(short.shape)),
        product_one,
        product_two,
        table,
        twist,
        short,
    )
    height = channels * 4 * (width // LANES)
    if whole:
        def ahead(value, steps):
            pairs = [(i, (i + steps) % lines) for i in range(lines)]
            return lax.ppermute(value, "seq", pairs)

        met = [sent[0]] + [ahead(sent[k], k) for k in range(1, lines)]
        size = lines * height + 2 * channels
        partial = call(
            lambda *refs: weights_kernel(channels, scale, lines, *refs),
            shape((size, LANES), bf16),
            line,
            place,
            short,
            *met,
            *pieces,
            in_specs=[scalar] * 2 + [held] * (1 + lines + len(pieces)),
        )
        moved = call(
            lambda *refs: return_kernel(channels, *refs),
            shape((plane, 3 * lines * channels, LANES), bf16),
            *met,
            partial,
        )
        partials = [partial] + [ahead(partial, k) for k in range(1, lines)]
        back = lax.all_to_all(moved, "fft", split_axis=0, concat_axis=0, tiled=True)
        grad_features = call(
            lambda *refs: moved_kernel(channels, lines, *refs),
            shape(features.shape, bf16),
            line,
            back,
            w_in,
            order,
            in_specs=[scalar] + [held] * 3,
            scratch_shapes=[pltpu.VMEM((3 * width, LANES), f32)],
        )
        rows_sum = call(sum_kernel, shape((size, LANES), bf16), *partials)
        grad_w_in, grad_w_out, short = call(
            lambda *refs: finish_kernel(channels, lines, *refs),
            (shape((3 * width, width)), shape((width, width)), shape((3, 3 * width))),
            place,
            *spread(rows_sum, plane),
            in_specs=[scalar] + [held] * plane,
            scratch_shapes=[pltpu.VMEM((width, width), f32), pltpu.VMEM((width, LANES), f32)],
        )
        return (grad_features, grad_w_in, grad_w_out, short.T, grad_one, grad_two)
    gathered = lax.all_gather(own, AXES, axis=0, tiled=False)
    sent = sent[0]
    sent = sent.reshape(4, blocks, channels, LANES)
    grad_in = jnp.einsum(
        "sbcp,bwp->scw", sent[:3], gathered[:, :width], preferred_element_type=f32
    )
    grad_out = jnp.einsum(
        "bcp,bwp->cw", sent[3], gathered[:, width:], preferred_element_type=f32
    )
    own = jnp.concatenate([grad_in, grad_out[None]]) * scale
    own = own.reshape(height, LANES)
    short = short.reshape(8 // channels, channels, LANES).sum(axis=0)
    own = jnp.concatenate([own, short]).astype(bf16)
    moved = sent[:3].transpose(1, 0, 2, 3).reshape(blocks, 3 * channels, LANES)
    own = jnp.broadcast_to(own[None], (blocks,) + own.shape)
    packed = jnp.concatenate([moved, own], axis=1)
    back = lax.all_to_all(packed, AXES, split_axis=0, concat_axis=0, tiled=True)
    moved = back[:, : 3 * channels].reshape(blocks, 3, channels, LANES)
    moved = moved.transpose(1, 0, 2, 3).reshape(3 * width, LANES)
    weights = back[:, 3 * channels : 3 * channels + height].astype(f32)
    weights = weights.reshape(blocks, 4, channels, width).transpose(1, 0, 2, 3)
    weights = weights.reshape(4 * width, width)
    short = back[:, 3 * channels + height :, :9].astype(f32).reshape(width, 3, 3)
    short = short.transpose(1, 0, 2).reshape(3 * width, 3)
    grad_features = call(
        features_kernel, shape(features.shape, bf16), moved, w_in, sink_order
    )
    grad_one, grad_two = [
        g.reshape(blocks, channels, LANES).transpose(1, 0, 2).reshape(channels, length)
        for g in (grad_one, grad_two)
    ]
    return (
        grad_features,
        weights[: 3 * width],
        weights[3 * width :].T,
        short,
        grad_one,
        grad_two,
    )


def solution(mesh):
    columns, blocks_first, copied = P(None, AXES), P(AXES, None), P()
    return jax.shard_map(
        local,
        mesh=mesh,
        in_specs=(
            columns,
            blocks_first,
            columns,
            copied,
            copied,
            copied,
            blocks_first,
            blocks_first,
        ),
        out_specs=(columns, copied, copied, copied, blocks_first, blocks_first),
        check_vma=False,
    )
```

```python
import math

import jax
import jax.numpy as jnp
import numpy as np
from jax import lax
from jax.experimental import pallas as pl
from jax.experimental.pallas import tpu as pltpu
from jax.sharding import PartitionSpec as P

AXES = ("seq", "fft")
LANES = 128
TAPS = 16
bf16 = jnp.bfloat16
f32 = jnp.float32
PARAMS = pltpu.CompilerParams(vmem_limit_bytes=24 * 1024 * 1024)


def halves(table):
    high = table.astype(np.float32).astype(jnp.bfloat16)
    low = (table - high.astype(np.float64)).astype(np.float32).astype(jnp.bfloat16)
    return high, low


def make_tables(count, channels):
    length = count * LANES
    outer = np.arange(count, dtype=np.float64) + 0.25
    inner = np.arange(LANES, dtype=np.float64)
    angle = 2.0 * np.pi * outer[:, None] * outer[None, :] / count
    first = np.kron(np.concatenate([np.cos(angle), np.sin(angle)], axis=0), np.eye(channels))
    turn = 2.0 * np.pi * (inner[:, None] * inner[None, :] % LANES) / LANES
    cos, sin = np.cos(turn), np.sin(turn)
    second = np.block([[cos, -sin], [sin, cos]])
    packed = [half for t in (first, second) for half in halves(t)]
    twist = 2.0 * np.pi * outer[:, None] * (inner[None, :] - LANES / 4) / length
    twist = np.repeat(twist, channels, axis=0)
    twist = np.concatenate([np.cos(twist), -np.sin(twist)], axis=1).astype(np.float32)
    return np.concatenate(packed, axis=0), twist


def tables_of(table, twist):
    rows = twist.shape[0]
    at, found = 0, []
    for size in (2 * rows, 2 * LANES):
        pair = []
        for half in range(2):
            pair.append(table[at : at + size])
            at += size
        found.append(tuple(pair))
    first, second = found
    back = tuple(jnp.concatenate([t[:rows], t[rows:]], axis=1) for t in first)
    return first, back, second, (twist[:, :LANES], twist[:, LANES:])


def split(value):
    high = value.astype(bf16)
    low = (value - high.astype(f32)).astype(bf16)
    return high, low


def dot(left, right):
    return jnp.dot(left, right, preferred_element_type=f32)


def dot_pairs(left, right):
    deep_left = jnp.concatenate([left[0], left[0], left[1]], axis=1)
    deep_right = jnp.concatenate([right[0], right[1], right[0]], axis=0)
    return dot(deep_left, deep_right)


def forward(signals, first, second, twist):
    rows = signals[0].shape[0]
    stage = dot_pairs(first, split(jnp.concatenate(signals, axis=1)))
    parts = []
    for i in range(len(signals)):
        cos = stage[:rows, i * LANES : (i + 1) * LANES]
        sin = stage[rows:, i * LANES : (i + 1) * LANES]
        parts.append(
            jnp.concatenate(
                [cos * twist[0] + sin * twist[1], cos * twist[1] - sin * twist[0]], axis=1
            )
        )
    specs = [dot_pairs(split(part), second) for part in parts]
    return [(spec[:, :LANES], spec[:, LANES:]) for spec in specs]


def backward(spectra, back, second, twist):
    parts = []
    for pair in spectra:
        stage = dot_pairs(split(jnp.concatenate(pair, axis=1)), second)
        re, im = stage[:, :LANES], stage[:, LANES:]
        parts.append(
            jnp.concatenate(
                [re * twist[0] - im * twist[1], re * twist[1] + im * twist[0]], axis=0
            )
        )
    out = dot_pairs(back, split(jnp.concatenate(parts, axis=1)))
    return [out[:, i * LANES : (i + 1) * LANES] for i in range(len(spectra))]


def times(a, b):
    return (a[0] * b[0] - a[1] * b[1], -(a[0] * b[1] + a[1] * b[0]))


def conj_times(a, b):
    return (a[0] * b[0] + a[1] * b[1], a[1] * b[0] - a[0] * b[1])


def one_hot(order):
    size = order.shape[1]
    place = lax.broadcasted_iota(jnp.int32, (size, size), 0)
    return (place == order).astype(f32).astype(bf16)


def project_kernel(
    features_at,
    order_at,
    cotangent_at,
    w_in_at,
    w_out_at,
    streams_out,
    gather_out,
    features,
    order,
    cotangent,
    w_in,
    w_out,
    done,
):
    copies = [
        pltpu.make_async_copy(source, target, done.at[i])
        for i, (source, target) in enumerate(
            [
                (order_at, order),
                (features_at, features),
                (w_in_at, w_in),
                (cotangent_at, cotangent),
                (w_out_at, w_out),
            ]
        )
    ]
    for copy in copies:
        copy.start()
    width, row_count = features.shape
    copies[0].wait()
    copies[1].wait()
    seq_input = dot(features[...], one_hot(order[...])).astype(bf16)
    copies[2].wait()
    projected = dot(w_in[...], seq_input)
    copies[3].wait()
    copies[4].wait()
    out_grad = lax.dot_general(
        w_out[...], cotangent[...], (((0,), (0,)), ((), ())), preferred_element_type=f32
    )
    if len(streams_out.shape) == 3:
        blocks = streams_out.shape[0]
        parts = [projected[s * width : (s + 1) * width] for s in range(3)] + [out_grad]
        parts = [part.reshape(blocks, width // blocks, row_count) for part in parts]
        streams_out[...] = jnp.concatenate(parts, axis=1).astype(bf16)
    else:
        streams_out[: 3 * width] = projected.astype(bf16)
        streams_out[3 * width :] = out_grad.astype(bf16)
    own = jnp.concatenate([seq_input, cotangent[...]], axis=0)
    gather_out[...] = own


def read_signal(ref, rows):
    if ref.shape[1] == LANES:
        return ref[...]
    return jnp.concatenate(
        [ref[:, i * LANES : (i + 1) * LANES] for i in range(ref.shape[1] // LANES)], axis=0
    )


def write_signal(ref, value):
    if ref.shape[1] == LANES:
        ref[...] = value
        return
    channels = ref.shape[0]
    for i in range(ref.shape[1] // LANES):
        ref[:, i * LANES : (i + 1) * LANES] = value[i * channels : (i + 1) * channels]


def filter_kernel(
    length,
    filter_one,
    filter_two,
    table,
    twist,
    order,
    spec_one,
    spec_two,
    table_out,
    twist_out,
    order_out,
):
    rows = spec_one.shape[0]
    signals = [read_signal(filter_one, rows), read_signal(filter_two, rows)]
    first, _, second, turns = tables_of(table, twist)
    one, two = forward(signals, first, second, turns)
    spec_one[...] = jnp.concatenate(one, axis=1) * (1.0 / length)
    spec_two[...] = jnp.concatenate(two, axis=1) * (1.0 / length)
    table_out[...] = table[...]
    twist_out[...] = twist[...]
    order_out[...] = order[...]


def stack_kernel(after, *refs):
    *sources, out = refs
    for i, source in enumerate(sources):
        out[i] = source[...]


def shifted(value, steps, channels):
    if steps == 0:
        return value
    rows, lanes = value.shape
    lane = lax.broadcasted_iota(jnp.int32, value.shape, 1)
    row = lax.broadcasted_iota(jnp.int32, value.shape, 0)
    turned = pltpu.roll(value, steps % lanes, 1)
    if steps > 0:
        carried = jnp.where(row < channels, 0.0, pltpu.roll(turned, channels, 0))
        return jnp.where(lane < steps, carried, turned)
    carried = jnp.where(row >= rows - channels, 0.0, pltpu.roll(turned, rows - channels, 0))
    return jnp.where(lane >= lanes + steps, carried, turned)


def mix_kernel(
    channels,
    scale,
    streams,
    taps,
    spec_one,
    spec_two,
    table,
    twist,
    line,
    short_out,
    product_one,
    product_two,
    *sent_out,
):
    rows = twist.shape[0]
    eight = taps.shape[0]
    first, back, second, twist = tables_of(table, twist)
    if streams.shape[0] == 4 and streams.shape[1] == rows:
        pieces = [streams[s].astype(f32) for s in range(4)]
    else:
        whole = streams[...].astype(f32)
        pieces = [
            whole[:, s * channels : (s + 1) * channels].reshape(rows, LANES) for s in range(4)
        ]
    out_grad = pieces[3]

    def tap(s, k):
        column = jnp.broadcast_to(taps[:, 3 * s + k : 3 * s + k + 1], (eight, LANES))
        column = jnp.broadcast_to(column[None], (rows // eight, eight, LANES))
        return column.reshape(rows, LANES)

    late = [[shifted(pieces[s], k, channels) for k in range(3)] for s in range(3)]
    value, gate_one, gate_two = [
        sum(tap(s, k) * late[s][k] for k in range(3)) for s in range(3)
    ]
    h_one = (spec_one[:, :LANES], spec_one[:, LANES:])
    h_two = (spec_two[:, :LANES], spec_two[:, LANES:])
    value_spec, second_spec = forward([value, out_grad * gate_two], first, second, twist)
    first_mix, grad_first_out = backward(
        [times(h_one, value_spec), conj_times(h_two, second_spec)],
        back,
        second,
        twist,
    )
    first_spec, grad_first_spec = forward(
        [gate_one * first_mix, gate_one * grad_first_out], first, second, twist
    )
    second_mix, grad_value = backward(
        [times(h_two, first_spec), conj_times(h_one, grad_first_spec)],
        back,
        second,
        twist,
    )
    product_one[...] = jnp.concatenate(conj_times(value_spec, grad_first_spec), axis=1)
    product_two[...] = jnp.concatenate(conj_times(first_spec, second_spec), axis=1)
    grads = [grad_value, grad_first_out * first_mix, out_grad * second_mix]
    sent = []
    lane = lax.broadcasted_iota(jnp.int32, (eight, LANES), 1)
    short = jnp.zeros((eight, LANES), f32)
    for s in range(3):
        sent.append(sum(tap(s, k) * shifted(grads[s], -k, channels) for k in range(3)))
        for k in range(3):
            folded = (grads[s] * late[s][k]).reshape(rows // eight, eight, LANES).sum(axis=0)
            total = jnp.sum(folded, axis=1, keepdims=True) * scale
            short = jnp.where(lane == 3 * s + k, total, short)
    sent.append(gate_two * second_mix)
    short_out[...] = short
    if len(sent_out) == 1:
        for s in range(4):
            sent_out[0][s] = sent[s].astype(bf16)
        return
    parts = [part.reshape(rows // channels, channels, LANES) for part in sent]
    packed = jnp.concatenate(parts, axis=1).astype(bf16)
    *sent_out, store = sent_out
    lines, plane = store.shape[:2]
    for i in range(lines):
        store[i] = packed[i * plane : (i + 1) * plane]
    for step in range(lines):
        sent_out[step][...] = store[member(line[0], step)]


def filter_grads_kernel(
    scale, product_one, product_two, table, twist, short, grad_one, grad_two, short_out
):
    _, back, second, twist = tables_of(table, twist)
    spectra = [(ref[:, :LANES], ref[:, LANES:]) for ref in (product_one, product_two)]
    one, two = backward(spectra, back, second, twist)
    write_signal(grad_one, one * scale)
    write_signal(grad_two, two * scale)
    short_out[...] = short[...]


def member(at, k):
    return jnp.bitwise_xor(at, k)


def weights_kernel(channels, scale, lines, *refs):
    line, place, short, *met, across, over, partial_out = refs
    pieces = [over[0], across[0]]
    for i in range(1, across.shape[0]):
        pieces += [across[i], over[i]]
    plane, width = len(pieces), across.shape[1] // 2
    height = 4 * channels
    total = jnp.zeros((lines * height, 2 * width), f32)
    step = 2 if plane % 2 == 0 else 1
    for i in range(0, plane, step):
        left = jnp.concatenate(
            [
                jnp.concatenate([m[member(place[0], i + j)] for m in met], axis=0)
                for j in range(step)
            ],
            axis=1,
        )
        right = jnp.concatenate([pieces[i + j] for j in range(step)], axis=1)
        total = total + lax.dot_general(
            left, right, (((1,), (1,)), ((), ())), preferred_element_type=f32
        )
    total = total * scale
    size = height * (width // LANES)
    for k in range(lines):
        parts = []
        for h in range(width // LANES):
            low, high = h * LANES, (h + 1) * LANES
            base = k * height
            parts.append(total[base : base + 3 * channels, low:high])
            parts.append(total[base + 3 * channels : base + height, width + low : width + high])
        owner = member(line[0], k)
        spot = pl.ds(pl.multiple_of(owner * size, size), size)
        partial_out[spot] = jnp.concatenate(parts, axis=0).astype(bf16)
    tail = pltpu.roll(short[...], line[0] * TAPS, 1)
    tail = jnp.concatenate([tail, jnp.zeros_like(tail)], axis=0)
    partial_out[lines * size :] = tail.astype(bf16)


def return_kernel(channels, *refs):
    *met, after, moved_out = refs
    parts = [m[...].astype(f32)[:, : 3 * channels] for m in met]
    moved_out[...] = jnp.concatenate(parts, axis=1).astype(bf16)


def sum_kernel(*refs):
    *partials, out = refs
    out[...] = sum(part[...].astype(f32) for part in partials).astype(bf16)


def unorder(grad_projected, w_in, order):
    grad_seq = lax.dot_general(
        w_in, grad_projected, (((0,), (0,)), ((), ())), preferred_element_type=f32
    ).astype(bf16)
    return lax.dot_general(
        grad_seq, one_hot(order), (((1,), (1,)), ((), ())), preferred_element_type=f32
    ).astype(bf16)


def moved_kernel(channels, lines, line, back, w_in, order, features_out, store):
    plane, width = back.shape[0], w_in.shape[1]
    share = plane * channels
    whole = back[...].astype(f32)
    for k in range(lines):
        owner = member(line[0], k)
        for s in range(3):
            start = (3 * k + s) * channels
            spot = pl.ds(pl.multiple_of(s * width + owner * share, share), share)
            store[spot] = whole[:, start : start + channels].reshape(share, LANES)
    features_out[...] = unorder(store[...].astype(bf16), w_in[...], order[...])


def finish_kernel(channels, lines, place, *refs):
    *pieces, w_in_out, w_out_out, short_out, out_rows, short_rows = refs
    width = w_out_out.shape[0]
    share = width // lines
    height = 4 * channels
    size = height * (width // LANES)
    for k, piece in enumerate(pieces):
        rows = piece[...].astype(f32)
        for i in range(lines):
            first = pl.multiple_of(i * share + member(place[0], k) * channels, channels)
            for h in range(width // LANES):
                low, high = h * LANES, (h + 1) * LANES
                base = i * size + h * height
                for s in range(3):
                    spot = pl.ds(pl.multiple_of(s * width + first, channels), channels)
                    start = base + s * channels
                    w_in_out[spot, low:high] = rows[start : start + channels]
                start = base + 3 * channels
                out_rows[pl.ds(first, channels), low:high] = rows[start : start + channels]
            start = lines * size
            short_rows[pl.ds(first, channels), :] = pltpu.roll(
                rows[start : start + channels], (LANES - i * TAPS) % LANES, 1
            )
    w_out_out[...] = out_rows[...].T
    short = short_rows[...].T
    for s in range(3):
        short_out[:, s * width : (s + 1) * width] = short[3 * s : 3 * s + 3, :]


def features_kernel(moved, w_in, order, features_out):
    features_out[...] = unorder(moved[...], w_in[...], order[...])


def swapped(value, plane, distance):
    return lax.ppermute(value, "fft", [(i, i ^ distance) for i in range(plane)])


def spread(value, plane):
    pieces = [value if k == 0 else swapped(value, plane, k) for k in range(0, plane, 2)]
    return [piece for own in pieces for piece in (own, swapped(own, plane, 1))]


def shape(dims, dtype=f32):
    return jax.ShapeDtypeStruct(dims, dtype)


def local(features, sink_order, cotangent, w_in, short_taps, w_out, filter_one, filter_two):
    width, row_count = features.shape
    lines, plane = lax.axis_size("seq"), lax.axis_size("fft")
    blocks = lines * plane
    channels, length = filter_one.shape
    rows = channels * blocks
    scale = 1.0 / math.sqrt(length)
    whole = channels % 8 == 0 and plane % 2 == 0 and plane & (plane - 1) == 0
    table, twist = make_tables(blocks, channels)
    eight = channels if whole else 8
    mine = lax.axis_index(AXES)

    def call(kernel, outs, *args, **options):
        return pl.pallas_call(kernel, out_shape=outs, compiler_params=PARAMS, **options)(*args)

    dims = (blocks, 4 * channels, LANES) if whole else (4 * width, LANES)
    streams, own = pl.pallas_call(
        project_kernel,
        out_shape=(shape(dims, bf16), shape((2 * width, row_count), bf16)),
        in_specs=[pl.BlockSpec(memory_space=pl.ANY)] * 5,
        scratch_shapes=[
            pltpu.VMEM(a.shape, a.dtype)
            for a in (features, sink_order, cotangent, w_in, w_out)
        ]
        + [pltpu.SemaphoreType.DMA((5,))],
        compiler_params=pltpu.CompilerParams(vmem_limit_bytes=60 * 1024 * 1024),
    )(features, sink_order, cotangent, w_in, w_out)
    if not whole:
        streams = streams.reshape(4, blocks, channels, LANES).transpose(1, 0, 2, 3)
        streams = streams.reshape(blocks, 4 * channels, LANES)
    arrived = lax.all_to_all(streams, AXES, split_axis=0, concat_axis=0, tiled=True)
    taps = lax.dynamic_slice_in_dim(short_taps.reshape(3, width, 3), mine * channels, channels, 1)
    taps = taps.transpose(1, 0, 2).reshape(channels, 9)
    if not whole:
        taps = jnp.tile(taps, (8 // channels, 1))
        arrived = arrived.reshape(blocks, 4, channels, LANES).transpose(1, 0, 2, 3)
        arrived = arrived.reshape(4, rows, LANES)
        filter_one, filter_two = [
            h.reshape(channels, blocks, LANES).transpose(1, 0, 2).reshape(rows, LANES)
            for h in (filter_one, filter_two)
        ]
    spec = shape((rows, 2 * LANES))
    spec_one, spec_two, table, twist, order = call(
        lambda *refs: filter_kernel(length, *refs),
        (
            spec,
            spec,
            shape(table.shape, bf16),
            shape(twist.shape),
            shape(sink_order.shape, jnp.int32),
        ),
        filter_one,
        filter_two,
        table,
        twist,
        sink_order,
    )
    line = lax.axis_index("seq").astype(jnp.int32).reshape(1)
    place = lax.axis_index("fft").astype(jnp.int32).reshape(1)
    scalar = pl.BlockSpec(memory_space=pltpu.SMEM)
    held = pl.BlockSpec(memory_space=pltpu.VMEM)
    chunk = (plane, 4 * channels, LANES)
    dims = [shape(chunk, bf16)] * lines if whole else [shape((4, rows, LANES), bf16)]
    short, product_one, product_two, *sent = call(
        lambda *refs: mix_kernel(channels, scale, *refs),
        (shape((eight, LANES)), spec, spec, *dims),
        arrived,
        taps,
        spec_one,
        spec_two,
        table,
        twist,
        line,
        in_specs=[held] * 6 + [scalar],
        scratch_shapes=[pltpu.VMEM((lines, *chunk), bf16)] if whole else [],
    )
    if whole:
        across = [swapped(own, plane, k) for k in (1, *range(2, plane, 2))]
        across = call(stack_kernel, shape((len(across), *own.shape), bf16), short, *across)
        pieces = (across, swapped(across, plane, 1))
    grad_one, grad_two, short = call(
        lambda *refs: filter_grads_kernel(scale / length, *refs),
        (shape(filter_one.shape), shape(filter_two.shape), shape(short.shape)),
        product_one,
        product_two,
        table,
        twist,
        short,
    )
    height = channels * 4 * (width // LANES)
    if whole:
        def across_lines(value, distance):
            pairs = [(i, i ^ distance) for i in range(lines)]
            return lax.ppermute(value, "seq", pairs)

        met = [sent[0]] + [across_lines(sent[k], k) for k in range(1, lines)]
        size = lines * height + 2 * channels
        partial = call(
            lambda *refs: weights_kernel(channels, scale, lines, *refs),
            shape((size, LANES), bf16),
            line,
            place,
            short,
            *met,
            *pieces,
            in_specs=[scalar] * 2 + [held] * (1 + lines + len(pieces)),
        )
        moved = call(
            lambda *refs: return_kernel(channels, *refs),
            shape((plane, 3 * lines * channels, LANES), bf16),
            *met,
            partial,
        )
        partials = [partial] + [across_lines(partial, k) for k in range(1, lines)]
        back = lax.all_to_all(moved, "fft", split_axis=0, concat_axis=0, tiled=True)
        grad_features = call(
            lambda *refs: moved_kernel(channels, lines, *refs),
            shape(features.shape, bf16),
            line,
            back,
            w_in,
            order,
            in_specs=[scalar] + [held] * 3,
            scratch_shapes=[pltpu.VMEM((3 * width, LANES), f32)],
        )
        rows_sum = call(sum_kernel, shape((size, LANES), bf16), *partials)
        grad_w_in, grad_w_out, short = call(
            lambda *refs: finish_kernel(channels, lines, *refs),
            (shape((3 * width, width)), shape((width, width)), shape((3, 3 * width))),
            place,
            *spread(rows_sum, plane),
            in_specs=[scalar] + [held] * plane,
            scratch_shapes=[pltpu.VMEM((width, width), f32), pltpu.VMEM((width, LANES), f32)],
        )
        return (grad_features, grad_w_in, grad_w_out, short.T, grad_one, grad_two)
    gathered = lax.all_gather(own, AXES, axis=0, tiled=False)
    sent = sent[0]
    sent = sent.reshape(4, blocks, channels, LANES)
    grad_in = jnp.einsum(
        "sbcp,bwp->scw", sent[:3], gathered[:, :width], preferred_element_type=f32
    )
    grad_out = jnp.einsum(
        "bcp,bwp->cw", sent[3], gathered[:, width:], preferred_element_type=f32
    )
    own = jnp.concatenate([grad_in, grad_out[None]]) * scale
    own = own.reshape(height, LANES)
    short = short.reshape(8 // channels, channels, LANES).sum(axis=0)
    own = jnp.concatenate([own, short]).astype(bf16)
    moved = sent[:3].transpose(1, 0, 2, 3).reshape(blocks, 3 * channels, LANES)
    own = jnp.broadcast_to(own[None], (blocks,) + own.shape)
    packed = jnp.concatenate([moved, own], axis=1)
    back = lax.all_to_all(packed, AXES, split_axis=0, concat_axis=0, tiled=True)
    moved = back[:, : 3 * channels].reshape(blocks, 3, channels, LANES)
    moved = moved.transpose(1, 0, 2, 3).reshape(3 * width, LANES)
    weights = back[:, 3 * channels : 3 * channels + height].astype(f32)
    weights = weights.reshape(blocks, 4, channels, width).transpose(1, 0, 2, 3)
    weights = weights.reshape(4 * width, width)
    short = back[:, 3 * channels + height :, :9].astype(f32).reshape(width, 3, 3)
    short = short.transpose(1, 0, 2).reshape(3 * width, 3)
    grad_features = call(
        features_kernel, shape(features.shape, bf16), moved, w_in, sink_order
    )
    grad_one, grad_two = [
        g.reshape(blocks, channels, LANES).transpose(1, 0, 2).reshape(channels, length)
        for g in (grad_one, grad_two)
    ]
    return (
        grad_features,
        weights[: 3 * width],
        weights[3 * width :].T,
        short,
        grad_one,
        grad_two,
    )


def solution(mesh):
    columns, blocks_first, copied = P(None, AXES), P(AXES, None), P()
    return jax.shard_map(
        local,
        mesh=mesh,
        in_specs=(
            columns,
            blocks_first,
            columns,
            copied,
            copied,
            copied,
            blocks_first,
            blocks_first,
        ),
        out_specs=(columns, copied, copied, copied, blocks_first, blocks_first),
        check_vma=False,
    )
```

```python
import math

import jax
import jax.numpy as jnp
import numpy as np
from jax import lax
from jax.experimental import pallas as pl
from jax.experimental.pallas import tpu as pltpu
from jax.sharding import PartitionSpec as P

AXES = ("seq", "fft")
LANES = 128
TAPS = 16
bf16 = jnp.bfloat16
f32 = jnp.float32
PARAMS = pltpu.CompilerParams(vmem_limit_bytes=24 * 1024 * 1024)


def halves(table):
    high = table.astype(np.float32).astype(jnp.bfloat16)
    low = (table - high.astype(np.float64)).astype(np.float32).astype(jnp.bfloat16)
    return high, low


def make_tables(count, channels):
    length = count * LANES
    outer = np.arange(count, dtype=np.float64) + 0.25
    inner = np.arange(LANES, dtype=np.float64)
    angle = 2.0 * np.pi * outer[:, None] * outer[None, :] / count
    first = np.kron(np.concatenate([np.cos(angle), np.sin(angle)], axis=0), np.eye(channels))
    turn = 2.0 * np.pi * (inner[:, None] * inner[None, :] % LANES) / LANES
    cos, sin = np.cos(turn), np.sin(turn)
    second = np.block([[cos, -sin], [sin, cos]])
    packed = [half for t in (first, second) for half in halves(t)]
    twist = 2.0 * np.pi * outer[:, None] * (inner[None, :] - LANES / 4) / length
    twist = np.repeat(twist, channels, axis=0)
    twist = np.concatenate([np.cos(twist), -np.sin(twist)], axis=1).astype(np.float32)
    return np.concatenate(packed, axis=0), twist


def tables_of(table, twist):
    rows = twist.shape[0]
    at, found = 0, []
    for size in (2 * rows, 2 * LANES):
        pair = []
        for half in range(2):
            pair.append(table[at : at + size])
            at += size
        found.append(tuple(pair))
    first, second = found
    back = tuple(jnp.concatenate([t[:rows], t[rows:]], axis=1) for t in first)
    return first, back, second, (twist[:, :LANES], twist[:, LANES:])


def split(value):
    high = value.astype(bf16)
    low = (value - high.astype(f32)).astype(bf16)
    return high, low


def dot(left, right):
    return jnp.dot(left, right, preferred_element_type=f32)


def dot_pairs(left, right):
    deep_left = jnp.concatenate([left[0], left[0], left[1]], axis=1)
    deep_right = jnp.concatenate([right[0], right[1], right[0]], axis=0)
    return dot(deep_left, deep_right)


def forward(signals, first, second, twist):
    rows = signals[0].shape[0]
    stage = dot_pairs(first, split(jnp.concatenate(signals, axis=1)))
    parts = []
    for i in range(len(signals)):
        cos = stage[:rows, i * LANES : (i + 1) * LANES]
        sin = stage[rows:, i * LANES : (i + 1) * LANES]
        parts.append(
            jnp.concatenate(
                [cos * twist[0] + sin * twist[1], cos * twist[1] - sin * twist[0]], axis=1
            )
        )
    specs = [dot_pairs(split(part), second) for part in parts]
    return [(spec[:, :LANES], spec[:, LANES:]) for spec in specs]


def backward(spectra, back, second, twist):
    parts = []
    for pair in spectra:
        stage = dot_pairs(split(jnp.concatenate(pair, axis=1)), second)
        re, im = stage[:, :LANES], stage[:, LANES:]
        parts.append(
            jnp.concatenate(
                [re * twist[0] - im * twist[1], re * twist[1] + im * twist[0]], axis=0
            )
        )
    out = dot_pairs(back, split(jnp.concatenate(parts, axis=1)))
    return [out[:, i * LANES : (i + 1) * LANES] for i in range(len(spectra))]


def times(a, b):
    return (a[0] * b[0] - a[1] * b[1], -(a[0] * b[1] + a[1] * b[0]))


def conj_times(a, b):
    return (a[0] * b[0] + a[1] * b[1], a[1] * b[0] - a[0] * b[1])


def one_hot(order):
    size = order.shape[1]
    place = lax.broadcasted_iota(jnp.int32, (size, size), 0)
    return (place == order).astype(f32).astype(bf16)


def project_kernel(
    features_at,
    order_at,
    cotangent_at,
    w_in_at,
    w_out_at,
    streams_out,
    gather_out,
    features,
    order,
    cotangent,
    w_in,
    w_out,
    done,
):
    copies = [
        pltpu.make_async_copy(source, target, done.at[i])
        for i, (source, target) in enumerate(
            [
                (order_at, order),
                (features_at, features),
                (w_in_at, w_in),
                (cotangent_at, cotangent),
                (w_out_at, w_out),
            ]
        )
    ]
    for copy in copies:
        copy.start()
    width, row_count = features.shape
    copies[0].wait()
    copies[1].wait()
    seq_input = dot(features[...], one_hot(order[...])).astype(bf16)
    copies[2].wait()
    projected = dot(w_in[...], seq_input)
    copies[3].wait()
    copies[4].wait()
    out_grad = lax.dot_general(
        w_out[...], cotangent[...], (((0,), (0,)), ((), ())), preferred_element_type=f32
    )
    if len(streams_out.shape) == 3:
        blocks = streams_out.shape[0]
        parts = [projected[s * width : (s + 1) * width] for s in range(3)] + [out_grad]
        parts = [part.reshape(blocks, width // blocks, row_count) for part in parts]
        streams_out[...] = jnp.concatenate(parts, axis=1).astype(bf16)
    else:
        streams_out[: 3 * width] = projected.astype(bf16)
        streams_out[3 * width :] = out_grad.astype(bf16)
    own = jnp.concatenate([seq_input, cotangent[...]], axis=0)
    gather_out[...] = own


def read_signal(ref, rows):
    if ref.shape[1] == LANES:
        return ref[...]
    return jnp.concatenate(
        [ref[:, i * LANES : (i + 1) * LANES] for i in range(ref.shape[1] // LANES)], axis=0
    )


def write_signal(ref, value):
    if ref.shape[1] == LANES:
        ref[...] = value
        return
    channels = ref.shape[0]
    for i in range(ref.shape[1] // LANES):
        ref[:, i * LANES : (i + 1) * LANES] = value[i * channels : (i + 1) * channels]


def filter_kernel(
    length,
    filter_one,
    filter_two,
    table,
    twist,
    order,
    spec_one,
    spec_two,
    table_out,
    twist_out,
    order_out,
):
    rows = spec_one.shape[0]
    signals = [read_signal(filter_one, rows), read_signal(filter_two, rows)]
    first, _, second, turns = tables_of(table, twist)
    one, two = forward(signals, first, second, turns)
    spec_one[...] = jnp.concatenate(one, axis=1) * (1.0 / length)
    spec_two[...] = jnp.concatenate(two, axis=1) * (1.0 / length)
    table_out[...] = table[...]
    twist_out[...] = twist[...]
    order_out[...] = order[...]


def stack_kernel(after, *refs):
    *sources, out = refs
    for i, source in enumerate(sources):
        out[i] = source[...]


def shifted(value, steps, channels):
    if steps == 0:
        return value
    rows, lanes = value.shape
    lane = lax.broadcasted_iota(jnp.int32, value.shape, 1)
    row = lax.broadcasted_iota(jnp.int32, value.shape, 0)
    turned = pltpu.roll(value, steps % lanes, 1)
    if steps > 0:
        carried = jnp.where(row < channels, 0.0, pltpu.roll(turned, channels, 0))
        return jnp.where(lane < steps, carried, turned)
    carried = jnp.where(row >= rows - channels, 0.0, pltpu.roll(turned, rows - channels, 0))
    return jnp.where(lane >= lanes + steps, carried, turned)


def mix_kernel(
    channels,
    scale,
    streams,
    taps,
    spec_one,
    spec_two,
    table,
    twist,
    line,
    short_out,
    product_one,
    product_two,
    *sent_out,
):
    rows = twist.shape[0]
    eight = taps.shape[0]
    first, back, second, twist = tables_of(table, twist)
    if streams.shape[0] == 4 and streams.shape[1] == rows:
        pieces = [streams[s].astype(f32) for s in range(4)]
    else:
        whole = streams[...].astype(f32)
        pieces = [
            whole[:, s * channels : (s + 1) * channels].reshape(rows, LANES) for s in range(4)
        ]
    out_grad = pieces[3]

    def tap(s, k):
        column = jnp.broadcast_to(taps[:, 3 * s + k : 3 * s + k + 1], (eight, LANES))
        column = jnp.broadcast_to(column[None], (rows // eight, eight, LANES))
        return column.reshape(rows, LANES)

    late = [[shifted(pieces[s], k, channels) for k in range(3)] for s in range(3)]
    value, gate_one, gate_two = [
        sum(tap(s, k) * late[s][k] for k in range(3)) for s in range(3)
    ]
    h_one = (spec_one[:, :LANES], spec_one[:, LANES:])
    h_two = (spec_two[:, :LANES], spec_two[:, LANES:])
    value_spec, second_spec = forward([value, out_grad * gate_two], first, second, twist)
    first_mix, grad_first_out = backward(
        [times(h_one, value_spec), conj_times(h_two, second_spec)],
        back,
        second,
        twist,
    )
    first_spec, grad_first_spec = forward(
        [gate_one * first_mix, gate_one * grad_first_out], first, second, twist
    )
    second_mix, grad_value = backward(
        [times(h_two, first_spec), conj_times(h_one, grad_first_spec)],
        back,
        second,
        twist,
    )
    product_one[...] = jnp.concatenate(conj_times(value_spec, grad_first_spec), axis=1)
    product_two[...] = jnp.concatenate(conj_times(first_spec, second_spec), axis=1)
    grads = [grad_value, grad_first_out * first_mix, out_grad * second_mix]
    sent = []
    lane = lax.broadcasted_iota(jnp.int32, (eight, LANES), 1)
    short = jnp.zeros((eight, LANES), f32)
    for s in range(3):
        sent.append(sum(tap(s, k) * shifted(grads[s], -k, channels) for k in range(3)))
        for k in range(3):
            folded = (grads[s] * late[s][k]).reshape(rows // eight, eight, LANES).sum(axis=0)
            total = jnp.sum(folded, axis=1, keepdims=True) * scale
            short = jnp.where(lane == 3 * s + k, total, short)
    sent.append(gate_two * second_mix)
    short_out[...] = short
    if len(sent_out) == 1:
        for s in range(4):
            sent_out[0][s] = sent[s].astype(bf16)
        return
    parts = [part.reshape(rows // channels, channels, LANES) for part in sent]
    packed = jnp.concatenate(parts, axis=1).astype(bf16)
    *sent_out, store = sent_out
    lines, plane = store.shape[:2]
    for i in range(lines):
        store[i] = packed[i * plane : (i + 1) * plane]
    for step in range(lines):
        sent_out[step][...] = store[lax.rem(line[0] + step, lines)]


def filter_grads_kernel(
    scale, product_one, product_two, table, twist, short, grad_one, grad_two, short_out
):
    _, back, second, twist = tables_of(table, twist)
    spectra = [(ref[:, :LANES], ref[:, LANES:]) for ref in (product_one, product_two)]
    one, two = backward(spectra, back, second, twist)
    write_signal(grad_one, one * scale)
    write_signal(grad_two, two * scale)
    short_out[...] = short[...]


def member(at, k):
    return jnp.bitwise_xor(at, k)


def weights_kernel(channels, scale, lines, *refs):
    line, place, short, *met, across, over, partial_out = refs
    pieces = [over[0], across[0]]
    for i in range(1, across.shape[0]):
        pieces += [across[i], over[i]]
    plane, width = len(pieces), across.shape[1] // 2
    height = 4 * channels
    total = jnp.zeros((lines * height, 2 * width), f32)
    step = 2 if plane % 2 == 0 else 1
    for i in range(0, plane, step):
        left = jnp.concatenate(
            [
                jnp.concatenate([m[member(place[0], i + j)] for m in met], axis=0)
                for j in range(step)
            ],
            axis=1,
        )
        right = jnp.concatenate([pieces[i + j] for j in range(step)], axis=1)
        total = total + lax.dot_general(
            left, right, (((1,), (1,)), ((), ())), preferred_element_type=f32
        )
    total = total * scale
    size = height * (width // LANES)
    for k in range(lines):
        parts = []
        for h in range(width // LANES):
            low, high = h * LANES, (h + 1) * LANES
            base = k * height
            parts.append(total[base : base + 3 * channels, low:high])
            parts.append(total[base + 3 * channels : base + height, width + low : width + high])
        owner = lax.rem(line[0] + lines - k, lines)
        spot = pl.ds(pl.multiple_of(owner * size, size), size)
        partial_out[spot] = jnp.concatenate(parts, axis=0).astype(bf16)
    tail = pltpu.roll(short[...], line[0] * TAPS, 1)
    tail = jnp.concatenate([tail, jnp.zeros_like(tail)], axis=0)
    partial_out[lines * size :] = tail.astype(bf16)


def return_kernel(channels, *refs):
    *met, after, moved_out = refs
    parts = [m[...].astype(f32)[:, : 3 * channels] for m in met]
    moved_out[...] = jnp.concatenate(parts, axis=1).astype(bf16)


def sum_kernel(*refs):
    *partials, out = refs
    out[...] = sum(part[...].astype(f32) for part in partials).astype(bf16)


def unorder(grad_projected, w_in, order):
    grad_seq = lax.dot_general(
        w_in, grad_projected, (((0,), (0,)), ((), ())), preferred_element_type=f32
    ).astype(bf16)
    return lax.dot_general(
        grad_seq, one_hot(order), (((1,), (1,)), ((), ())), preferred_element_type=f32
    ).astype(bf16)


def moved_kernel(channels, lines, line, back, w_in, order, features_out, store):
    plane, width = back.shape[0], w_in.shape[1]
    share = plane * channels
    whole = back[...].astype(f32)
    for k in range(lines):
        owner = lax.rem(line[0] + lines - k, lines)
        for s in range(3):
            start = (3 * k + s) * channels
            spot = pl.ds(pl.multiple_of(s * width + owner * share, share), share)
            store[spot] = whole[:, start : start + channels].reshape(share, LANES)
    features_out[...] = unorder(store[...].astype(bf16), w_in[...], order[...])


def finish_kernel(channels, lines, place, *refs):
    *pieces, w_in_out, w_out_out, short_out, out_rows, short_rows = refs
    width = w_out_out.shape[0]
    share = width // lines
    height = 4 * channels
    size = height * (width // LANES)
    for k, piece in enumerate(pieces):
        rows = piece[...].astype(f32)
        for i in range(lines):
            first = pl.multiple_of(i * share + member(place[0], k) * channels, channels)
            for h in range(width // LANES):
                low, high = h * LANES, (h + 1) * LANES
                base = i * size + h * height
                for s in range(3):
                    spot = pl.ds(pl.multiple_of(s * width + first, channels), channels)
                    start = base + s * channels
                    w_in_out[spot, low:high] = rows[start : start + channels]
                start = base + 3 * channels
                out_rows[pl.ds(first, channels), low:high] = rows[start : start + channels]
            start = lines * size
            short_rows[pl.ds(first, channels), :] = pltpu.roll(
                rows[start : start + channels], (LANES - i * TAPS) % LANES, 1
            )
    w_out_out[...] = out_rows[...].T
    short = short_rows[...].T
    for s in range(3):
        short_out[:, s * width : (s + 1) * width] = short[3 * s : 3 * s + 3, :]


def features_kernel(moved, w_in, order, features_out):
    features_out[...] = unorder(moved[...], w_in[...], order[...])


def swapped(value, plane, distance):
    return lax.ppermute(value, "fft", [(i, i ^ distance) for i in range(plane)])


def spread(value, plane):
    pieces = [value if k == 0 else swapped(value, plane, k) for k in range(0, plane, 2)]
    return [piece for own in pieces for piece in (own, swapped(own, plane, 1))]


def shape(dims, dtype=f32):
    return jax.ShapeDtypeStruct(dims, dtype)


def local(features, sink_order, cotangent, w_in, short_taps, w_out, filter_one, filter_two):
    width, row_count = features.shape
    lines, plane = lax.axis_size("seq"), lax.axis_size("fft")
    blocks = lines * plane
    channels, length = filter_one.shape
    rows = channels * blocks
    scale = 1.0 / math.sqrt(length)
    whole = channels % 8 == 0 and plane % 2 == 0 and plane & (plane - 1) == 0
    table, twist = make_tables(blocks, channels)
    eight = channels if whole else 8
    mine = lax.axis_index(AXES)

    def call(kernel, outs, *args, **options):
        return pl.pallas_call(kernel, out_shape=outs, compiler_params=PARAMS, **options)(*args)

    dims = (blocks, 4 * channels, LANES) if whole else (4 * width, LANES)
    streams, own = pl.pallas_call(
        project_kernel,
        out_shape=(shape(dims, bf16), shape((2 * width, row_count), bf16)),
        in_specs=[pl.BlockSpec(memory_space=pl.ANY)] * 5,
        scratch_shapes=[
            pltpu.VMEM(a.shape, a.dtype)
            for a in (features, sink_order, cotangent, w_in, w_out)
        ]
        + [pltpu.SemaphoreType.DMA((5,))],
        compiler_params=pltpu.CompilerParams(vmem_limit_bytes=60 * 1024 * 1024),
    )(features, sink_order, cotangent, w_in, w_out)
    if not whole:
        streams = streams.reshape(4, blocks, channels, LANES).transpose(1, 0, 2, 3)
        streams = streams.reshape(blocks, 4 * channels, LANES)
    arrived = lax.all_to_all(streams, AXES, split_axis=0, concat_axis=0, tiled=True)
    taps = lax.dynamic_slice_in_dim(short_taps.reshape(3, width, 3), mine * channels, channels, 1)
    taps = taps.transpose(1, 0, 2).reshape(channels, 9)
    if not whole:
        taps = jnp.tile(taps, (8 // channels, 1))
        arrived = arrived.reshape(blocks, 4, channels, LANES).transpose(1, 0, 2, 3)
        arrived = arrived.reshape(4, rows, LANES)
        filter_one, filter_two = [
            h.reshape(channels, blocks, LANES).transpose(1, 0, 2).reshape(rows, LANES)
            for h in (filter_one, filter_two)
        ]
    spec = shape((rows, 2 * LANES))
    spec_one, spec_two, table, twist, order = call(
        lambda *refs: filter_kernel(length, *refs),
        (
            spec,
            spec,
            shape(table.shape, bf16),
            shape(twist.shape),
            shape(sink_order.shape, jnp.int32),
        ),
        filter_one,
        filter_two,
        table,
        twist,
        sink_order,
    )
    line = lax.axis_index("seq").astype(jnp.int32).reshape(1)
    place = lax.axis_index("fft").astype(jnp.int32).reshape(1)
    scalar = pl.BlockSpec(memory_space=pltpu.SMEM)
    held = pl.BlockSpec(memory_space=pltpu.VMEM)
    chunk = (plane, 4 * channels, LANES)
    dims = [shape(chunk, bf16)] * lines if whole else [shape((4, rows, LANES), bf16)]
    short, product_one, product_two, *sent = call(
        lambda *refs: mix_kernel(channels, scale, *refs),
        (shape((eight, LANES)), spec, spec, *dims),
        arrived,
        taps,
        spec_one,
        spec_two,
        table,
        twist,
        line,
        in_specs=[held] * 6 + [scalar],
        scratch_shapes=[pltpu.VMEM((lines, *chunk), bf16)] if whole else [],
    )
    if whole:
        across = [swapped(own, plane, k) for k in (1, *range(2, plane, 2))]
        across = call(stack_kernel, shape((len(across), *own.shape), bf16), short, *across)
        pieces = (across, swapped(across, plane, 1))
    grad_one, grad_two, short = call(
        lambda *refs: filter_grads_kernel(scale / length, *refs),
        (shape(filter_one.shape), shape(filter_two.shape), shape(short.shape)),
        product_one,
        product_two,
        table,
        twist,
        short,
    )
    height = channels * 4 * (width // LANES)
    if whole:
        def ahead(value, steps):
            pairs = [(i, (i + steps) % lines) for i in range(lines)]
            return lax.ppermute(value, "seq", pairs)

        met = [sent[0]] + [ahead(sent[k], k) for k in range(1, lines)]
        size = lines * height + 2 * channels
        partial = call(
            lambda *refs: weights_kernel(channels, scale, lines, *refs),
            shape((size, LANES), bf16),
            line,
            place,
            short,
            *met,
            *pieces,
            in_specs=[scalar] * 2 + [held] * (1 + lines + len(pieces)),
        )
        moved = call(
            lambda *refs: return_kernel(channels, *refs),
            shape((plane, 3 * lines * channels, LANES), bf16),
            *met,
            partial,
        )
        pairs = [[(i, i ^ k) for i in range(lines)] for k in range(1, lines)]
        partials = [partial] + [lax.ppermute(partial, "seq", pair) for pair in pairs]
        back = lax.all_to_all(moved, "fft", split_axis=0, concat_axis=0, tiled=True)
        grad_features = call(
            lambda *refs: moved_kernel(channels, lines, *refs),
            shape(features.shape, bf16),
            line,
            back,
            w_in,
            order,
            in_specs=[scalar] + [held] * 3,
            scratch_shapes=[pltpu.VMEM((3 * width, LANES), f32)],
        )
        rows_sum = call(sum_kernel, shape((size, LANES), bf16), *partials)
        grad_w_in, grad_w_out, short = call(
            lambda *refs: finish_kernel(channels, lines, *refs),
            (shape((3 * width, width)), shape((width, width)), shape((3, 3 * width))),
            place,
            *spread(rows_sum, plane),
            in_specs=[scalar] + [held] * plane,
            scratch_shapes=[pltpu.VMEM((width, width), f32), pltpu.VMEM((width, LANES), f32)],
        )
        return (grad_features, grad_w_in, grad_w_out, short.T, grad_one, grad_two)
    gathered = lax.all_gather(own, AXES, axis=0, tiled=False)
    sent = sent[0]
    sent = sent.reshape(4, blocks, channels, LANES)
    grad_in = jnp.einsum(
        "sbcp,bwp->scw", sent[:3], gathered[:, :width], preferred_element_type=f32
    )
    grad_out = jnp.einsum(
        "bcp,bwp->cw", sent[3], gathered[:, width:], preferred_element_type=f32
    )
    own = jnp.concatenate([grad_in, grad_out[None]]) * scale
    own = own.reshape(height, LANES)
    short = short.reshape(8 // channels, channels, LANES).sum(axis=0)
    own = jnp.concatenate([own, short]).astype(bf16)
    moved = sent[:3].transpose(1, 0, 2, 3).reshape(blocks, 3 * channels, LANES)
    own = jnp.broadcast_to(own[None], (blocks,) + own.shape)
    packed = jnp.concatenate([moved, own], axis=1)
    back = lax.all_to_all(packed, AXES, split_axis=0, concat_axis=0, tiled=True)
    moved = back[:, : 3 * channels].reshape(blocks, 3, channels, LANES)
    moved = moved.transpose(1, 0, 2, 3).reshape(3 * width, LANES)
    weights = back[:, 3 * channels : 3 * channels + height].astype(f32)
    weights = weights.reshape(blocks, 4, channels, width).transpose(1, 0, 2, 3)
    weights = weights.reshape(4 * width, width)
    short = back[:, 3 * channels + height :, :9].astype(f32).reshape(width, 3, 3)
    short = short.transpose(1, 0, 2).reshape(3 * width, 3)
    grad_features = call(
        features_kernel, shape(features.shape, bf16), moved, w_in, sink_order
    )
    grad_one, grad_two = [
        g.reshape(blocks, channels, LANES).transpose(1, 0, 2).reshape(channels, length)
        for g in (grad_one, grad_two)
    ]
    return (
        grad_features,
        weights[: 3 * width],
        weights[3 * width :].T,
        short,
        grad_one,
        grad_two,
    )


def solution(mesh):
    columns, blocks_first, copied = P(None, AXES), P(AXES, None), P()
    return jax.shard_map(
        local,
        mesh=mesh,
        in_specs=(
            columns,
            blocks_first,
            columns,
            copied,
            copied,
            copied,
            blocks_first,
            blocks_first,
        ),
        out_specs=(columns, copied, copied, copied, blocks_first, blocks_first),
        check_vma=False,
    )
```
